512 devices in a mesh: gx: 8 (over y, core), gy: 4 (over x), gz: 16 (over z).
Axes of the slice: x: 4, y: 4, z: 16, core: 2. Of those that a mesh axis runs over, the one named last changes fastest.
Arguments:
- right_side: float32 [64, 256, 2048], P('gx', 'gy', 'gz'), may hold values from -4 to 4
- start: float32 [64, 256, 2048], P('gx', 'gy', 'gz'), may hold values from -6 to 6
Outputs:
- solution: float32 [64, 256, 2048], P('gx', 'gy', 'gz')
The draws below stay inside these ranges and needn't reach their ends.
All inputs are finite; a program needn't handle non-finite values.
Results may differ from the reference program's by a relative error of at most 0.0003.
Values sent between devices are 32-bit elements; how exact they have to be, the bound alone decides.
No kernel may reach another device: no remote copies, remote signals or barrier semaphores. Data moves between devices by JAX's collectives and lax.ppermute only.
A program may use at most 128 MiB of HBM per device.

```python
import jax
import jax.numpy as jnp
from jax import lax

LEVELS = 4
SWEEPS = 2
CSWEEPS = 8
NX = 64
NY = 256
NZ = 2048


def draw_right_side(key, part):
    values = jnp.clip(jax.random.normal(key, (NX, NY, NZ), jnp.float32), -4.0, 4.0)
    return values


def steps_of(key, shape, pieces, low, top_value):
    def one(axis_at, shards_of):
        draws = jax.random.uniform(jax.random.fold_in(jax.random.fold_in(key, 6), axis_at), (shards_of,), jnp.float32, low / len(pieces), top_value / len(pieces))
        return jnp.repeat(jnp.exp(draws), shape[axis_at] // shards_of).reshape((-1,) + (1,) * (len(shape) - axis_at - 1))

    factor_of = one(*pieces[0])
    for cut in pieces[1:]:
        factor_of = factor_of * one(*cut)
    return factor_of


def scatter_about(own_key, shape, deviation, reach, pieces=(), held_as=jnp.bfloat16):
    factor_of = steps_of(own_key, shape, pieces, -0.22, 0.18) if pieces else 1.0
    entries = jax.random.normal(own_key, shape, jnp.float32) * deviation * factor_of
    return jnp.minimum(jnp.maximum(entries, -reach), reach).astype(held_as)


def setup_inputs(seed: int = 0) -> dict:
    streams_of = jax.random.split(jax.random.key(seed), 3)
    right_side = draw_right_side(jax.random.fold_in(streams_of[2], 71), 0)
    start = scatter_about(streams_of[1], (NX, NY, NZ), 1.0, 6.0, ((0, 8), (1, 4), (2, 16)), jnp.float32)
    return {"right_side": right_side, "start": start}


def neighbours(padded):
    total = padded[2:, 1:-1, 1:-1] + padded[:-2, 1:-1, 1:-1]
    total = total + padded[1:-1, 2:, 1:-1] + padded[1:-1, :-2, 1:-1]
    return total + padded[1:-1, 1:-1, 2:] + padded[1:-1, 1:-1, :-2]


def parity(dims):
    first = lax.broadcasted_iota(jnp.int32, dims, 0)
    second = lax.broadcasted_iota(jnp.int32, dims, 1)
    third = lax.broadcasted_iota(jnp.int32, dims, 2)
    return (first + second + third) % 2


def smooth(correction, source, factor, colours, count):
    for pass_index in range(count):
        for colour in (0, 1):
            beside_all = neighbours(jnp.pad(correction, 1))
            correction = jnp.where(colours == colour, (factor * source + beside_all) / 6.0, correction)
    return correction


def restrict(residual):
    sx, sy, sz = residual.shape
    return residual.reshape(sx // 2, 2, sy // 2, 2, sz // 2, 2).mean(axis=(1, 3, 5))


def prolong(coarse):
    return jnp.repeat(jnp.repeat(jnp.repeat(coarse, 2, axis=0), 2, axis=1), 2, axis=2)


def reference(right_side, start):
    stored = []
    correction = start
    source = right_side
    for depth in range(LEVELS - 1):
        factor = 4.0 ** depth
        if depth > 0:
            correction = jnp.zeros_like(source)
        colours = parity(source.shape)
        correction = smooth(correction, source, factor, colours, SWEEPS)
        residual = source - (6.0 * correction - neighbours(jnp.pad(correction, 1))) / factor
        stored.append((correction, source, colours))
        source = restrict(residual)
    correction = smooth(jnp.zeros_like(source), source, 4.0 ** (LEVELS - 1), parity(source.shape), CSWEEPS)
    for depth in reversed(range(LEVELS - 1)):
        fine_value, fine_source, colours = stored[depth]
        correction = smooth(fine_value + prolong(correction), fine_source, 4.0 ** depth, colours, SWEEPS)
    return correction
```

```python
import functools

import jax
import jax.numpy as jnp
from jax import lax
from jax.experimental import pallas as pl
from jax.experimental.pallas import tpu as pltpu
from jax.sharding import PartitionSpec as P

F32 = jnp.float32
SIXTH = 1.0 / 6.0
EY = 24
ROWS0 = 64 + 2 * EY
ROWS1 = ROWS0 // 2
UP0 = EY - 8
VMEM_LIMIT = 40 * 1024 * 1024


def call(kernel, outs, scratch=(), flops=0):
    shapes = [jax.ShapeDtypeStruct(s, F32) for s in outs]
    return pl.pallas_call(
        kernel,
        out_shape=shapes,
        scratch_shapes=[pltpu.VMEM(s, F32) for s in scratch],
        compiler_params=pltpu.CompilerParams(vmem_limit_bytes=VMEM_LIMIT),
    )


def even_mask(shape):
    rows = lax.broadcasted_iota(jnp.int32, shape, 0)
    lanes = lax.broadcasted_iota(jnp.int32, shape, 1)
    return ((rows + lanes) & 1) == 0


def lane_of(shape):
    return lax.broadcasted_iota(jnp.int32, shape, 1)


def domain(shape, row0, rows, lane0, lanes, lane_limit=None):
    y = lax.broadcasted_iota(jnp.int32, shape, 0) + row0
    z = lax.broadcasted_iota(jnp.int32, shape, 1)
    inside = (y >= 0) & (y < rows) & (z + lane0 >= 0) & (z + lane0 < lanes)
    if lane_limit is not None:
        inside = inside & (z < lane_limit)
    return jnp.where(inside, F32(SIXTH), F32(0.0))


def beside(src, i, even, red):
    c = src[i]
    y, z = c.shape
    below, above = src[i - 1], src[i + 1]
    s = c + (jnp.where(even, below, above) if red else jnp.where(even, above, below))
    s = s + (pltpu.roll(c, 1, 0) + pltpu.roll(c, y - 1, 0))
    return s + (pltpu.roll(c, 1, 1) + pltpu.roll(c, z - 1, 1))


def half(dst, src, b, shift, weight, even, red, lo, hi):
    def body(i, carry):
        dst[i + 1] = (b[i + shift] + beside(src, i + 1, even, red)) * weight[...]
        return carry

    lax.fori_loop(lo, hi, body, 0)


def pair_sum(mat_rows, mat_cols, of):
    k = lax.broadcasted_iota(jnp.int32, (mat_rows, mat_cols), 0)
    c = lax.broadcasted_iota(jnp.int32, (mat_rows, mat_cols), 1)
    return of(k, c)


def dot(a, b):
    return jnp.dot(a, b, precision=lax.Precision.HIGHEST, preferred_element_type=F32)


def pack_kernel(start, right, s, up, down):
    even = even_mask((64, 128))
    low = lane_of((64, 128)) < 64
    planes = []
    for p in range(4):
        planes.append(jnp.where(even, start[2 * p + 1], start[2 * p]))
    for p in range(4):
        planes.append(jnp.where(even, right[2 * p], right[2 * p + 1]))
    for p in range(4):
        planes.append(jnp.where(even, right[2 * p + 1], right[2 * p]))
    for p in range(12):
        s[p] = planes[p]
    for p in range(6):
        a, b = planes[p], planes[p + 6]
        up[p] = jnp.where(low, pltpu.roll(a, 64, 1), b)
        down[p] = jnp.where(low, a, pltpu.roll(b, 64, 1))


def widen_kernel(s, left, right, z, first, last):
    low = lane_of((64, 128)) < 64
    for p in range(12):
        own = pltpu.roll(s[p], 64, 1)
        if p < 6:
            a, b = left[p], pltpu.roll(right[p], 64, 1)
        else:
            a, b = pltpu.roll(left[p - 6], 64, 1), right[p - 6]
        v0 = jnp.where(low, a, own)
        v1 = jnp.where(low, own, b)
        z[p, :, :128] = v0
        z[p, :, 128:] = v1
        first[p, :, :128] = v0[:EY]
        first[p, :, 128:] = v1[:EY]
        last[p, :, :128] = v0[64 - EY :]
        last[p, :, 128:] = v1[64 - EY :]


def lengthen_kernel(z, before, after, a):
    a[:, :EY] = before[...]
    a[:, EY : EY + 64] = z[...]
    a[:, EY + 64 :] = after[...]


def fine_down_kernel(n, own, left, right, coarse, black_out, red_b_out, black_b_out, red, black, rb, bb, weight, pairs):
    gx, gy, gz = (lax.axis_index(a) for a in ("gx", "gy", "gz"))
    shape = (ROWS0, 256)
    even = even_mask(shape)
    weight[...] = domain(shape, 64 * gy - EY, 64 * n[1], 128 * gz - 64, 128 * n[2])
    zero = jnp.zeros(shape, F32)
    for i in (0, 13):
        black[i] = zero
        red[i] = zero
    has_left, has_right = gx > 0, gx < n[0] - 1
    for p in range(4):
        black[p + 5] = own[p]
        rb[p + 4] = own[p + 4]
        bb[p + 4] = own[p + 8]
        rb[p] = left[p + 4]
        bb[p] = left[p + 8]
        rb[p + 8] = right[p + 4]
        bb[p + 8] = right[p + 8]
        black[p + 1] = jnp.where(has_left, left[p], zero)
        black[p + 9] = jnp.where(has_right, right[p], zero)
        red[p + 1] = zero
        red[p + 9] = zero
    first = jnp.where(has_left, 0, 4)
    end = jnp.where(has_right, 12, 8)
    for dst, src, b, is_red, lo in ((red, black, rb, True, 0), (black, red, bb, False, 1), (red, black, rb, True, 1), (black, red, bb, False, 2)):
        half(dst, src, b, 0, weight, even, is_red, jnp.maximum(first, lo), jnp.minimum(end, 12 - lo))

    def residual(p, carry):
        i = p + 5
        r = (rb[p + 4] - 6.0 * red[i] + beside(black, i, even, True)) + (bb[p + 4] - 6.0 * black[i] + beside(red, i, even, False))
        pairs[2 * p] = r[:, :128]
        pairs[2 * p + 1] = r[:, 128:]
        return carry

    lax.fori_loop(0, 4, residual, 0)
    rows = []
    for p in range(4):
        parts = [pairs[2 * p + h, pl.ds(0, ROWS1, stride=2), :] + pairs[2 * p + h, pl.ds(1, ROWS1, stride=2), :] for h in (0, 1)]
        rows.append(jnp.concatenate(parts, axis=1))
    take = pair_sum(256, 128, lambda k, c: jnp.where((k >> 1) == c, F32(0.5), F32(0.0)))
    result = dot(jnp.concatenate(rows, axis=0), take)
    for p in range(4):
        coarse[p] = result[p * ROWS1 : (p + 1) * ROWS1]
    for p in range(8):
        black_out[p] = black[p + 3, UP0 : UP0 + 80]
        red_b_out[p] = rb[p + 2, UP0 : UP0 + 80]
        black_b_out[p] = bb[p + 2, UP0 : UP0 + 80]


def middle_down_kernel(n, b1, coarse, black_out, red_b, black_b, red, black, weight, pairs):
    gy, gz = lax.axis_index("gy"), lax.axis_index("gz")
    shape = (ROWS1, 128)
    count = 2 * n[0]
    even = even_mask(shape)
    weight[...] = domain(shape, 32 * gy - EY // 2, 32 * n[1], 64 * gz - 32, 64 * n[2])
    zero = jnp.zeros(shape, F32)
    for i in (0, count + 1):
        red[i] = zero
        black[i] = zero

    def begin(i, carry):
        a, b = b1[2 * i], b1[2 * i + 1]
        r = jnp.where(even, a, b)
        red_b[i] = r
        black_b[i] = jnp.where(even, b, a)
        red[i + 1] = r * weight[...]
        return carry

    lax.fori_loop(0, count, begin, 0)
    half(black, red, black_b, 0, weight, even, False, 0, count)
    half(red, black, red_b, 0, weight, even, True, 0, count)
    half(black, red, black_b, 0, weight, even, False, 0, count)

    def residual(i, carry):
        r = (red_b[i] - 6.0 * red[i + 1] + beside(black, i + 1, even, True)) + (black_b[i] - 6.0 * black[i + 1] + beside(red, i + 1, even, False))
        pairs[i] = r
        black_out[i] = black[i + 1]
        return carry

    lax.fori_loop(0, count, residual, 0)
    top = EY // 2
    sums = [pairs[i, pl.ds(top, 16, stride=2), :] + pairs[i, pl.ds(top + 1, 16, stride=2), :] for i in range(count)]
    left = jnp.concatenate(sums[: n[0]], axis=0)
    right = jnp.concatenate(sums[n[0] :], axis=0)
    take_low = pair_sum(128, 128, lambda k, c: jnp.where((k >> 1) == c, F32(0.5), F32(0.0)))
    take_high = pair_sum(128, 128, lambda k, c: jnp.where((k >> 1) == c - 64, F32(0.5), F32(0.0)))
    result = dot(left, take_low) + dot(right, take_high)
    for i in range(n[0]):
        coarse[i] = result[16 * i : 16 * i + 16]


def widen_coarse_kernel(n, own, left, right, wide):
    lanes = lane_of((16, 128))
    is_left, is_own = lanes < 48, lanes < 80
    for i in range(n[0]):
        w, a, b = own[i], left[i], right[i]
        wide[i] = jnp.where(is_left, a, jnp.where(is_own, pltpu.roll(w, 32, 1), pltpu.roll(b, 64, 1)))
        wide[i + n[0]] = jnp.where(is_left, pltpu.roll(a, 64, 1), jnp.where(is_own, pltpu.roll(w, 96, 1), b))


def up_kernel(
    n, b2, black1, red_b1, black_b1, black0, red_b0, black_b0, out,
    rb2, bb2, red2, black2, weight2, pairs2,
    rb3, bb3, red3, black3, weight3, add2,
    win2, exp2, add1, red1, weight1, add0,
    red0, weight0, bl1, bl0,
):
    gx, gy, gz = (lax.axis_index(a) for a in ("gx", "gy", "gz"))
    rows2, rows3 = 16 * n[1], 8 * n[1]
    shape2 = (rows2 + 8, 128)
    even2 = even_mask(shape2)
    weight2[...] = domain(shape2, 0, rows2, 32 * gz - 48, 32 * n[2])
    zero2 = jnp.zeros(shape2, F32)
    pairs_2 = n[0]
    for i in (0, pairs_2 + 1):
        red2[i] = zero2
        black2[i] = zero2
    even16 = even_mask((16, 128))
    for i in range(pairs_2):
        for g in range(n[1]):
            a, b = b2[g, 2 * i], b2[g, 2 * i + 1]
            rb2[i, 16 * g : 16 * g + 16] = jnp.where(even16, a, b)
            bb2[i, 16 * g : 16 * g + 16] = jnp.where(even16, b, a)
        rb2[i, rows2:] = jnp.zeros((8, 128), F32)
        bb2[i, rows2:] = jnp.zeros((8, 128), F32)

    def begin2(i, carry):
        red2[i + 1] = rb2[i] * weight2[...]
        return carry

    lax.fori_loop(0, pairs_2, begin2, 0)
    half(black2, red2, bb2, 0, weight2, even2, False, 0, pairs_2)
    half(red2, black2, rb2, 0, weight2, even2, True, 0, pairs_2)
    half(black2, red2, bb2, 0, weight2, even2, False, 0, pairs_2)

    def residual2(i, carry):
        pairs2[i] = (rb2[i] - 6.0 * red2[i + 1] + beside(black2, i + 1, even2, True)) + (bb2[i] - 6.0 * black2[i + 1] + beside(red2, i + 1, even2, False))
        return carry

    lax.fori_loop(0, pairs_2, residual2, 0)
    sums = [pairs2[i, pl.ds(0, rows3, stride=2), :] + pairs2[i, pl.ds(1, rows3, stride=2), :] for i in range(pairs_2)]
    take = pair_sum(128, 128, lambda k, c: jnp.where((k >> 1) == c, F32(0.5), F32(0.0)))
    b3 = dot(jnp.concatenate(sums, axis=0), take)

    shape3 = (rows3 + 8, 128)
    even3 = even_mask(shape3)
    even3s = even_mask((rows3, 128))
    weight3[...] = domain(shape3, 0, rows3, 16 * gz - 24, 16 * n[2], 64)
    zero3 = jnp.zeros(shape3, F32)
    pairs_3 = n[0] // 2
    for i in (0, pairs_3 + 1):
        red3[i] = zero3
        black3[i] = zero3
    for i in range(pairs_3):
        a = b3[2 * i * rows3 : (2 * i + 1) * rows3]
        b = b3[(2 * i + 1) * rows3 : (2 * i + 2) * rows3]
        rb3[i, :rows3] = jnp.where(even3s, a, b)
        bb3[i, :rows3] = jnp.where(even3s, b, a)
        rb3[i, rows3:] = jnp.zeros((8, 128), F32)
        bb3[i, rows3:] = jnp.zeros((8, 128), F32)
        red3[i + 1] = rb3[i] * weight3[...]

    def half3(dst, src, b, red):
        for i in range(pairs_3):
            dst[i + 1] = (b[i] + beside(src, i + 1, even3, red)) * weight3[...]

    half3(black3, red3, bb3, False)

    def sweep3(_, carry):
        half3(red3, black3, rb3, True)
        half3(black3, red3, bb3, False)
        return carry

    lax.fori_loop(0, 7, sweep3, 0)
    planes = []
    for i in range(pairs_3):
        r, b = red3[i + 1, :rows3], black3[i + 1, :rows3]
        planes += [jnp.where(even3s, r, b), jnp.where(even3s, b, r)]
    spread3 = pair_sum(128, 128, lambda k, c: jnp.where(k == (c >> 1), F32(1.0), F32(0.0)))
    wide = dot(jnp.concatenate(planes, axis=0), spread3)
    for i in range(pairs_2):
        w = wide[i * rows3 : (i + 1) * rows3]
        add2[i, pl.ds(0, rows3, stride=2), :] = w
        add2[i, pl.ds(1, rows3, stride=2), :] = w
        black2[i + 1, :rows2] = black2[i + 1, :rows2] + add2[i]
    for dst, src, b, is_red in ((red2, black2, rb2, True), (black2, red2, bb2, False)) * 2:
        half(dst, src, b, 0, weight2, even2, is_red, 0, pairs_2)

    even2s = even_mask((rows2, 128))
    for i in range(pairs_2):
        r, b = red2[i + 1, :rows2], black2[i + 1, :rows2]
        for q, v in ((2 * i, jnp.where(even2s, r, b)), (2 * i + 1, jnp.where(even2s, b, r))):
            win2[q, :8] = jnp.zeros((8, 128), F32)
            win2[q, 8 : 8 + rows2] = v
            win2[q, 8 + rows2 :] = jnp.zeros((24, 128), F32)
    count = 2 * n[0]
    top = pl.multiple_of(16 * gy, 8)
    cut = jnp.concatenate([win2[q, pl.ds(top, 40), :] for q in range(count)], axis=0)
    spread2 = pair_sum(128, 128, lambda k, c: jnp.where(k == (c >> 1) + 32, F32(1.0), F32(0.0)))
    wide = dot(cut, spread2)
    shape1 = (ROWS1, 128)
    even1 = even_mask(shape1)
    weight1[...] = domain(shape1, 32 * gy - EY // 2, 32 * n[1], 64 * gz - 32, 64 * n[2])
    zero1 = jnp.zeros(shape1, F32)
    skip = 8 - EY // 4
    for i in (0, count + 1):
        red1[i] = zero1
        bl1[i] = zero1
    for i in range(count):
        w = wide[40 * i + skip : 40 * i + skip + ROWS1 // 2]
        add1[i, pl.ds(0, ROWS1 // 2, stride=2), :] = w
        add1[i, pl.ds(1, ROWS1 // 2, stride=2), :] = w
        bl1[i + 1] = black1[i] + add1[i]
    for dst, src, b, is_red in ((red1, bl1, red_b1, True), (bl1, red1, black_b1, False)) * 2:
        half(dst, src, b, 0, weight1, even1, is_red, 0, count)

    low1 = UP0 // 2
    even40 = even_mask((40, 128))
    planes = []
    for i in range(8):
        q = 2 * gx + i // 2
        r, b = red1[q, low1 : low1 + 40], bl1[q, low1 : low1 + 40]
        planes.append(jnp.where(even40, r, b) if i % 2 == 0 else jnp.where(even40, b, r))
    stacked = jnp.concatenate(planes, axis=0)
    shape0 = (80, 256)
    even0 = even_mask(shape0)
    weight0[...] = domain(shape0, 64 * gy - 8, 64 * n[1], 128 * gz - 64, 128 * n[2])
    zero0 = jnp.zeros(shape0, F32)
    for h in (0, 1):
        spread1 = pair_sum(128, 128, lambda k, c: jnp.where(k == (c >> 1) + 64 * h, F32(1.0), F32(0.0)))
        wide = dot(stacked, spread1)
        for i in range(8):
            w = wide[40 * i : 40 * i + 40]
            add0[2 * i + h, pl.ds(0, 40, stride=2), :] = w
            add0[2 * i + h, pl.ds(1, 40, stride=2), :] = w
    for i in range(10):
        red0[i] = zero0
    bl0[0] = zero0
    bl0[9] = zero0
    for i in range(8):
        bl0[i + 1] = black0[i] + jnp.concatenate([add0[2 * i], add0[2 * i + 1]], axis=1)
    first = jnp.where(gx > 0, 0, 2)
    end = jnp.where(gx < n[0] - 1, 8, 6)
    for dst, src, b, is_red, lo in ((red0, bl0, red_b0, True, 0), (bl0, red0, black_b0, False, 1), (red0, bl0, red_b0, True, 1), (bl0, red0, black_b0, False, 2)):
        half(dst, src, b, 0, weight0, even0, is_red, jnp.maximum(first, lo), jnp.minimum(end, 8 - lo))
    even64 = even_mask((64, 128))
    for p in range(4):
        r = pltpu.roll(red0[p + 3, 8:72], 192, 1)[:, :128]
        b = pltpu.roll(bl0[p + 3, 8:72], 192, 1)[:, :128]
        out[2 * p] = jnp.where(even64, r, b)
        out[2 * p + 1] = jnp.where(even64, b, r)


def from_both(up_value, down_value, axis):
    size = lax.axis_size(axis)
    up = [(i, i + 1) for i in range(size - 1)]
    return lax.ppermute(up_value, axis, up), lax.ppermute(down_value, axis, [(b, a) for a, b in up])


def from_both_round(value, axis):
    size = lax.axis_size(axis)
    up = [(i, (i + 1) % size) for i in range(size)]
    return lax.ppermute(value, axis, up), lax.ppermute(value, axis, [(b, a) for a, b in up])


def gathered(value, axis):
    copies = jnp.broadcast_to(value, (lax.axis_size(axis), *value.shape))
    return lax.all_to_all(copies, axis, split_axis=0, concat_axis=0, tiled=True)


def local(right_side, start):
    n = tuple(lax.axis_size(a) for a in ("gx", "gy", "gz"))
    s, up, down = call(pack_kernel, [(12, 64, 128), (6, 64, 128), (6, 64, 128)])(start, right_side)
    left, right = from_both(up, down, "gz")
    z, first, last = call(widen_kernel, [(12, 64, 256), (12, EY, 256), (12, EY, 256)])(s, left, right)
    before, after = from_both(last, first, "gy")
    (own,) = call(lengthen_kernel, [(12, ROWS0, 256)])(z, before, after)
    left, right = from_both_round(own, "gx")
    wide0 = (ROWS0, 256)
    up0 = (8, 80, 256)
    b1, black0, red_b0, black_b0 = call(
        functools.partial(fine_down_kernel, n),
        [(4, ROWS1, 128), up0, up0, up0],
        [(14, *wide0), (14, *wide0), (12, *wide0), (12, *wide0), wide0, (8, ROWS0, 128)],
    )(own, left, right)
    b1 = gathered(b1, "gx").reshape(4 * n[0], ROWS1, 128)
    all1 = (2 * n[0], ROWS1, 128)
    pad1 = (2 * n[0] + 2, ROWS1, 128)
    b2, black1, red_b1, black_b1 = call(
        functools.partial(middle_down_kernel, n),
        [(n[0], 16, 128), all1, all1, all1],
        [pad1, pad1, (ROWS1, 128), all1],
    )(b1)
    left, right = from_both(b2, b2, "gz")
    (b2,) = call(functools.partial(widen_coarse_kernel, n), [(2 * n[0], 16, 128)])(b2, left, right)
    b2 = gathered(b2, "gy").reshape(n[1], 2 * n[0], 16, 128)
    rows2, rows3 = 16 * n[1], 8 * n[1]
    p2, p3 = n[0], n[0] // 2
    w2, w3 = (rows2 + 8, 128), (rows3 + 8, 128)
    (out,) = call(
        functools.partial(up_kernel, n),
        [(8, 64, 128)],
        [
            (p2, *w2), (p2, *w2), (p2 + 2, *w2), (p2 + 2, *w2), w2, (p2, *w2),
            (p3, *w3), (p3, *w3), (p3 + 2, *w3), (p3 + 2, *w3), w3, (p2, rows2, 128),
            (2 * n[0], rows2 + 32, 128), (2 * n[0], 40, 128), all1, pad1, (ROWS1, 128), (16, 80, 128),
            (10, 80, 256), (80, 256), pad1, (10, 80, 256),
        ],
    )(b2, black1, red_b1, black_b1, black0, red_b0, black_b0)
    return out


def solution(mesh):
    in_specs = (P("gx", "gy", "gz"), P("gx", "gy", "gz"))
    out_specs = P("gx", "gy", "gz")
    return jax.shard_map(local, mesh=mesh, in_specs=in_specs, out_specs=out_specs, check_vma=False)
```

```python
import functools

import jax
import jax.numpy as jnp
from jax import lax
from jax.experimental import pallas as pl
from jax.experimental.pallas import tpu as pltpu
from jax.sharding import PartitionSpec as P

F32 = jnp.float32
BF16 = jnp.bfloat16
SIXTH = 1.0 / 6.0
EY = 24
ROWS0 = 64 + 2 * EY
ROWS1 = ROWS0 // 2
PAD = 8
UP0 = EY - 8
VMEM_LIMIT = 40 * 1024 * 1024


def call(kernel, outs, scratch=(), in_specs=None):
    shapes = [jax.ShapeDtypeStruct(s, F32) for s in outs]
    extra = {} if in_specs is None else {"in_specs": in_specs}
    return pl.pallas_call(
        kernel,
        out_shape=shapes,
        scratch_shapes=[pltpu.VMEM(s, F32) if isinstance(s, tuple) else s for s in scratch],
        compiler_params=pltpu.CompilerParams(vmem_limit_bytes=VMEM_LIMIT),
        **extra,
    )


def even_mask(shape):
    rows = lax.broadcasted_iota(jnp.int32, shape, 0)
    lanes = lax.broadcasted_iota(jnp.int32, shape, 1)
    return ((rows + lanes) & 1) == 0


def lane_of(shape):
    return lax.broadcasted_iota(jnp.int32, shape, 1)


def domain(shape, row0, rows, lane0, lanes, cut, unused=None):
    y = lax.broadcasted_iota(jnp.int32, shape, 0) + row0
    k = lane_of(shape)
    z = jnp.where(k < cut, k, k - shape[1]) + lane0
    inside = (y >= 0) & (y < rows) & (z >= 0) & (z < lanes)
    if unused is not None:
        inside = inside & ((k < unused[0]) | (k >= unused[1]))
    return jnp.where(inside, F32(SIXTH), F32(0.0))


def beside(src, i, r, rows, even, red):
    at = PAD + r
    c = src[i + 1, at : at + rows]
    below, above = src[i, at : at + rows], src[i + 2, at : at + rows]
    s = c + (jnp.where(even, below, above) if red else jnp.where(even, above, below))
    s = s + (src[i + 1, at - 1 : at - 1 + rows] + src[i + 1, at + 1 : at + 1 + rows])
    return s + (pltpu.roll(c, 1, 1) + pltpu.roll(c, c.shape[1] - 1, 1))


def half(dst, src, b, weight, red, pairs, rows, step):
    even = even_mask((step, dst.shape[2]))
    for i in pairs:
        for r in range(0, rows, step):
            value = (b[i, r : r + step] + beside(src, i, r, step, even, red)) * weight(i, r, step)
            dst[i + 1, PAD + r : PAD + r + step] = value


def residual_sum(red, black, red_b, black_b, i, r, step, even):
    at = PAD + r
    x = red_b[i, r : r + step] - 6.0 * red[i + 1, at : at + step] + beside(black, i, r, step, even, True)
    y = black_b[i, r : r + step] - 6.0 * black[i + 1, at : at + step] + beside(red, i, r, step, even, False)
    return x + y


def clear_pads(*colours):
    for ref in colours:
        pairs, rows, lanes = ref.shape
        for i in (0, pairs - 1):
            ref[i] = jnp.zeros((rows, lanes), F32)
        for i in range(1, pairs - 1):
            ref[i, :PAD] = jnp.zeros((PAD, lanes), F32)
            ref[i, rows - PAD :] = jnp.zeros((PAD, lanes), F32)


def table(rows, cols, of, value=1.0):
    k = lax.broadcasted_iota(jnp.int32, (rows, cols), 0)
    c = lax.broadcasted_iota(jnp.int32, (rows, cols), 1)
    return jnp.where(of(k, c), F32(value), F32(0.0)).astype(BF16)


def dot(a, m):
    high = a.astype(BF16)
    rest = a - high.astype(F32)
    middle = rest.astype(BF16)
    low = (rest - middle.astype(F32)).astype(BF16)
    parts = jnp.concatenate([high, middle, low], axis=1)
    return jnp.dot(parts, jnp.concatenate([m, m, m], axis=0), preferred_element_type=F32)


def pack_kernel(start_hbm, right_hbm, s, up, down, start, right, sem_a, sem_b):
    copy_a = pltpu.make_async_copy(start_hbm, start, sem_a)
    copy_b = pltpu.make_async_copy(right_hbm, right, sem_b)
    copy_a.start()
    copy_b.start()
    even = even_mask((64, 128))
    low = lane_of((64, 128)) < 64
    copy_a.wait()
    copy_b.wait()
    for p in range(4):
        s[p] = jnp.where(even, start[2 * p + 1], start[2 * p])
        s[p + 4] = jnp.where(even, right[2 * p], right[2 * p + 1])
        s[p + 8] = jnp.where(even, right[2 * p + 1], right[2 * p])
    for p in range(6):
        a, b = s[p], pltpu.roll(s[p + 6], 64, 1)
        up[p] = jnp.where(low, b, a)
        down[p] = jnp.where(low, a, b)


def widen_kernel(s, up, down, v, first, last):
    low = lane_of((64, 128)) < 64
    for p in range(6):
        v[p] = jnp.where(low, down[p], up[p])
        v[p + 6] = pltpu.roll(jnp.where(low, up[p], down[p]), 64, 1)
    for p in range(12):
        first[p, :, :128] = s[p, :EY]
        first[p, :, 128:] = v[p, :EY]
        last[p, :, :128] = s[p, 64 - EY :]
        last[p, :, 128:] = v[p, 64 - EY :]


def strips_kernel(before, after, up, down):
    for a in range(3):
        for q in range(2):
            for ref, near, far in ((up, 2 + q, q), (down, q, 2 + q)):
                j = 2 * a + q
                ref[j, :EY] = before[4 * a + near]
                ref[j, EY : 2 * EY] = after[4 * a + near]
                ref[j, 48:56] = before[4 * a + far, EY - 8 :]
                ref[j, 56:64] = after[4 * a + far, :8]


def fine_down_kernel(
    n, s, v, before, after, s_left, s_right, v_left, v_right, y_left, y_right,
    coarse, black_out, red_b_out, black_b_out, red, black, rb, bb, weight, pairs,
):
    gx, gy, gz = (lax.axis_index(a) for a in ("gx", "gy", "gz"))
    inner = domain((ROWS0, 256), 64 * gy - EY, 64 * n[1], 128 * gz, 128 * n[2], 192)
    has_left, has_right = gx > 0, gx < n[0] - 1
    weight[0] = jnp.where(has_left, inner, 0.0)
    weight[1] = inner
    weight[2] = jnp.where(has_right, inner, 0.0)
    clear_pads(black, red)
    zero8 = jnp.zeros((8, 256), F32)
    for a, ref in enumerate((black, rb, bb)):
        off, top = (1, PAD) if a == 0 else (0, 0)
        mid, end = top + EY, top + EY + 64

        def put(i, lo, value, keep, ref=ref, off=off, a=a):
            hi = lo + value.shape[0]
            lanes = slice(0, 256) if value.shape[1] == 256 else keep[1]
            if a == 0 and keep[0] is not None:
                value = jnp.where(keep[0], value, 0.0)
            ref[i + off, lo:hi, lanes] = value

        for p in range(4):
            j = 4 * a + p
            for base, centre, strip, there in ((4, s, v, None), (0, s_left, v_left, has_left), (8, s_right, v_right, has_right)):
                put(base + p, mid, centre[j], (there, slice(0, 128)))
                put(base + p, mid, strip[j], (there, slice(128, 256)))
            put(4 + p, top, before[j], (None, None))
            put(4 + p, end, after[j], (None, None))
        for q in range(2):
            j = 2 * a + q
            for base, y, near, far, there in ((0, y_left, 2 + q, q, has_left), (8, y_right, q, 2 + q, has_right)):
                put(base + near, top, y[j, :EY], (there, None))
                put(base + near, end, y[j, EY : 2 * EY], (there, None))
                for k in range(2):
                    put(base + far, top + 8 * k, zero8, (None, None))
                    put(base + far, end + 8 + 8 * k, zero8, (None, None))
                put(base + far, mid - 8, y[j, 48:56], (there, None))
                put(base + far, end, y[j, 56:64], (there, None))

    def weights(i, r, step):
        return weight[i // 4, r : r + step]

    half(red, black, rb, weights, True, range(0, 12), ROWS0, 16)
    half(black, red, bb, weights, False, range(1, 11), ROWS0, 16)
    half(red, black, rb, weights, True, range(1, 11), ROWS0, 16)
    half(black, red, bb, weights, False, range(2, 10), ROWS0, 16)
    even = even_mask((16, 256))
    for p in range(4):
        for r in range(0, ROWS0, 16):
            value = residual_sum(red, black, rb, bb, p + 4, r, 16, even)
            pairs[2 * p, r : r + 16] = value[:, :128]
            pairs[2 * p + 1, r : r + 16] = value[:, 128:]
    rows = []
    for p in range(4):
        parts = [pairs[2 * p + h, pl.ds(0, ROWS1, stride=2), :] + pairs[2 * p + h, pl.ds(1, ROWS1, stride=2), :] for h in (0, 1)]
        rows.append(jnp.concatenate(parts, axis=1))
    result = dot(jnp.concatenate(rows, axis=0), table(256, 128, lambda k, c: (k >> 1) == c, 0.5))
    for p in range(4):
        coarse[p] = result[p * ROWS1 : (p + 1) * ROWS1]
    for p in range(8):
        black_out[p] = black[p + 3, PAD + UP0 : PAD + UP0 + 80]
        red_b_out[p] = rb[p + 2, UP0 : UP0 + 80]
        black_b_out[p] = bb[p + 2, UP0 : UP0 + 80]


def middle_down_kernel(n, b1, coarse, black_out, red_b_out, black_b_out, red, black, rb, bb, weight, pairs):
    gx, gy, gz = (lax.axis_index(a) for a in ("gx", "gy", "gz"))
    count = 2 * n[0]
    even = even_mask((ROWS1, 128))
    weight[...] = domain((ROWS1, 128), 32 * gy - EY // 2, 32 * n[1], 64 * gz, 64 * n[2], 96)
    clear_pads(red, black)
    for i in range(count):
        a, b = b1[2 * i], b1[2 * i + 1]
        r = jnp.where(even, a, b)
        rb[i] = r
        bb[i] = jnp.where(even, b, a)
        red[i + 1, PAD : PAD + ROWS1] = r * weight[...]

    def weights(i, r, step):
        return weight[r : r + step]

    every = range(count)
    half(black, red, bb, weights, False, every, ROWS1, ROWS1)
    half(red, black, rb, weights, True, every, ROWS1, ROWS1)
    half(black, red, bb, weights, False, every, ROWS1, ROWS1)
    for i in range(8):
        q = 2 * gx - 3 + i
        inside = jnp.clip(q, 0, count - 1)
        black_out[i] = black[jnp.clip(q + 1, 0, count + 1), PAD : PAD + ROWS1]
        red_b_out[i] = rb[inside]
        black_b_out[i] = bb[inside]
    top = EY // 2 - 4
    even40 = even_mask((40, 128))
    for i in every:
        pairs[i] = residual_sum(red, black, rb, bb, i, top, 40, even40)
    sums = [pairs[i, pl.ds(4, 16, stride=2), :] + pairs[i, pl.ds(5, 16, stride=2), :] for i in every]
    low = jnp.concatenate(sums[: n[0]], axis=0)
    high = jnp.concatenate(sums[n[0] :], axis=0)
    result = dot(jnp.concatenate([low, high], axis=1), table(256, 128, lambda k, c: (k >> 1) == c, 0.5))
    for i in range(n[0]):
        coarse[i] = result[16 * i : 16 * i + 16]


def widen_coarse_kernel(n, own, left, right, wide):
    lanes = lane_of((16, 128))
    for i in range(n[0]):
        w, a, b = own[i], left[i], right[i]
        a32, a96, b32, b96 = pltpu.roll(a, 32, 1), pltpu.roll(a, 96, 1), pltpu.roll(b, 32, 1), pltpu.roll(b, 96, 1)
        for k, x, y, z0, z1 in ((i, w, b32, a32, a96), (i + n[0], pltpu.roll(w, 64, 1), b96, a96, a32)):
            wide[k] = jnp.where(lanes < 32, x, jnp.where(lanes < 80, y, jnp.where(lanes < 96, z0, z1)))


def up_kernel(
    n, b2, black1, red_b1, black_b1, black0, red_b0, black_b0, out,
    rb2, bb2, red2, black2, weight2, pairs2,
    rb3, bb3, red3, black3, weight3, add2,
    add1, red1, bl1, weight1,
    add0, red0, bl0, weight0,
):
    gx, gy, gz = (lax.axis_index(a) for a in ("gx", "gy", "gz"))
    rows2, rows3 = 16 * n[1], 8 * n[1]
    pairs_2, pairs_3 = n[0], n[0] // 2

    weight2[...] = domain((rows2, 128), 0, rows2, 32 * gz, 32 * n[2], 80)
    clear_pads(red2, black2)
    even16 = even_mask((16, 128))
    for i in range(pairs_2):
        for g in range(n[1]):
            a, b = b2[g, 2 * i], b2[g, 2 * i + 1]
            at = 16 * g
            r = jnp.where(even16, a, b)
            rb2[i, at : at + 16] = r
            bb2[i, at : at + 16] = jnp.where(even16, b, a)
            red2[i + 1, PAD + at : PAD + at + 16] = r * weight2[at : at + 16]

    def weights2(i, r, step):
        return weight2[r : r + step]

    every2 = range(pairs_2)
    half(black2, red2, bb2, weights2, False, every2, rows2, rows2)
    half(red2, black2, rb2, weights2, True, every2, rows2, rows2)
    half(black2, red2, bb2, weights2, False, every2, rows2, rows2)
    even2 = even_mask((rows2, 128))
    for i in every2:
        pairs2[i] = residual_sum(red2, black2, rb2, bb2, i, 0, rows2, even2)
    sums = [pairs2[i, pl.ds(0, rows3, stride=2), :] + pairs2[i, pl.ds(1, rows3, stride=2), :] for i in every2]
    to3 = lambda k, c: jnp.where(k < 80, k >> 1, (k >> 1) + 64) == c
    b3 = dot(jnp.concatenate(sums, axis=0), table(128, 128, to3, 0.5))

    even3 = even_mask((rows3, 128))
    weight3[...] = domain((rows3, 128), 0, rows3, 16 * gz, 16 * n[2], 64, (40, 104))
    clear_pads(red3, black3)
    for i in range(pairs_3):
        a = b3[2 * i * rows3 : (2 * i + 1) * rows3]
        b = b3[(2 * i + 1) * rows3 : (2 * i + 2) * rows3]
        r = jnp.where(even3, a, b)
        rb3[i] = r
        bb3[i] = jnp.where(even3, b, a)
        red3[i + 1, PAD : PAD + rows3] = r * weight3[...]

    def weights3(i, r, step):
        return weight3[r : r + step]

    every3 = range(pairs_3)
    half(black3, red3, bb3, weights3, False, every3, rows3, rows3)

    def sweep3(_, carry):
        half(red3, black3, rb3, weights3, True, every3, rows3, rows3)
        half(black3, red3, bb3, weights3, False, every3, rows3, rows3)
        return carry

    lax.fori_loop(0, 7, sweep3, 0)
    planes = []
    for i in every3:
        r, b = red3[i + 1, PAD : PAD + rows3], black3[i + 1, PAD : PAD + rows3]
        planes += [jnp.where(even3, r, b), jnp.where(even3, b, r)]
    wide = dot(jnp.concatenate(planes, axis=0), table(128, 128, lambda k, c: to3(c, k)))
    for i in every2:
        w = wide[i * rows3 : (i + 1) * rows3]
        add2[i, pl.ds(0, rows3, stride=2), :] = w
        add2[i, pl.ds(1, rows3, stride=2), :] = w
        black2[i + 1, PAD : PAD + rows2] = black2[i + 1, PAD : PAD + rows2] + add2[i]
    for _ in range(2):
        half(red2, black2, rb2, weights2, True, every2, rows2, rows2)
        half(black2, red2, bb2, weights2, False, every2, rows2, rows2)

    even32 = even_mask((32, 128))
    top = pl.multiple_of(16 * gy, 8)
    planes = []
    for i in range(8):
        q = jnp.clip(gx - 1 + (i + 1) // 2, 0, n[0] + 1)
        r, b = red2[q, pl.ds(top, 32), :], black2[q, pl.ds(top, 32), :]
        planes.append(jnp.where(even32, r, b) if i % 2 == 1 else jnp.where(even32, b, r))
    to2 = lambda k, c: jnp.where(c < 96, c >> 1, (c >> 1) + 64) == k
    wide = dot(jnp.concatenate(planes, axis=0), table(128, 128, to2))
    inner = domain((ROWS1, 128), 32 * gy - EY // 2, 32 * n[1], 64 * gz, 64 * n[2], 96)
    clear_pads(red1, bl1)
    skip = PAD - EY // 4
    for i in range(8):
        q = 2 * gx - 3 + i
        weight1[i] = jnp.where((q >= 0) & (q < 2 * n[0]), inner, 0.0)
        w = wide[32 * i + skip : 32 * i + skip + ROWS1 // 2]
        add1[i, pl.ds(0, ROWS1 // 2, stride=2), :] = w
        add1[i, pl.ds(1, ROWS1 // 2, stride=2), :] = w
        bl1[i + 1, PAD : PAD + ROWS1] = black1[i] + add1[i]

    def weights1(i, r, step):
        return weight1[i, r : r + step]

    half(red1, bl1, red_b1, weights1, True, range(0, 8), ROWS1, ROWS1)
    half(bl1, red1, black_b1, weights1, False, range(1, 7), ROWS1, ROWS1)
    half(red1, bl1, red_b1, weights1, True, range(1, 7), ROWS1, ROWS1)
    half(bl1, red1, black_b1, weights1, False, range(2, 6), ROWS1, ROWS1)

    low1 = PAD + UP0 // 2
    even40 = even_mask((40, 128))
    planes = []
    for i in range(8):
        r, b = red1[3 + i // 2, low1 : low1 + 40], bl1[3 + i // 2, low1 : low1 + 40]
        planes.append(jnp.where(even40, r, b) if i % 2 == 0 else jnp.where(even40, b, r))
    wide = dot(jnp.concatenate(planes, axis=0), table(128, 256, lambda k, c: (c >> 1) == k))
    inner = domain((80, 256), 64 * gy - 8, 64 * n[1], 128 * gz, 128 * n[2], 192)
    weight0[0] = jnp.where(gx > 0, inner, 0.0)
    weight0[1] = inner
    weight0[2] = jnp.where(gx < n[0] - 1, inner, 0.0)
    clear_pads(red0, bl0)
    for i in range(8):
        for h in (0, 1):
            w = wide[40 * i : 40 * i + 40, 128 * h : 128 * h + 128]
            add0[2 * i + h, pl.ds(0, 40, stride=2), :] = w
            add0[2 * i + h, pl.ds(1, 40, stride=2), :] = w
            bl0[i + 1, PAD : PAD + 80, 128 * h : 128 * h + 128] = black0[i, :, 128 * h : 128 * h + 128] + add0[2 * i + h]

    def weights0(i, r, step):
        return weight0[(i + 2) // 4, r : r + step]

    half(red0, bl0, red_b0, weights0, True, range(0, 8), 80, 16)
    half(bl0, red0, black_b0, weights0, False, range(1, 7), 80, 16)
    half(red0, bl0, red_b0, weights0, True, range(1, 7), 80, 16)
    half(bl0, red0, black_b0, weights0, False, range(2, 6), 80, 16)
    even64 = even_mask((64, 128))
    for p in range(4):
        r = red0[p + 3, PAD + 8 : PAD + 72, :128]
        b = bl0[p + 3, PAD + 8 : PAD + 72, :128]
        out[2 * p] = jnp.where(even64, r, b)
        out[2 * p + 1] = jnp.where(even64, b, r)


def from_both(up_value, down_value, axis):
    size = lax.axis_size(axis)
    up = [(i, i + 1) for i in range(size - 1)]
    return lax.ppermute(up_value, axis, up), lax.ppermute(down_value, axis, [(b, a) for a, b in up])


def from_both_round(up_value, down_value, axis):
    size = lax.axis_size(axis)
    up = [(i, (i + 1) % size) for i in range(size)]
    return lax.ppermute(up_value, axis, up), lax.ppermute(down_value, axis, [(b, a) for a, b in up])


def gathered(value, axis):
    copies = jnp.broadcast_to(value, (lax.axis_size(axis), *value.shape))
    return lax.all_to_all(copies, axis, split_axis=0, concat_axis=0, tiled=True)


def local(right_side, start):
    n = tuple(lax.axis_size(a) for a in ("gx", "gy", "gz"))
    block = (12, 64, 128)
    s, up, down = call(
        pack_kernel,
        [block, (6, 64, 128), (6, 64, 128)],
        [(8, 64, 128), (8, 64, 128), pltpu.SemaphoreType.DMA, pltpu.SemaphoreType.DMA],
        [pl.BlockSpec(memory_space=pltpu.HBM)] * 2,
    )(start, right_side)
    s_left, s_right = from_both_round(s, s, "gx")
    up, down = from_both(up, down, "gz")
    v, first, last = call(widen_kernel, [block, (12, EY, 256), (12, EY, 256)])(s, up, down)
    v_left, v_right = from_both_round(v, v, "gx")
    before, after = from_both(last, first, "gy")
    up, down = call(strips_kernel, [(6, 64, 256)] * 2)(before, after)
    y_left, y_right = from_both_round(up, down, "gx")
    up0 = (8, 80, 256)
    b1, black0, red_b0, black_b0 = call(
        functools.partial(fine_down_kernel, n),
        [(4, ROWS1, 128), up0, up0, up0],
        [(14, ROWS0 + 2 * PAD, 256)] * 2 + [(12, ROWS0, 256)] * 2 + [(3, ROWS0, 256), (8, ROWS0, 128)],
    )(s, v, before, after, s_left, s_right, v_left, v_right, y_left, y_right)
    b1 = gathered(b1, "gx").reshape(4 * n[0], ROWS1, 128)
    all1 = (2 * n[0], ROWS1, 128)
    colour1 = (2 * n[0] + 2, ROWS1 + 2 * PAD, 128)
    window1 = (8, ROWS1, 128)
    b2, black1, red_b1, black_b1 = call(
        functools.partial(middle_down_kernel, n),
        [(n[0], 16, 128), window1, window1, window1],
        [colour1, colour1, all1, all1, (ROWS1, 128), (2 * n[0], 40, 128)],
    )(b1)
    left, right = from_both(b2, b2, "gz")
    (b2,) = call(functools.partial(widen_coarse_kernel, n), [(2 * n[0], 16, 128)])(b2, left, right)
    b2 = gathered(b2, "gy").reshape(n[1], 2 * n[0], 16, 128)
    rows2, rows3 = 16 * n[1], 8 * n[1]
    p2, p3 = n[0], n[0] // 2
    colour2, colour3 = (p2 + 2, rows2 + 2 * PAD, 128), (p3 + 2, rows3 + 2 * PAD, 128)
    (out,) = call(
        functools.partial(up_kernel, n),
        [(8, 64, 128)],
        [
            (p2, rows2, 128), (p2, rows2, 128), colour2, colour2, (rows2, 128), (p2, rows2, 128),
            (p3, rows3, 128), (p3, rows3, 128), colour3, colour3, (rows3, 128), (p2, rows2, 128),
            window1, (10, ROWS1 + 2 * PAD, 128), (10, ROWS1 + 2 * PAD, 128), window1,
            (16, 80, 128), (10, 80 + 2 * PAD, 256), (10, 80 + 2 * PAD, 256), (3, 80, 256),
        ],
    )(b2, black1, red_b1, black_b1, black0, red_b0, black_b0)
    return out


def solution(mesh):
    in_specs = (P("gx", "gy", "gz"), P("gx", "gy", "gz"))
    out_specs = P("gx", "gy", "gz")
    return jax.shard_map(local, mesh=mesh, in_specs=in_specs, out_specs=out_specs, check_vma=False)
```

```python
import functools

import jax
import jax.numpy as jnp
from jax import lax
from jax.experimental import pallas as pl
from jax.experimental.pallas import tpu as pltpu
from jax.sharding import PartitionSpec as P

F32 = jnp.float32
BF16 = jnp.bfloat16
SIXTH = 1.0 / 6.0
EY = 24
ROWS0 = 64 + 2 * EY
ROWS1 = ROWS0 // 2
SENT1 = ROWS1 - 8
PAD = 8
UP0 = EY - 8
VMEM_LIMIT = 40 * 1024 * 1024


def call(kernel, outs, scratch=(), in_specs=None):
    shapes = [jax.ShapeDtypeStruct(s, F32) for s in outs]
    extra = {} if in_specs is None else {"in_specs": in_specs}
    return pl.pallas_call(
        kernel,
        out_shape=shapes,
        scratch_shapes=[pltpu.VMEM(s, F32) if isinstance(s, tuple) else s for s in scratch],
        compiler_params=pltpu.CompilerParams(vmem_limit_bytes=VMEM_LIMIT),
        **extra,
    )


def even_mask(shape):
    rows = lax.broadcasted_iota(jnp.int32, shape, 0)
    lanes = lax.broadcasted_iota(jnp.int32, shape, 1)
    return ((rows + lanes) & 1) == 0


def lane_of(shape):
    return lax.broadcasted_iota(jnp.int32, shape, 1)


def domain(shape, row0, rows, lane0, lanes, cut, unused=None):
    y = lax.broadcasted_iota(jnp.int32, shape, 0) + row0
    k = lane_of(shape)
    z = jnp.where(k < cut, k, k - shape[1]) + lane0
    inside = (y >= 0) & (y < rows) & (z >= 0) & (z < lanes)
    if unused is not None:
        inside = inside & ((k < unused[0]) | (k >= unused[1]))
    return jnp.where(inside, F32(SIXTH), F32(0.0))


def beside(src, i, r, rows, even, red):
    at = PAD + r
    c = src[i + 1, at : at + rows]
    below, above = src[i, at : at + rows], src[i + 2, at : at + rows]
    s = c + (jnp.where(even, below, above) if red else jnp.where(even, above, below))
    s = s + (src[i + 1, at - 1 : at - 1 + rows] + src[i + 1, at + 1 : at + 1 + rows])
    return s + (pltpu.roll(c, 1, 1) + pltpu.roll(c, c.shape[1] - 1, 1))


def half(dst, src, b, weight, red, pairs, rows, step):
    even = even_mask((step, dst.shape[2]))
    for i in pairs:
        for r in range(0, rows, step):
            value = (b[i, r : r + step] + beside(src, i, r, step, even, red)) * weight(i, r, step)
            dst[i + 1, PAD + r : PAD + r + step] = value


def residual_sum(red, black, red_b, black_b, i, r, step, even):
    at = PAD + r
    x = red_b[i, r : r + step] - 6.0 * red[i + 1, at : at + step] + beside(black, i, r, step, even, True)
    y = black_b[i, r : r + step] - 6.0 * black[i + 1, at : at + step] + beside(red, i, r, step, even, False)
    return x + y


def clear_pads(*colours):
    for ref in colours:
        pairs, rows, lanes = ref.shape
        for i in (0, pairs - 1):
            ref[i] = jnp.zeros((rows, lanes), F32)
        for i in range(1, pairs - 1):
            ref[i, :PAD] = jnp.zeros((PAD, lanes), F32)
            ref[i, rows - PAD :] = jnp.zeros((PAD, lanes), F32)


def table(rows, cols, of, value=1.0):
    k = lax.broadcasted_iota(jnp.int32, (rows, cols), 0)
    c = lax.broadcasted_iota(jnp.int32, (rows, cols), 1)
    return jnp.where(of(k, c), F32(value), F32(0.0)).astype(BF16)


def dot(a, m):
    high = a.astype(BF16)
    rest = a - high.astype(F32)
    middle = rest.astype(BF16)
    low = (rest - middle.astype(F32)).astype(BF16)
    parts = jnp.concatenate([high, middle, low], axis=1)
    return jnp.dot(parts, jnp.concatenate([m, m, m], axis=0), preferred_element_type=F32)


def pack_kernel(start_hbm, right_hbm, s, up, down, start, right, sem_a, sem_b):
    copy_a = pltpu.make_async_copy(start_hbm, start, sem_a)
    copy_b = pltpu.make_async_copy(right_hbm, right, sem_b)
    copy_a.start()
    copy_b.start()
    even = even_mask((64, 128))
    low = lane_of((64, 128)) < 64
    copy_a.wait()
    copy_b.wait()
    for p in range(4):
        s[p] = jnp.where(even, start[2 * p + 1], start[2 * p])
        s[p + 4] = jnp.where(even, right[2 * p], right[2 * p + 1])
        s[p + 8] = jnp.where(even, right[2 * p + 1], right[2 * p])
    for p in range(6):
        a, b = s[p], pltpu.roll(s[p + 6], 64, 1)
        up[p] = jnp.where(low, b, a)
        down[p] = jnp.where(low, a, b)


def widen_kernel(s, up, down, sv, first, last):
    low = lane_of((64, 128)) < 64
    for p in range(6):
        sv[p + 12] = jnp.where(low, down[p], up[p])
        sv[p + 18] = pltpu.roll(jnp.where(low, up[p], down[p]), 64, 1)
    for p in range(12):
        sv[p] = s[p]
        first[p, :, :128] = s[p, :EY]
        first[p, :, 128:] = sv[p + 12, :EY]
        last[p, :, :128] = s[p, 64 - EY :]
        last[p, :, 128:] = sv[p + 12, 64 - EY :]


def strips_kernel(before, after, up, down):
    for a in range(3):
        for q in range(2):
            for ref, near, far in ((up, 2 + q, q), (down, q, 2 + q)):
                j = 2 * a + q
                ref[j, :EY] = before[4 * a + near]
                ref[j, EY : 2 * EY] = after[4 * a + near]
                ref[j, 48:56] = before[4 * a + far, EY - 8 :]
                ref[j, 56:64] = after[4 * a + far, :8]


def fine_down_kernel(
    n, s, before, after, s_left, s_right, y_left, y_right,
    coarse, sent, black_out, red_b_out, black_b_out, red, black, rb, bb, weight, pairs,
):
    gx, gy, gz = (lax.axis_index(a) for a in ("gx", "gy", "gz"))
    inner = domain((ROWS0, 256), 64 * gy - EY, 64 * n[1], 128 * gz, 128 * n[2], 192)
    has_left, has_right = gx > 0, gx < n[0] - 1
    weight[0] = jnp.where(has_left, inner, 0.0)
    weight[1] = inner
    weight[2] = jnp.where(has_right, inner, 0.0)
    clear_pads(black, red)
    zero8 = jnp.zeros((8, 256), F32)
    for a, ref in enumerate((black, rb, bb)):
        off, top = (1, PAD) if a == 0 else (0, 0)
        mid, end = top + EY, top + EY + 64

        def put(i, lo, value, keep, ref=ref, off=off, a=a):
            hi = lo + value.shape[0]
            lanes = slice(0, 256) if value.shape[1] == 256 else keep[1]
            if a == 0 and keep[0] is not None:
                value = jnp.where(keep[0], value, 0.0)
            ref[i + off, lo:hi, lanes] = value

        for p in range(4):
            j = 4 * a + p
            for base, whole, there in ((4, s, None), (0, s_left, has_left), (8, s_right, has_right)):
                put(base + p, mid, whole[j], (there, slice(0, 128)))
                put(base + p, mid, whole[j + 12], (there, slice(128, 256)))
            put(4 + p, top, before[j], (None, None))
            put(4 + p, end, after[j], (None, None))
        for q in range(2):
            j = 2 * a + q
            for base, y, near, far, there in ((0, y_left, 2 + q, q, has_left), (8, y_right, q, 2 + q, has_right)):
                put(base + near, top, y[j, :EY], (there, None))
                put(base + near, end, y[j, EY : 2 * EY], (there, None))
                for k in range(2):
                    put(base + far, top + 8 * k, zero8, (None, None))
                    put(base + far, end + 8 + 8 * k, zero8, (None, None))
                put(base + far, mid - 8, y[j, 48:56], (there, None))
                put(base + far, end, y[j, 56:64], (there, None))

    def weights(i, r, step):
        return weight[i // 4, r : r + step]

    half(red, black, rb, weights, True, range(0, 12), ROWS0, 16)
    half(black, red, bb, weights, False, range(1, 11), ROWS0, 16)
    half(red, black, rb, weights, True, range(1, 11), ROWS0, 16)
    half(black, red, bb, weights, False, range(2, 10), ROWS0, 16)
    even = even_mask((16, 256))
    for p in range(4):
        for r in range(0, ROWS0, 16):
            value = residual_sum(red, black, rb, bb, p + 4, r, 16, even)
            pairs[2 * p, r : r + 16] = value[:, :128]
            pairs[2 * p + 1, r : r + 16] = value[:, 128:]
    rows = []
    for p in range(4):
        parts = [pairs[2 * p + h, pl.ds(0, ROWS1, stride=2), :] + pairs[2 * p + h, pl.ds(1, ROWS1, stride=2), :] for h in (0, 1)]
        rows.append(jnp.concatenate(parts, axis=1))
    result = dot(jnp.concatenate(rows, axis=0), table(256, 128, lambda k, c: (k >> 1) == c, 0.5))
    for p in range(4):
        coarse[p] = result[p * ROWS1 : (p + 1) * ROWS1]
        sent[p] = coarse[p, 4 : 4 + SENT1]
    for p in range(8):
        black_out[p] = black[p + 3, PAD + UP0 : PAD + UP0 + 80]
        red_b_out[p] = rb[p + 2, UP0 : UP0 + 80]
        black_b_out[p] = bb[p + 2, UP0 : UP0 + 80]


def middle_down_kernel(
    n, own, same, other, coarse, black_out, red_b_out, black_b_out, red, black, rb, bb, weight, pairs
):
    gx, gy, gz = (lax.axis_index(a) for a in ("gx", "gy", "gz"))
    count = 2 * n[0]
    core = gx % 2
    even = even_mask((ROWS1, 128))
    even_sent = even_mask((SENT1, 128))
    weight[...] = domain((ROWS1, 128), 32 * gy - EY // 2, 32 * n[1], 64 * gz, 64 * n[2], 96)
    clear_pads(red, black)
    zero4 = jnp.zeros((4, 128), F32)
    for i in range(count):
        block, q = i // 2, 2 * (i % 2)
        mine = core == block % 2
        a = jnp.where(mine, same[block // 2, q], other[block // 2, q])
        b = jnp.where(mine, same[block // 2, q + 1], other[block // 2, q + 1])
        for ref, v in ((rb, jnp.where(even_sent, a, b)), (bb, jnp.where(even_sent, b, a))):
            ref[i, :4] = zero4
            ref[i, 4 : 4 + SENT1] = v
            ref[i, 4 + SENT1 :] = zero4
    for h in range(2):
        a, b = own[2 * h], own[2 * h + 1]
        rb[2 * gx + h] = jnp.where(even, a, b)
        bb[2 * gx + h] = jnp.where(even, b, a)
    for i in range(count):
        red[i + 1, PAD : PAD + ROWS1] = rb[i] * weight[...]

    def weights(i, r, step):
        return weight[r : r + step]

    every = range(count)
    half(black, red, bb, weights, False, every, ROWS1, ROWS1)
    half(red, black, rb, weights, True, every, ROWS1, ROWS1)
    half(black, red, bb, weights, False, every, ROWS1, ROWS1)
    for i in range(8):
        q = 2 * gx - 3 + i
        inside = jnp.clip(q, 0, count - 1)
        black_out[i] = black[jnp.clip(q + 1, 0, count + 1), PAD : PAD + ROWS1]
        red_b_out[i] = rb[inside]
        black_b_out[i] = bb[inside]
    top = EY // 2 - 4
    even40 = even_mask((40, 128))
    for i in every:
        pairs[i] = residual_sum(red, black, rb, bb, i, top, 40, even40)
    sums = [pairs[i, pl.ds(4, 16, stride=2), :] + pairs[i, pl.ds(5, 16, stride=2), :] for i in every]
    to2 = lambda k: jnp.where(k < 96, (k >> 1) + 16, (k >> 1) - 48)
    low = jnp.concatenate(sums[: n[0]], axis=0)
    high = jnp.concatenate(sums[n[0] :], axis=0)
    take = table(256, 128, lambda k, c: to2(k & 127) + (k & 128) // 2 == c, 0.5)
    result = dot(jnp.concatenate([low, high], axis=1), take)
    for i in range(n[0]):
        coarse[i] = result[16 * i : 16 * i + 16]


def wrap_pairs(ref, rows):
    last = ref.shape[0] - 2
    low = lane_of((rows, 128)) < 64
    ref[0, PAD : PAD + rows] = jnp.where(low, 0.0, pltpu.roll(ref[last, PAD : PAD + rows], 64, 1))
    ref[last + 1, PAD : PAD + rows] = jnp.where(low, pltpu.roll(ref[1, PAD : PAD + rows], 64, 1), 0.0)


def domain2(n, gz, rows):
    y = lane_of((rows, 128))
    z = (y & 63) - 16 + 32 * gz
    return jnp.where((z >= 0) & (z < 32 * n[2]), F32(SIXTH), F32(0.0))


def third_place(n, i):
    packed = n[0] // 2
    arrays = max(1, packed // 2)
    p = i % packed
    return p % arrays, 64 * (i // packed) + 32 * (p // arrays)


def coarse_down_kernel(n, b2, coarse, black_out, rb, bb, red, black, weight, pairs):
    gz = lax.axis_index("gz")
    rows, packed = 16 * n[1], n[0] // 2
    weight[...] = domain2(n, gz, rows)
    clear_pads(red, black)
    even16 = even_mask((16, 128))
    for i in range(packed):
        for g in range(n[1]):
            a, b = b2[g, 2 * i], b2[g, 2 * i + 1]
            at = 16 * g
            r = jnp.where(even16, a, b)
            rb[i, at : at + 16] = r
            bb[i, at : at + 16] = jnp.where(even16, b, a)
            red[i + 1, PAD + at : PAD + at + 16] = r * weight[at : at + 16]

    def weights(i, r, step):
        return weight[r : r + step]

    every = range(packed)
    wrap_pairs(red, rows)
    half(black, red, bb, weights, False, every, rows, rows)
    wrap_pairs(black, rows)
    half(red, black, rb, weights, True, every, rows, rows)
    wrap_pairs(red, rows)
    half(black, red, bb, weights, False, every, rows, rows)
    wrap_pairs(black, rows)
    even = even_mask((rows, 128))
    for i in every:
        pairs[i] = residual_sum(red, black, rb, bb, i, 0, rows, even)
        black_out[i] = black[i + 1, PAD : PAD + rows]
    rows3 = rows // 2
    sums = [pairs[i, pl.ds(0, rows3, stride=2), :] + pairs[i, pl.ds(1, rows3, stride=2), :] for i in every]
    take = table(128, 128, lambda k, c: ((k & 63) >> 1) + (k & 64) == c, 0.5)
    result = dot(jnp.concatenate(sums, axis=0), take)
    arrays = coarse.shape[0]
    for r in range(arrays):
        total = result[r * rows3 : (r + 1) * rows3]
        if packed > arrays:
            total = total + pltpu.roll(result[(r + arrays) * rows3 : (r + arrays + 1) * rows3], 32, 1)
        coarse[r] = total


def up_kernel(
    n, b3, b3_left, b3_right, start2, rb2, bb2, black1, red_b1, black_b1, black0, red_b0, black_b0, out,
    red2, black2, weight2,
    rb3, bb3, red3, black3, weight3, add2,
    add1, red1, bl1, weight1,
    add0, red0, bl0, weight0,
):
    gx, gy, gz = (lax.axis_index(a) for a in ("gx", "gy", "gz"))
    rows2, rows3 = 16 * n[1], 8 * n[1]
    packed, pairs_3 = n[0] // 2, n[0] // 2

    shape3 = (rows3, 128)
    even3 = even_mask(shape3)
    lane3 = lane_of(shape3)
    z3 = lane3 - 24 + 16 * gz
    weight3[...] = jnp.where((z3 >= 0) & (z3 < 16 * n[2]) & (lane3 < 64), F32(SIXTH), F32(0.0))
    clear_pads(red3, black3)

    def plane3(i):
        at, lane = third_place(n, i)
        own, left, right = (pltpu.roll(ref[at], (to - lane) % 128, 1) if (to - lane) % 128 else ref[at] for ref, to in ((b3, 16), (b3_left, 0), (b3_right, 32)))
        return jnp.where(lane3 < 24, left, jnp.where(lane3 < 40, own, right))

    for i in range(pairs_3):
        a, b = plane3(2 * i), plane3(2 * i + 1)
        r = jnp.where(even3, a, b)
        rb3[i] = r
        bb3[i] = jnp.where(even3, b, a)
        red3[i + 1, PAD : PAD + rows3] = r * weight3[...]

    def weights3(i, r, step):
        return weight3[r : r + step]

    every3 = range(pairs_3)
    half(black3, red3, bb3, weights3, False, every3, rows3, rows3)

    def sweep3(_, carry):
        half(red3, black3, rb3, weights3, True, every3, rows3, rows3)
        half(black3, red3, bb3, weights3, False, every3, rows3, rows3)
        return carry

    lax.fori_loop(0, 7, sweep3, 0)
    planes = []
    for i in every3:
        r, b = red3[i + 1, PAD : PAD + rows3], black3[i + 1, PAD : PAD + rows3]
        planes += [jnp.where(even3, r, b), jnp.where(even3, b, r)]

    halves = [jnp.concatenate(planes[:packed], axis=0), jnp.concatenate(planes[packed:], axis=0)]
    spread = table(256, 128, lambda k, c: ((c & 63) >> 1) + 16 + 2 * (c & 64) == k)
    wide = dot(jnp.concatenate(halves, axis=1), spread)
    weight2[...] = domain2(n, gz, rows2)
    clear_pads(red2, black2)
    every2 = range(packed)
    for i in every2:
        w = wide[i * rows3 : (i + 1) * rows3]
        add2[i, pl.ds(0, rows3, stride=2), :] = w
        add2[i, pl.ds(1, rows3, stride=2), :] = w
        black2[i + 1, PAD : PAD + rows2] = start2[i] + add2[i]

    def weights2(i, r, step):
        return weight2[r : r + step]

    for _ in range(2):
        wrap_pairs(black2, rows2)
        half(red2, black2, rb2, weights2, True, every2, rows2, rows2)
        wrap_pairs(red2, rows2)
        half(black2, red2, bb2, weights2, False, every2, rows2, rows2)

    even32 = even_mask((32, 128))
    top = pl.multiple_of(16 * gy, 8)
    planes = []
    second = lane_of((32, 128)) >= 64
    for i in range(8):
        q = gx - 2 + (i + 1) // 2
        there = (q >= 0) & (q < n[0])
        upper = q >= packed
        at = jnp.clip(jnp.where(upper, q - packed, q), 0, packed - 1) + 1
        r, b = red2[at, pl.ds(top, 32), :], black2[at, pl.ds(top, 32), :]
        plane = jnp.where(even32, r, b) if i % 2 == 1 else jnp.where(even32, b, r)
        planes.append(jnp.where(there & (second == upper), plane, 0.0))
    to2 = lambda k, c: jnp.where(c < 96, (c >> 1) + 16, (c >> 1) - 48) == (k & 63)
    wide = dot(jnp.concatenate(planes, axis=0), table(128, 128, to2))
    inner = domain((ROWS1, 128), 32 * gy - EY // 2, 32 * n[1], 64 * gz, 64 * n[2], 96)
    clear_pads(red1, bl1)
    skip = PAD - EY // 4
    for i in range(8):
        q = 2 * gx - 3 + i
        weight1[i] = jnp.where((q >= 0) & (q < 2 * n[0]), inner, 0.0)
        w = wide[32 * i + skip : 32 * i + skip + ROWS1 // 2]
        add1[i, pl.ds(0, ROWS1 // 2, stride=2), :] = w
        add1[i, pl.ds(1, ROWS1 // 2, stride=2), :] = w
        bl1[i + 1, PAD : PAD + ROWS1] = black1[i] + add1[i]

    def weights1(i, r, step):
        return weight1[i, r : r + step]

    half(red1, bl1, red_b1, weights1, True, range(0, 8), ROWS1, ROWS1)
    half(bl1, red1, black_b1, weights1, False, range(1, 7), ROWS1, ROWS1)
    half(red1, bl1, red_b1, weights1, True, range(1, 7), ROWS1, ROWS1)
    half(bl1, red1, black_b1, weights1, False, range(2, 6), ROWS1, ROWS1)

    low1 = PAD + UP0 // 2
    even40 = even_mask((40, 128))
    planes = []
    for i in range(8):
        r, b = red1[3 + i // 2, low1 : low1 + 40], bl1[3 + i // 2, low1 : low1 + 40]
        planes.append(jnp.where(even40, r, b) if i % 2 == 0 else jnp.where(even40, b, r))
    wide = dot(jnp.concatenate(planes, axis=0), table(128, 256, lambda k, c: (c >> 1) == k))
    inner = domain((80, 256), 64 * gy - 8, 64 * n[1], 128 * gz, 128 * n[2], 192)
    weight0[0] = jnp.where(gx > 0, inner, 0.0)
    weight0[1] = inner
    weight0[2] = jnp.where(gx < n[0] - 1, inner, 0.0)
    clear_pads(red0, bl0)
    for i in range(8):
        for h in (0, 1):
            w = wide[40 * i : 40 * i + 40, 128 * h : 128 * h + 128]
            add0[2 * i + h, pl.ds(0, 40, stride=2), :] = w
            add0[2 * i + h, pl.ds(1, 40, stride=2), :] = w
            bl0[i + 1, PAD : PAD + 80, 128 * h : 128 * h + 128] = black0[i, :, 128 * h : 128 * h + 128] + add0[2 * i + h]

    def weights0(i, r, step):
        return weight0[(i + 2) // 4, r : r + step]

    half(red0, bl0, red_b0, weights0, True, range(0, 8), 80, 16)
    half(bl0, red0, black_b0, weights0, False, range(1, 7), 80, 16)
    half(red0, bl0, red_b0, weights0, True, range(1, 7), 80, 16)
    half(bl0, red0, black_b0, weights0, False, range(2, 6), 80, 16)
    even64 = even_mask((64, 128))
    for p in range(4):
        r = red0[p + 3, PAD + 8 : PAD + 72, :128]
        b = bl0[p + 3, PAD + 8 : PAD + 72, :128]
        out[2 * p] = jnp.where(even64, r, b)
        out[2 * p + 1] = jnp.where(even64, b, r)


def from_both(up_value, down_value, axis):
    size = lax.axis_size(axis)
    up = [(i, i + 1) for i in range(size - 1)]
    return lax.ppermute(up_value, axis, up), lax.ppermute(down_value, axis, [(b, a) for a, b in up])


def from_both_round(up_value, down_value, axis):
    size = lax.axis_size(axis)
    up = [(i, (i + 1) % size) for i in range(size)]
    return lax.ppermute(up_value, axis, up), lax.ppermute(down_value, axis, [(b, a) for a, b in up])


def gathered(value, axis, groups=None):
    size = lax.axis_size(axis) if groups is None else len(groups[0])
    copies = jnp.broadcast_to(value, (size, *value.shape))
    return lax.all_to_all(copies, axis, split_axis=0, concat_axis=0, axis_index_groups=groups, tiled=True)


def local(right_side, start):
    n = tuple(lax.axis_size(a) for a in ("gx", "gy", "gz"))
    s, up, down = call(
        pack_kernel,
        [(12, 64, 128), (6, 64, 128), (6, 64, 128)],
        [(8, 64, 128), (8, 64, 128), pltpu.SemaphoreType.DMA, pltpu.SemaphoreType.DMA],
        [pl.BlockSpec(memory_space=pltpu.HBM)] * 2,
    )(start, right_side)
    up, down = from_both(up, down, "gz")
    sv, first, last = call(widen_kernel, [(24, 64, 128), (12, EY, 256), (12, EY, 256)])(s, up, down)
    s_left, s_right = from_both_round(sv, sv, "gx")
    before, after = from_both(last, first, "gy")
    up, down = call(strips_kernel, [(6, 64, 256)] * 2)(before, after)
    y_left, y_right = from_both_round(up, down, "gx")
    up0 = (8, 80, 256)
    b1, sent, black0, red_b0, black_b0 = call(
        functools.partial(fine_down_kernel, n),
        [(4, ROWS1, 128), (4, SENT1, 128), up0, up0, up0],
        [(14, ROWS0 + 2 * PAD, 256)] * 2 + [(12, ROWS0, 256)] * 2 + [(3, ROWS0, 256), (8, ROWS0, 128)],
    )(sv, before, after, s_left, s_right, y_left, y_right)
    groups = [[2 * chip + core for chip in range(n[0] // 2)] for core in range(2)]
    same = gathered(sent[None], "gx", groups)
    other = lax.ppermute(same, "gx", [(i, i ^ 1) for i in range(n[0])])
    all1 = (2 * n[0], ROWS1, 128)
    colour1 = (2 * n[0] + 2, ROWS1 + 2 * PAD, 128)
    window1 = (8, ROWS1, 128)
    blocks = (n[0] // 2, 4, SENT1, 128)
    b2, black1, red_b1, black_b1 = call(
        functools.partial(middle_down_kernel, n),
        [(n[0], 16, 128), window1, window1, window1],
        [colour1, colour1, all1, all1, (ROWS1, 128), (2 * n[0], 40, 128)],
    )(b1, same.reshape(blocks), other.reshape(blocks))
    b2 = gathered(b2, "gy").reshape(n[1], n[0], 16, 128)
    rows2, rows3 = 16 * n[1], 8 * n[1]
    packed = n[0] // 2
    all2, colour2, colour3 = (packed, rows2, 128), (packed + 2, rows2 + 2 * PAD, 128), (packed + 2, rows3 + 2 * PAD, 128)
    b3, black2, red_b2, black_b2 = call(
        functools.partial(coarse_down_kernel, n),
        [(max(1, packed // 2), rows3, 128), all2, all2, all2],
        [colour2, colour2, (rows2, 128), all2],
    )(b2)
    left, right = from_both(b3, b3, "gz")
    (out,) = call(
        functools.partial(up_kernel, n),
        [(8, 64, 128)],
        [
            colour2, colour2, (rows2, 128),
            (packed, rows3, 128), (packed, rows3, 128), colour3, colour3, (rows3, 128), all2,
            window1, (10, ROWS1 + 2 * PAD, 128), (10, ROWS1 + 2 * PAD, 128), window1,
            (16, 80, 128), (10, 80 + 2 * PAD, 256), (10, 80 + 2 * PAD, 256), (3, 80, 256),
        ],
    )(b3, left, right, black2, red_b2, black_b2, black1, red_b1, black_b1, black0, red_b0, black_b0)
    return out


def solution(mesh):
    in_specs = (P("gx", "gy", "gz"), P("gx", "gy", "gz"))
    out_specs = P("gx", "gy", "gz")
    return jax.shard_map(local, mesh=mesh, in_specs=in_specs, out_specs=out_specs, check_vma=False)
```

```python
import functools

import jax
import jax.numpy as jnp
from jax import lax
from jax.experimental import pallas as pl
from jax.experimental.pallas import tpu as pltpu
from jax.sharding import PartitionSpec as P

F32 = jnp.float32
BF16 = jnp.bfloat16
SIXTH = 1.0 / 6.0
EY = 24
ROWS0 = 64 + 2 * EY
ROWS1 = ROWS0 // 2
SENT1 = 50
SENT1_AT = 3
PAD = 8
UP0 = EY - 8
VMEM_LIMIT = 40 * 1024 * 1024


def call(kernel, outs, scratch=(), in_specs=None):
    shapes = [jax.ShapeDtypeStruct(s, F32) for s in outs]
    extra = {} if in_specs is None else {"in_specs": in_specs}
    return pl.pallas_call(
        kernel,
        out_shape=shapes,
        scratch_shapes=[pltpu.VMEM(s, F32) if isinstance(s, tuple) else s for s in scratch],
        compiler_params=pltpu.CompilerParams(vmem_limit_bytes=VMEM_LIMIT),
        **extra,
    )


def even_mask(shape):
    rows = lax.broadcasted_iota(jnp.int32, shape, 0)
    lanes = lax.broadcasted_iota(jnp.int32, shape, 1)
    return ((rows + lanes) & 1) == 0


def lane_of(shape):
    return lax.broadcasted_iota(jnp.int32, shape, 1)


def domain(shape, row0, rows, lane0, lanes, cut, unused=None):
    y = lax.broadcasted_iota(jnp.int32, shape, 0) + row0
    k = lane_of(shape)
    z = jnp.where(k < cut, k, k - shape[1]) + lane0
    inside = (y >= 0) & (y < rows) & (z >= 0) & (z < lanes)
    if unused is not None:
        inside = inside & ((k < unused[0]) | (k >= unused[1]))
    return jnp.where(inside, F32(SIXTH), F32(0.0))


def beside(src, i, r, rows, even, red):
    at = PAD + r
    c = src[i + 1, at : at + rows]
    below, above = src[i, at : at + rows], src[i + 2, at : at + rows]
    s = c + (jnp.where(even, below, above) if red else jnp.where(even, above, below))
    s = s + (src[i + 1, at - 1 : at - 1 + rows] + src[i + 1, at + 1 : at + 1 + rows])
    return s + (pltpu.roll(c, 1, 1) + pltpu.roll(c, c.shape[1] - 1, 1))


def half(dst, src, b, weight, red, pairs, rows, step):
    even = even_mask((step, dst.shape[2]))
    for i in pairs:
        for r in range(0, rows, step):
            value = (b[i, r : r + step] + beside(src, i, r, step, even, red)) * weight(i, r, step)
            dst[i + 1, PAD + r : PAD + r + step] = value


def residual_sum(red, black, red_b, black_b, i, r, step, even):
    at = PAD + r
    x = red_b[i, r : r + step] - 6.0 * red[i + 1, at : at + step] + beside(black, i, r, step, even, True)
    y = black_b[i, r : r + step] - 6.0 * black[i + 1, at : at + step] + beside(red, i, r, step, even, False)
    return x + y


def clear_pads(*colours):
    for ref in colours:
        pairs, rows, lanes = ref.shape
        for i in (0, pairs - 1):
            ref[i] = jnp.zeros((rows, lanes), F32)
        for i in range(1, pairs - 1):
            ref[i, :PAD] = jnp.zeros((PAD, lanes), F32)
            ref[i, rows - PAD :] = jnp.zeros((PAD, lanes), F32)


def table(rows, cols, of, value=1.0):
    k = lax.broadcasted_iota(jnp.int32, (rows, cols), 0)
    c = lax.broadcasted_iota(jnp.int32, (rows, cols), 1)
    return jnp.where(of(k, c), F32(value), F32(0.0)).astype(BF16)


def dot(a, m):
    high = a.astype(BF16)
    rest = a - high.astype(F32)
    middle = rest.astype(BF16)
    low = (rest - middle.astype(F32)).astype(BF16)
    parts = jnp.concatenate([high, middle, low], axis=1)
    return jnp.dot(parts, jnp.concatenate([m, m, m], axis=0), preferred_element_type=F32)


def pack_kernel(start_hbm, right_hbm, s, up, down, start, right, sem_a, sem_b):
    copy_a = pltpu.make_async_copy(start_hbm, start, sem_a)
    copy_b = pltpu.make_async_copy(right_hbm, right, sem_b)
    copy_a.start()
    copy_b.start()
    even = even_mask((64, 128))
    low = lane_of((64, 128)) < 64
    copy_a.wait()
    copy_b.wait()
    for p in range(4):
        s[p] = jnp.where(even, start[2 * p + 1], start[2 * p])
        s[p + 4] = jnp.where(even, right[2 * p], right[2 * p + 1])
        s[p + 8] = jnp.where(even, right[2 * p + 1], right[2 * p])
    for p in range(6):
        a, b = s[p], pltpu.roll(s[p + 6], 64, 1)
        up[p] = jnp.where(low, b, a)
        down[p] = jnp.where(low, a, b)


def pack16(planes, first=0):
    lanes = lane_of(planes[0].shape)
    total = jnp.zeros(planes[0].shape, F32)
    for k, plane in enumerate(planes):
        at = 16 * (k + first)
        total = jnp.where((lanes >= at) & (lanes < at + 16), pltpu.roll(plane, (8 + at) % 128, 1), total)
    return total


def unpack16(packed, k):
    lanes = lane_of(packed.shape)
    shift = (-8 - 16 * k) % 128
    plane = pltpu.roll(packed, shift, 1) if shift else packed
    return jnp.where((lanes < 8) | (lanes >= 120), plane, 0.0)


UP_NEAR, UP_FAR = (1, 2, 3, 6, 7, 10, 11), (0, 4, 5, 8, 9)
DOWN_NEAR, DOWN_FAR = (0, 1, 2, 4, 5, 8, 9), (3, 6, 7, 10, 11)
NEAR, FAR = len(UP_NEAR), len(UP_FAR)
CROSS_Y = 12 * 24 + 12 * 16 + 2 * 8
STRIP_AT = 48 * NEAR
FAR_AT = STRIP_AT + 32 * NEAR
PACKED_AT = FAR_AT + 16 * FAR
CROSS_X = PACKED_AT + 2 * 16


def widen_kernel(s, up, down, v, v_up, v_down, first, last):
    low = lane_of((64, 128)) < 64
    for p in range(6):
        v[p] = jnp.where(low, down[p], up[p])
        v[p + 6] = pltpu.roll(jnp.where(low, up[p], down[p]), 64, 1)
    for p in range(12):
        first[24 * p : 24 * p + 24] = s[p, :24]
        last[24 * p : 24 * p + 24] = s[p, 40:]
        at = 288 + 16 * p
        first[at : at + 16] = v[p, :16]
        last[at : at + 16] = v[p, 48:]
    for t in range(2):
        at = 480 + 8 * t
        first[at : at + 8] = pack16([v[6 * t + k, 16:24] for k in range(6)])
        last[at : at + 8] = pack16([v[6 * t + k, 40:48] for k in range(6)])
    for ref, near, far in ((v_up, UP_NEAR, UP_FAR), (v_down, DOWN_NEAR, DOWN_FAR)):
        for k, p in enumerate(near):
            ref[k] = v[p]
        ref[NEAR] = pack16([v[p] for p in far])


def strips_kernel(before, after, *rest):
    lanes = lane_of((8, 128))
    for ref, near, far in ((rest[-2], UP_NEAR, UP_FAR), (rest[-1], DOWN_NEAR, DOWN_FAR)):
        outer = [jnp.zeros((8, 128), F32), jnp.zeros((8, 128), F32)]
        for k, p in enumerate(near):
            ref[48 * k : 48 * k + 24] = before[24 * p : 24 * p + 24]
            ref[48 * k + 24 : 48 * k + 48] = after[24 * p : 24 * p + 24]
            at, inner = STRIP_AT + 32 * k, 288 + 16 * p
            ref[at : at + 16] = before[inner : inner + 16]
            ref[at + 16 : at + 32] = after[inner : inner + 16]
            at, shift = 480 + 8 * (p // 6), 16 * (k - p % 6) % 128
            for h, strip in enumerate((before, after)):
                plane = strip[at : at + 8]
                plane = pltpu.roll(plane, shift, 1) if shift else plane
                outer[h] = jnp.where((lanes >= 16 * k) & (lanes < 16 * k + 16), plane, outer[h])
        edges = [[], []]
        for k, p in enumerate(far):
            at, inner = FAR_AT + 16 * k, 288 + 16 * p
            ref[at : at + 8] = before[24 * p + 16 : 24 * p + 24]
            ref[at + 8 : at + 16] = after[24 * p : 24 * p + 8]
            edges[0].append(before[inner + 8 : inner + 16])
            edges[1].append(after[inner : inner + 8])
        for h in range(2):
            at = PACKED_AT + 8 * h
            ref[at : at + 8] = outer[h]
            ref[at + 16 : at + 24] = pack16(edges[h])


def fine_down_kernel(
    n, s, v, before, after, s_left, s_right, v_left, v_right, y_left, y_right,
    coarse, sent, black_out, red_b_out, black_b_out, red, black, rb, bb, weight, pairs,
):
    gx, gy, gz = (lax.axis_index(a) for a in ("gx", "gy", "gz"))
    inner = domain((ROWS0, 256), 64 * gy - EY, 64 * n[1], 128 * gz, 128 * n[2], 192)
    has_left, has_right = gx > 0, gx < n[0] - 1
    weight[0] = jnp.where(has_left, inner, 0.0)
    weight[1] = inner
    weight[2] = jnp.where(has_right, inner, 0.0)
    clear_pads(black, red)
    block, strip = slice(0, 128), slice(128, 256)
    zero8 = jnp.zeros((8, 128), F32)
    for a, ref in enumerate((black, rb, bb)):
        off, top = (1, PAD) if a == 0 else (0, 0)

        def put(i, lo, lanes, value, there=None, ref=ref, off=off, top=top, a=a):
            if a == 0 and there is not None:
                value = jnp.where(there, value, 0.0)
            ref[i + off, top + lo : top + lo + value.shape[0], lanes] = value

        for p in range(4):
            j, i = 4 * a + p, 4 + p
            put(i, EY, block, s[j])
            put(i, EY, strip, v[j])
            put(p, EY, block, s_left[j], has_left)
            put(8 + p, EY, block, s_right[j], has_right)
            put(i, 0, block, before[24 * j : 24 * j + 24])
            put(i, EY + 64, block, after[24 * j : 24 * j + 24])
            at = 288 + 16 * j
            put(i, 8, strip, before[at : at + 16])
            put(i, EY + 64, strip, after[at : at + 16])
            at = 480 + 8 * (j // 6)
            put(i, 0, strip, unpack16(before[at : at + 8], j % 6))
            put(i, EY + 80, strip, unpack16(after[at : at + 8], j % 6))
        sides = ((0, UP_NEAR, UP_FAR, v_left, y_left, has_left), (8, DOWN_NEAR, DOWN_FAR, v_right, y_right, has_right))
        for base, near, far, strips, y, there in sides:
            for k, p in enumerate(near):
                if p // 4 != a:
                    continue
                i = base + p % 4
                put(i, EY, strip, strips[k], there)
                put(i, 0, block, y[48 * k : 48 * k + 24], there)
                put(i, EY + 64, block, y[48 * k + 24 : 48 * k + 48], there)
                at = STRIP_AT + 32 * k
                put(i, 8, strip, y[at : at + 16], there)
                put(i, EY + 64, strip, y[at + 16 : at + 32], there)
                put(i, 0, strip, unpack16(y[PACKED_AT : PACKED_AT + 8], k), there)
                put(i, EY + 80, strip, unpack16(y[PACKED_AT + 8 : PACKED_AT + 16], k), there)
            for k, p in enumerate(far):
                if p // 4 != a:
                    continue
                i = base + p % 4
                put(i, EY, strip, unpack16(strips[NEAR], k), there)
                at = FAR_AT + 16 * k
                put(i, 16, block, y[at : at + 8], there)
                put(i, EY + 64, block, y[at + 8 : at + 16], there)
                put(i, 16, strip, unpack16(y[PACKED_AT + 16 : PACKED_AT + 24], k), there)
                put(i, EY + 64, strip, unpack16(y[PACKED_AT + 24 : PACKED_AT + 32], k), there)
                for lanes in (block, strip):
                    for lo in (0, 8, EY + 72, EY + 80):
                        put(i, lo, lanes, zero8)

    def weights(i, r, step):
        return weight[i // 4, r : r + step]

    half(red, black, rb, weights, True, range(0, 12), ROWS0, 16)
    half(black, red, bb, weights, False, range(1, 11), ROWS0, 16)
    half(red, black, rb, weights, True, range(1, 11), ROWS0, 16)
    half(black, red, bb, weights, False, range(2, 10), ROWS0, 16)
    even = even_mask((16, 256))
    for p in range(4):
        for r in range(0, ROWS0, 16):
            value = residual_sum(red, black, rb, bb, p + 4, r, 16, even)
            pairs[2 * p, r : r + 16] = value[:, :128]
            pairs[2 * p + 1, r : r + 16] = value[:, 128:]
    rows = []
    for p in range(4):
        parts = [pairs[2 * p + h, pl.ds(0, ROWS1, stride=2), :] + pairs[2 * p + h, pl.ds(1, ROWS1, stride=2), :] for h in (0, 1)]
        rows.append(jnp.concatenate(parts, axis=1))
    result = dot(jnp.concatenate(rows, axis=0), table(256, 128, lambda k, c: (k >> 1) == c, 0.5))
    for p in range(4):
        coarse[p] = result[p * ROWS1 : (p + 1) * ROWS1]
        sent[SENT1 * p : SENT1 * p + SENT1] = coarse[p, SENT1_AT : SENT1_AT + SENT1]
    for p in range(8):
        black_out[p] = black[p + 3, PAD + UP0 : PAD + UP0 + 80]
        red_b_out[p] = rb[p + 2, UP0 : UP0 + 80]
        black_b_out[p] = bb[p + 2, UP0 : UP0 + 80]


def middle_down_kernel(
    n, own, same, other, coarse, black_out, red_b_out, black_b_out, red, black, rb, bb, weight, pairs
):
    gx, gy, gz = (lax.axis_index(a) for a in ("gx", "gy", "gz"))
    count = 2 * n[0]
    core = gx % 2
    even = even_mask((ROWS1, 128))
    even_sent = even_mask((SENT1, 128)) ^ (SENT1_AT % 2 == 1)
    weight[...] = domain((ROWS1, 128), 32 * gy - EY // 2, 32 * n[1], 64 * gz, 64 * n[2], 96)
    clear_pads(red, black)
    zero = jnp.zeros((SENT1_AT, 128), F32)
    for i in range(count):
        block, q = i // 2, 2 * SENT1 * (i % 2)
        mine = core == block % 2
        a, b = (jnp.where(mine, same[block // 2, at : at + SENT1], other[block // 2, at : at + SENT1]) for at in (q, q + SENT1))
        for ref, v in ((rb, jnp.where(even_sent, a, b)), (bb, jnp.where(even_sent, b, a))):
            ref[i, :SENT1_AT] = zero
            ref[i, SENT1_AT : SENT1_AT + SENT1] = v
            ref[i, SENT1_AT + SENT1 :] = zero
    for h in range(2):
        a, b = own[2 * h], own[2 * h + 1]
        rb[2 * gx + h] = jnp.where(even, a, b)
        bb[2 * gx + h] = jnp.where(even, b, a)
    for i in range(count):
        red[i + 1, PAD : PAD + ROWS1] = rb[i] * weight[...]

    def weights(i, r, step):
        return weight[r : r + step]

    every = range(count)
    half(black, red, bb, weights, False, every, ROWS1, ROWS1)
    half(red, black, rb, weights, True, every, ROWS1, ROWS1)
    half(black, red, bb, weights, False, every, ROWS1, ROWS1)
    for i in range(8):
        q = 2 * gx - 3 + i
        inside = jnp.clip(q, 0, count - 1)
        black_out[i] = black[jnp.clip(q + 1, 0, count + 1), PAD : PAD + ROWS1]
        red_b_out[i] = rb[inside]
        black_b_out[i] = bb[inside]
    top = EY // 2 - 4
    even40 = even_mask((40, 128))
    for i in every:
        pairs[i] = residual_sum(red, black, rb, bb, i, top, 40, even40)
    sums = [pairs[i, pl.ds(4, 16, stride=2), :] + pairs[i, pl.ds(5, 16, stride=2), :] for i in every]
    to2 = lambda k: jnp.where(k < 96, (k >> 1) + 16, (k >> 1) - 48)
    low = jnp.concatenate(sums[: n[0]], axis=0)
    high = jnp.concatenate(sums[n[0] :], axis=0)
    take = table(256, 128, lambda k, c: to2(k & 127) + (k & 128) // 2 == c, 0.5)
    result = dot(jnp.concatenate([low, high], axis=1), take)
    for i in range(n[0]):
        coarse[i] = result[16 * i : 16 * i + 16]


def wrap_pairs(ref, rows):
    last = ref.shape[0] - 2
    low = lane_of((rows, 128)) < 64
    ref[0, PAD : PAD + rows] = jnp.where(low, 0.0, pltpu.roll(ref[last, PAD : PAD + rows], 64, 1))
    ref[last + 1, PAD : PAD + rows] = jnp.where(low, pltpu.roll(ref[1, PAD : PAD + rows], 64, 1), 0.0)


def domain2(n, gz, rows):
    y = lane_of((rows, 128))
    z = (y & 63) - 16 + 32 * gz
    return jnp.where((z >= 0) & (z < 32 * n[2]), F32(SIXTH), F32(0.0))


def third_place(n, i):
    packed = n[0] // 2
    arrays = max(1, packed // 2)
    p = i % packed
    return p % arrays, 64 * (i // packed) + 32 * (p // arrays)


def coarse_down_kernel(n, b2, coarse, black_out, rb, bb, red, black, weight, pairs):
    gz = lax.axis_index("gz")
    rows, packed = 16 * n[1], n[0] // 2
    weight[...] = domain2(n, gz, rows)
    clear_pads(red, black)
    even16 = even_mask((16, 128))
    for i in range(packed):
        for g in range(n[1]):
            a, b = b2[g, 2 * i], b2[g, 2 * i + 1]
            at = 16 * g
            r = jnp.where(even16, a, b)
            rb[i, at : at + 16] = r
            bb[i, at : at + 16] = jnp.where(even16, b, a)
            red[i + 1, PAD + at : PAD + at + 16] = r * weight[at : at + 16]

    def weights(i, r, step):
        return weight[r : r + step]

    every = range(packed)
    wrap_pairs(red, rows)
    half(black, red, bb, weights, False, every, rows, rows)
    wrap_pairs(black, rows)
    half(red, black, rb, weights, True, every, rows, rows)
    wrap_pairs(red, rows)
    half(black, red, bb, weights, False, every, rows, rows)
    wrap_pairs(black, rows)
    even = even_mask((rows, 128))
    for i in every:
        pairs[i] = residual_sum(red, black, rb, bb, i, 0, rows, even)
        black_out[i] = black[i + 1, PAD : PAD + rows]
    rows3 = rows // 2
    sums = [pairs[i, pl.ds(0, rows3, stride=2), :] + pairs[i, pl.ds(1, rows3, stride=2), :] for i in every]
    take = table(128, 128, lambda k, c: ((k & 63) >> 1) + (k & 64) == c, 0.5)
    result = dot(jnp.concatenate(sums, axis=0), take)
    arrays = coarse.shape[0]
    for r in range(arrays):
        total = result[r * rows3 : (r + 1) * rows3]
        if packed > arrays:
            total = total + pltpu.roll(result[(r + arrays) * rows3 : (r + arrays + 1) * rows3], 32, 1)
        coarse[r] = total


def up_kernel(
    n, b3, b3_left, b3_right, start2, rb2, bb2, black1, red_b1, black_b1, black0, red_b0, black_b0, out,
    red2, black2, weight2,
    rb3, bb3, red3, black3, weight3, add2,
    add1, red1, bl1, weight1,
    add0, red0, bl0, weight0,
):
    gx, gy, gz = (lax.axis_index(a) for a in ("gx", "gy", "gz"))
    rows2, rows3 = 16 * n[1], 8 * n[1]
    packed, pairs_3 = n[0] // 2, n[0] // 2

    shape3 = (rows3, 128)
    even3 = even_mask(shape3)
    lane3 = lane_of(shape3)
    z3 = lane3 - 24 + 16 * gz
    weight3[...] = jnp.where((z3 >= 0) & (z3 < 16 * n[2]) & (lane3 < 64), F32(SIXTH), F32(0.0))
    clear_pads(red3, black3)

    def plane3(i):
        at, lane = third_place(n, i)
        own, left, right = (pltpu.roll(ref[at], (to - lane) % 128, 1) if (to - lane) % 128 else ref[at] for ref, to in ((b3, 16), (b3_left, 0), (b3_right, 32)))
        return jnp.where(lane3 < 24, left, jnp.where(lane3 < 40, own, right))

    for i in range(pairs_3):
        a, b = plane3(2 * i), plane3(2 * i + 1)
        r = jnp.where(even3, a, b)
        rb3[i] = r
        bb3[i] = jnp.where(even3, b, a)
        red3[i + 1, PAD : PAD + rows3] = r * weight3[...]

    def weights3(i, r, step):
        return weight3[r : r + step]

    every3 = range(pairs_3)
    half(black3, red3, bb3, weights3, False, every3, rows3, rows3)

    def sweep3(_, carry):
        half(red3, black3, rb3, weights3, True, every3, rows3, rows3)
        half(black3, red3, bb3, weights3, False, every3, rows3, rows3)
        return carry

    lax.fori_loop(0, 7, sweep3, 0)
    planes = []
    for i in every3:
        r, b = red3[i + 1, PAD : PAD + rows3], black3[i + 1, PAD : PAD + rows3]
        planes += [jnp.where(even3, r, b), jnp.where(even3, b, r)]

    halves = [jnp.concatenate(planes[:packed], axis=0), jnp.concatenate(planes[packed:], axis=0)]
    spread = table(256, 128, lambda k, c: ((c & 63) >> 1) + 16 + 2 * (c & 64) == k)
    wide = dot(jnp.concatenate(halves, axis=1), spread)
    weight2[...] = domain2(n, gz, rows2)
    clear_pads(red2, black2)
    every2 = range(packed)
    for i in every2:
        w = wide[i * rows3 : (i + 1) * rows3]
        add2[i, pl.ds(0, rows3, stride=2), :] = w
        add2[i, pl.ds(1, rows3, stride=2), :] = w
        black2[i + 1, PAD : PAD + rows2] = start2[i] + add2[i]

    def weights2(i, r, step):
        return weight2[r : r + step]

    for _ in range(2):
        wrap_pairs(black2, rows2)
        half(red2, black2, rb2, weights2, True, every2, rows2, rows2)
        wrap_pairs(red2, rows2)
        half(black2, red2, bb2, weights2, False, every2, rows2, rows2)

    even32 = even_mask((32, 128))
    top = pl.multiple_of(16 * gy, 8)
    planes = []
    second = lane_of((32, 128)) >= 64
    for i in range(8):
        q = gx - 2 + (i + 1) // 2
        there = (q >= 0) & (q < n[0])
        upper = q >= packed
        at = jnp.clip(jnp.where(upper, q - packed, q), 0, packed - 1) + 1
        r, b = red2[at, pl.ds(top, 32), :], black2[at, pl.ds(top, 32), :]
        plane = jnp.where(even32, r, b) if i % 2 == 1 else jnp.where(even32, b, r)
        planes.append(jnp.where(there & (second == upper), plane, 0.0))
    to2 = lambda k, c: jnp.where(c < 96, (c >> 1) + 16, (c >> 1) - 48) == (k & 63)
    wide = dot(jnp.concatenate(planes, axis=0), table(128, 128, to2))
    inner = domain((ROWS1, 128), 32 * gy - EY // 2, 32 * n[1], 64 * gz, 64 * n[2], 96)
    clear_pads(red1, bl1)
    skip = PAD - EY // 4
    for i in range(8):
        q = 2 * gx - 3 + i
        weight1[i] = jnp.where((q >= 0) & (q < 2 * n[0]), inner, 0.0)
        w = wide[32 * i + skip : 32 * i + skip + ROWS1 // 2]
        add1[i, pl.ds(0, ROWS1 // 2, stride=2), :] = w
        add1[i, pl.ds(1, ROWS1 // 2, stride=2), :] = w
        bl1[i + 1, PAD : PAD + ROWS1] = black1[i] + add1[i]

    def weights1(i, r, step):
        return weight1[i, r : r + step]

    half(red1, bl1, red_b1, weights1, True, range(0, 8), ROWS1, ROWS1)
    half(bl1, red1, black_b1, weights1, False, range(1, 7), ROWS1, ROWS1)
    half(red1, bl1, red_b1, weights1, True, range(1, 7), ROWS1, ROWS1)
    half(bl1, red1, black_b1, weights1, False, range(2, 6), ROWS1, ROWS1)

    low1 = PAD + UP0 // 2
    even40 = even_mask((40, 128))
    planes = []
    for i in range(8):
        r, b = red1[3 + i // 2, low1 : low1 + 40], bl1[3 + i // 2, low1 : low1 + 40]
        planes.append(jnp.where(even40, r, b) if i % 2 == 0 else jnp.where(even40, b, r))
    wide = dot(jnp.concatenate(planes, axis=0), table(128, 256, lambda k, c: (c >> 1) == k))
    inner = domain((80, 256), 64 * gy - 8, 64 * n[1], 128 * gz, 128 * n[2], 192)
    weight0[0] = jnp.where(gx > 0, inner, 0.0)
    weight0[1] = inner
    weight0[2] = jnp.where(gx < n[0] - 1, inner, 0.0)
    clear_pads(red0, bl0)
    for i in range(8):
        for h in (0, 1):
            w = wide[40 * i : 40 * i + 40, 128 * h : 128 * h + 128]
            add0[2 * i + h, pl.ds(0, 40, stride=2), :] = w
            add0[2 * i + h, pl.ds(1, 40, stride=2), :] = w
            bl0[i + 1, PAD : PAD + 80, 128 * h : 128 * h + 128] = black0[i, :, 128 * h : 128 * h + 128] + add0[2 * i + h]

    def weights0(i, r, step):
        return weight0[(i + 2) // 4, r : r + step]

    half(red0, bl0, red_b0, weights0, True, range(0, 8), 80, 16)
    half(bl0, red0, black_b0, weights0, False, range(1, 7), 80, 16)
    half(red0, bl0, red_b0, weights0, True, range(1, 7), 80, 16)
    half(bl0, red0, black_b0, weights0, False, range(2, 6), 80, 16)
    even64 = even_mask((64, 128))
    for p in range(4):
        r = red0[p + 3, PAD + 8 : PAD + 72, :128]
        b = bl0[p + 3, PAD + 8 : PAD + 72, :128]
        out[2 * p] = jnp.where(even64, r, b)
        out[2 * p + 1] = jnp.where(even64, b, r)


def from_both(up_value, down_value, axis):
    size = lax.axis_size(axis)
    up = [(i, i + 1) for i in range(size - 1)]
    return lax.ppermute(up_value, axis, up), lax.ppermute(down_value, axis, [(b, a) for a, b in up])


def from_both_round(up_value, down_value, axis):
    size = lax.axis_size(axis)
    up = [(i, (i + 1) % size) for i in range(size)]
    return lax.ppermute(up_value, axis, up), lax.ppermute(down_value, axis, [(b, a) for a, b in up])


def gathered(value, axis, groups=None):
    size = lax.axis_size(axis) if groups is None else len(groups[0])
    copies = jnp.broadcast_to(value, (size, *value.shape))
    return lax.all_to_all(copies, axis, split_axis=0, concat_axis=0, axis_index_groups=groups, tiled=True)


def local(right_side, start):
    n = tuple(lax.axis_size(a) for a in ("gx", "gy", "gz"))
    s, up, down = call(
        pack_kernel,
        [(12, 64, 128), (6, 64, 128), (6, 64, 128)],
        [(8, 64, 128), (8, 64, 128), pltpu.SemaphoreType.DMA, pltpu.SemaphoreType.DMA],
        [pl.BlockSpec(memory_space=pltpu.HBM)] * 2,
    )(start, right_side)
    up, down = from_both(up, down, "gz")
    s_left, s_right = from_both_round(s, s, "gx")
    v, v_up, v_down, first, last = call(
        widen_kernel, [(12, 64, 128), (NEAR + 1, 64, 128), (NEAR + 1, 64, 128), (CROSS_Y, 128), (CROSS_Y, 128)]
    )(s, up, down)
    v_left, v_right = from_both_round(v_up, v_down, "gx")
    before, after = from_both(last, first, "gy")
    up, down = call(strips_kernel, [(CROSS_X, 128)] * 2)(before, after, s_left, s_right, v_left, v_right)
    y_left, y_right = from_both_round(up, down, "gx")
    up0 = (8, 80, 256)
    b1, sent, black0, red_b0, black_b0 = call(
        functools.partial(fine_down_kernel, n),
        [(4, ROWS1, 128), (4 * SENT1, 128), up0, up0, up0],
        [(14, ROWS0 + 2 * PAD, 256)] * 2 + [(12, ROWS0, 256)] * 2 + [(3, ROWS0, 256), (8, ROWS0, 128)],
    )(s, v, before, after, s_left, s_right, v_left, v_right, y_left, y_right)
    groups = [[2 * chip + core for chip in range(n[0] // 2)] for core in range(2)]
    same = gathered(sent[None], "gx", groups)
    other = lax.ppermute(same, "gx", [(i, i ^ 1) for i in range(n[0])])
    all1 = (2 * n[0], ROWS1, 128)
    colour1 = (2 * n[0] + 2, ROWS1 + 2 * PAD, 128)
    window1 = (8, ROWS1, 128)
    blocks = (n[0] // 2, 4 * SENT1, 128)
    b2, black1, red_b1, black_b1 = call(
        functools.partial(middle_down_kernel, n),
        [(n[0], 16, 128), window1, window1, window1],
        [colour1, colour1, all1, all1, (ROWS1, 128), (2 * n[0], 40, 128)],
    )(b1, same.reshape(blocks), other.reshape(blocks))
    b2 = gathered(b2, "gy").reshape(n[1], n[0], 16, 128)
    rows2, rows3 = 16 * n[1], 8 * n[1]
    packed = n[0] // 2
    all2, colour2, colour3 = (packed, rows2, 128), (packed + 2, rows2 + 2 * PAD, 128), (packed + 2, rows3 + 2 * PAD, 128)
    b3, black2, red_b2, black_b2 = call(
        functools.partial(coarse_down_kernel, n),
        [(max(1, packed // 2), rows3, 128), all2, all2, all2],
        [colour2, colour2, (rows2, 128), all2],
    )(b2)
    left, right = from_both(b3, b3, "gz")
    (out,) = call(
        functools.partial(up_kernel, n),
        [(8, 64, 128)],
        [
            colour2, colour2, (rows2, 128),
            (packed, rows3, 128), (packed, rows3, 128), colour3, colour3, (rows3, 128), all2,
            window1, (10, ROWS1 + 2 * PAD, 128), (10, ROWS1 + 2 * PAD, 128), window1,
            (16, 80, 128), (10, 80 + 2 * PAD, 256), (10, 80 + 2 * PAD, 256), (3, 80, 256),
        ],
    )(b3, left, right, black2, red_b2, black_b2, black1, red_b1, black_b1, black0, red_b0, black_b0)
    return out


def solution(mesh):
    in_specs = (P("gx", "gy", "gz"), P("gx", "gy", "gz"))
    out_specs = P("gx", "gy", "gz")
    return jax.shard_map(local, mesh=mesh, in_specs=in_specs, out_specs=out_specs, check_vma=False)
```

```python
import functools

import jax
import jax.numpy as jnp
from jax import lax
from jax.experimental import pallas as pl
from jax.experimental.pallas import tpu as pltpu
from jax.sharding import PartitionSpec as P

F32 = jnp.float32
BF16 = jnp.bfloat16
SIXTH = 1.0 / 6.0
EY = 24
ROWS0 = 64 + 2 * EY
ROWS1 = ROWS0 // 2
SENT1 = 50
SENT1_AT = 3
PAD = 8
UP0 = EY - 8
VMEM_LIMIT = 40 * 1024 * 1024


def call(kernel, outs, scratch=(), in_specs=None):
    shapes = [jax.ShapeDtypeStruct(s, F32) for s in outs]
    extra = {} if in_specs is None else {"in_specs": in_specs}
    return pl.pallas_call(
        kernel,
        out_shape=shapes,
        scratch_shapes=[pltpu.VMEM(s, F32) if isinstance(s, tuple) else s for s in scratch],
        compiler_params=pltpu.CompilerParams(vmem_limit_bytes=VMEM_LIMIT),
        **extra,
    )


def even_mask(shape):
    rows = lax.broadcasted_iota(jnp.int32, shape, 0)
    lanes = lax.broadcasted_iota(jnp.int32, shape, 1)
    return ((rows + lanes) & 1) == 0


def lane_of(shape):
    return lax.broadcasted_iota(jnp.int32, shape, 1)


def domain(shape, row0, rows, lane0, lanes, cut, unused=None):
    y = lax.broadcasted_iota(jnp.int32, shape, 0) + row0
    k = lane_of(shape)
    z = jnp.where(k < cut, k, k - shape[1]) + lane0
    inside = (y >= 0) & (y < rows) & (z >= 0) & (z < lanes)
    if unused is not None:
        inside = inside & ((k < unused[0]) | (k >= unused[1]))
    return jnp.where(inside, F32(SIXTH), F32(0.0))


def beside(src, i, r, rows, even, red):
    at = PAD + r
    c = src[i + 1, at : at + rows]
    below, above = src[i, at : at + rows], src[i + 2, at : at + rows]
    s = c + (jnp.where(even, below, above) if red else jnp.where(even, above, below))
    s = s + (src[i + 1, at - 1 : at - 1 + rows] + src[i + 1, at + 1 : at + 1 + rows])
    return s + (pltpu.roll(c, 1, 1) + pltpu.roll(c, c.shape[1] - 1, 1))


def half(dst, src, b, weight, red, pairs, rows, step):
    even = even_mask((step, dst.shape[2]))
    for i in pairs:
        for r in range(0, rows, step):
            value = (b[i, r : r + step] + beside(src, i, r, step, even, red)) * weight(i, r, step)
            dst[i + 1, PAD + r : PAD + r + step] = value


def residual_sum(red, black, red_b, black_b, i, r, step, even):
    at = PAD + r
    x = red_b[i, r : r + step] - 6.0 * red[i + 1, at : at + step] + beside(black, i, r, step, even, True)
    y = black_b[i, r : r + step] - 6.0 * black[i + 1, at : at + step] + beside(red, i, r, step, even, False)
    return x + y


def clear_pads(*colours):
    for ref in colours:
        pairs, rows, lanes = ref.shape
        for i in (0, pairs - 1):
            ref[i] = jnp.zeros((rows, lanes), F32)
        for i in range(1, pairs - 1):
            ref[i, :PAD] = jnp.zeros((PAD, lanes), F32)
            ref[i, rows - PAD :] = jnp.zeros((PAD, lanes), F32)


def table(rows, cols, of, value=1.0):
    k = lax.broadcasted_iota(jnp.int32, (rows, cols), 0)
    c = lax.broadcasted_iota(jnp.int32, (rows, cols), 1)
    return jnp.where(of(k, c), F32(value), F32(0.0)).astype(BF16)


def dot(a, m):
    high = a.astype(BF16)
    rest = a - high.astype(F32)
    middle = rest.astype(BF16)
    low = (rest - middle.astype(F32)).astype(BF16)
    parts = jnp.concatenate([high, middle, low], axis=1)
    return jnp.dot(parts, jnp.concatenate([m, m, m], axis=0), preferred_element_type=F32)


def pack_kernel(start_hbm, right_hbm, s, up, down, start, right, sem_a, sem_b):
    copy_a = pltpu.make_async_copy(start_hbm, start, sem_a)
    copy_b = pltpu.make_async_copy(right_hbm, right, sem_b)
    copy_a.start()
    copy_b.start()
    even = even_mask((64, 128))
    low = lane_of((64, 128)) < 64
    copy_a.wait()
    copy_b.wait()
    for p in range(4):
        s[p] = jnp.where(even, start[2 * p + 1], start[2 * p])
        s[p + 4] = jnp.where(even, right[2 * p], right[2 * p + 1])
        s[p + 8] = jnp.where(even, right[2 * p + 1], right[2 * p])
    for p in range(6):
        a, b = s[p], pltpu.roll(s[p + 6], 64, 1)
        up[p] = jnp.where(low, b, a)
        down[p] = jnp.where(low, a, b)


def pack16(planes, first=0):
    lanes = lane_of(planes[0].shape)
    total = jnp.zeros(planes[0].shape, F32)
    for k, plane in enumerate(planes):
        at = 16 * (k + first)
        total = jnp.where((lanes >= at) & (lanes < at + 16), pltpu.roll(plane, (8 + at) % 128, 1), total)
    return total


def unpack16(packed, k):
    lanes = lane_of(packed.shape)
    shift = (-8 - 16 * k) % 128
    plane = pltpu.roll(packed, shift, 1) if shift else packed
    return jnp.where((lanes < 8) | (lanes >= 120), plane, 0.0)


UP_NEAR, UP_FAR = (1, 2, 3, 6, 7, 10, 11), (0, 4, 5, 8, 9)
DOWN_NEAR, DOWN_FAR = (0, 1, 2, 4, 5, 8, 9), (3, 6, 7, 10, 11)
NEAR, FAR = len(UP_NEAR), len(UP_FAR)
CROSS_Y = 12 * 24 + 12 * 16 + 2 * 8
STRIP_AT = 48 * NEAR
FAR_AT = STRIP_AT + 32 * NEAR
PACKED_AT = FAR_AT + 16 * FAR
WHOLE_AT = PACKED_AT + 2 * 16
CROSS_X = WHOLE_AT + 64 * (NEAR + 1)


def widen_kernel(s, up, down, v, first, last):
    low = lane_of((64, 128)) < 64
    for p in range(6):
        v[p] = jnp.where(low, down[p], up[p])
        v[p + 6] = pltpu.roll(jnp.where(low, up[p], down[p]), 64, 1)
    for p in range(12):
        first[24 * p : 24 * p + 24] = s[p, :24]
        last[24 * p : 24 * p + 24] = s[p, 40:]
        at = 288 + 16 * p
        first[at : at + 16] = v[p, :16]
        last[at : at + 16] = v[p, 48:]
    for t in range(2):
        at = 480 + 8 * t
        first[at : at + 8] = pack16([v[6 * t + k, 16:24] for k in range(6)])
        last[at : at + 8] = pack16([v[6 * t + k, 40:48] for k in range(6)])


def strips_kernel(v, before, after, *rest):
    lanes = lane_of((8, 128))
    for ref, near, far in ((rest[-2], UP_NEAR, UP_FAR), (rest[-1], DOWN_NEAR, DOWN_FAR)):
        outer = [jnp.zeros((8, 128), F32), jnp.zeros((8, 128), F32)]
        for k, p in enumerate(near):
            ref[WHOLE_AT + 64 * k : WHOLE_AT + 64 * k + 64] = v[p]
            ref[48 * k : 48 * k + 24] = before[24 * p : 24 * p + 24]
            ref[48 * k + 24 : 48 * k + 48] = after[24 * p : 24 * p + 24]
            at, inner = STRIP_AT + 32 * k, 288 + 16 * p
            ref[at : at + 16] = before[inner : inner + 16]
            ref[at + 16 : at + 32] = after[inner : inner + 16]
            at, shift = 480 + 8 * (p // 6), 16 * (k - p % 6) % 128
            for h, strip in enumerate((before, after)):
                plane = strip[at : at + 8]
                plane = pltpu.roll(plane, shift, 1) if shift else plane
                outer[h] = jnp.where((lanes >= 16 * k) & (lanes < 16 * k + 16), plane, outer[h])
        ref[WHOLE_AT + 64 * NEAR :] = pack16([v[p] for p in far])
        edges = [[], []]
        for k, p in enumerate(far):
            at, inner = FAR_AT + 16 * k, 288 + 16 * p
            ref[at : at + 8] = before[24 * p + 16 : 24 * p + 24]
            ref[at + 8 : at + 16] = after[24 * p : 24 * p + 8]
            edges[0].append(before[inner + 8 : inner + 16])
            edges[1].append(after[inner : inner + 8])
        for h in range(2):
            at = PACKED_AT + 8 * h
            ref[at : at + 8] = outer[h]
            ref[at + 16 : at + 24] = pack16(edges[h])


def fine_down_kernel(
    n, s, v, before, after, s_left, s_right, y_left, y_right,
    coarse, sent, black_out, red_b_out, black_b_out, red, black, rb, bb, weight, pairs,
):
    gx, gy, gz = (lax.axis_index(a) for a in ("gx", "gy", "gz"))
    inner = domain((ROWS0, 256), 64 * gy - EY, 64 * n[1], 128 * gz, 128 * n[2], 192)
    has_left, has_right = gx > 0, gx < n[0] - 1
    weight[0] = jnp.where(has_left, inner, 0.0)
    weight[1] = inner
    weight[2] = jnp.where(has_right, inner, 0.0)
    clear_pads(black, red)
    block, strip = slice(0, 128), slice(128, 256)
    zero8 = jnp.zeros((8, 128), F32)
    for a, ref in enumerate((black, rb, bb)):
        off, top = (1, PAD) if a == 0 else (0, 0)

        def put(i, lo, lanes, value, there=None, ref=ref, off=off, top=top, a=a):
            if a == 0 and there is not None:
                value = jnp.where(there, value, 0.0)
            ref[i + off, top + lo : top + lo + value.shape[0], lanes] = value

        for p in range(4):
            j, i = 4 * a + p, 4 + p
            put(i, EY, block, s[j])
            put(i, EY, strip, v[j])
            put(p, EY, block, s_left[j], has_left)
            put(8 + p, EY, block, s_right[j], has_right)
            put(i, 0, block, before[24 * j : 24 * j + 24])
            put(i, EY + 64, block, after[24 * j : 24 * j + 24])
            at = 288 + 16 * j
            put(i, 8, strip, before[at : at + 16])
            put(i, EY + 64, strip, after[at : at + 16])
            at = 480 + 8 * (j // 6)
            put(i, 0, strip, unpack16(before[at : at + 8], j % 6))
            put(i, EY + 80, strip, unpack16(after[at : at + 8], j % 6))
        sides = ((0, UP_NEAR, UP_FAR, y_left, has_left), (8, DOWN_NEAR, DOWN_FAR, y_right, has_right))
        for base, near, far, y, there in sides:
            for k, p in enumerate(near):
                if p // 4 != a:
                    continue
                i = base + p % 4
                put(i, EY, strip, y[WHOLE_AT + 64 * k : WHOLE_AT + 64 * k + 64], there)
                put(i, 0, block, y[48 * k : 48 * k + 24], there)
                put(i, EY + 64, block, y[48 * k + 24 : 48 * k + 48], there)
                at = STRIP_AT + 32 * k
                put(i, 8, strip, y[at : at + 16], there)
                put(i, EY + 64, strip, y[at + 16 : at + 32], there)
                put(i, 0, strip, unpack16(y[PACKED_AT : PACKED_AT + 8], k), there)
                put(i, EY + 80, strip, unpack16(y[PACKED_AT + 8 : PACKED_AT + 16], k), there)
            for k, p in enumerate(far):
                if p // 4 != a:
                    continue
                i = base + p % 4
                put(i, EY, strip, unpack16(y[WHOLE_AT + 64 * NEAR :], k), there)
                at = FAR_AT + 16 * k
                put(i, 16, block, y[at : at + 8], there)
                put(i, EY + 64, block, y[at + 8 : at + 16], there)
                put(i, 16, strip, unpack16(y[PACKED_AT + 16 : PACKED_AT + 24], k), there)
                put(i, EY + 64, strip, unpack16(y[PACKED_AT + 24 : PACKED_AT + 32], k), there)
                for lanes in (block, strip):
                    for lo in (0, 8, EY + 72, EY + 80):
                        put(i, lo, lanes, zero8)

    def weights(i, r, step):
        return weight[i // 4, r : r + step]

    half(red, black, rb, weights, True, range(0, 12), ROWS0, 16)
    half(black, red, bb, weights, False, range(1, 11), ROWS0, 16)
    half(red, black, rb, weights, True, range(1, 11), ROWS0, 16)
    half(black, red, bb, weights, False, range(2, 10), ROWS0, 16)
    even = even_mask((16, 256))
    for p in range(4):
        for r in range(0, ROWS0, 16):
            value = residual_sum(red, black, rb, bb, p + 4, r, 16, even)
            pairs[2 * p, r : r + 16] = value[:, :128]
            pairs[2 * p + 1, r : r + 16] = value[:, 128:]
    rows = []
    for p in range(4):
        parts = [pairs[2 * p + h, pl.ds(0, ROWS1, stride=2), :] + pairs[2 * p + h, pl.ds(1, ROWS1, stride=2), :] for h in (0, 1)]
        rows.append(jnp.concatenate(parts, axis=1))
    result = dot(jnp.concatenate(rows, axis=0), table(256, 128, lambda k, c: (k >> 1) == c, 0.5))
    for p in range(4):
        coarse[p] = result[p * ROWS1 : (p + 1) * ROWS1]
        sent[SENT1 * p : SENT1 * p + SENT1] = coarse[p, SENT1_AT : SENT1_AT + SENT1]
    for p in range(8):
        black_out[p] = black[p + 3, PAD + UP0 : PAD + UP0 + 80]
        red_b_out[p] = rb[p + 2, UP0 : UP0 + 80]
        black_b_out[p] = bb[p + 2, UP0 : UP0 + 80]


def middle_down_kernel(
    n, own, same, other, coarse, black_out, red_b_out, black_b_out, red, black, rb, bb, weight, pairs
):
    gx, gy, gz = (lax.axis_index(a) for a in ("gx", "gy", "gz"))
    count = 2 * n[0]
    core = gx % 2
    even = even_mask((ROWS1, 128))
    even_sent = even_mask((SENT1, 128)) ^ (SENT1_AT % 2 == 1)
    weight[...] = domain((ROWS1, 128), 32 * gy - EY // 2, 32 * n[1], 64 * gz, 64 * n[2], 96)
    clear_pads(red, black)
    zero = jnp.zeros((SENT1_AT, 128), F32)
    for i in range(count):
        block, q = i // 2, 2 * SENT1 * (i % 2)
        mine = core == block % 2
        a, b = (jnp.where(mine, same[block // 2, at : at + SENT1], other[block // 2, at : at + SENT1]) for at in (q, q + SENT1))
        for ref, v in ((rb, jnp.where(even_sent, a, b)), (bb, jnp.where(even_sent, b, a))):
            ref[i, :SENT1_AT] = zero
            ref[i, SENT1_AT : SENT1_AT + SENT1] = v
            ref[i, SENT1_AT + SENT1 :] = zero
    for h in range(2):
        a, b = own[2 * h], own[2 * h + 1]
        rb[2 * gx + h] = jnp.where(even, a, b)
        bb[2 * gx + h] = jnp.where(even, b, a)
    for i in range(count):
        red[i + 1, PAD : PAD + ROWS1] = rb[i] * weight[...]

    def weights(i, r, step):
        return weight[r : r + step]

    every = range(count)
    half(black, red, bb, weights, False, every, ROWS1, ROWS1)
    half(red, black, rb, weights, True, every, ROWS1, ROWS1)
    half(black, red, bb, weights, False, every, ROWS1, ROWS1)
    for i in range(8):
        q = 2 * gx - 3 + i
        inside = jnp.clip(q, 0, count - 1)
        black_out[i] = black[jnp.clip(q + 1, 0, count + 1), PAD : PAD + ROWS1]
        red_b_out[i] = rb[inside]
        black_b_out[i] = bb[inside]
    top = EY // 2 - 4
    even40 = even_mask((40, 128))
    for i in every:
        pairs[i] = residual_sum(red, black, rb, bb, i, top, 40, even40)
    sums = [pairs[i, pl.ds(4, 16, stride=2), :] + pairs[i, pl.ds(5, 16, stride=2), :] for i in every]
    to2 = lambda k: jnp.where(k < 96, (k >> 1) + 16, (k >> 1) - 48)
    low = jnp.concatenate(sums[: n[0]], axis=0)
    high = jnp.concatenate(sums[n[0] :], axis=0)
    take = table(256, 128, lambda k, c: to2(k & 127) + (k & 128) // 2 == c, 0.5)
    result = dot(jnp.concatenate([low, high], axis=1), take)
    for i in range(n[0]):
        coarse[i] = result[16 * i : 16 * i + 16]


def wrap_pairs(ref, rows):
    last = ref.shape[0] - 2
    low = lane_of((rows, 128)) < 64
    ref[0, PAD : PAD + rows] = jnp.where(low, 0.0, pltpu.roll(ref[last, PAD : PAD + rows], 64, 1))
    ref[last + 1, PAD : PAD + rows] = jnp.where(low, pltpu.roll(ref[1, PAD : PAD + rows], 64, 1), 0.0)


def domain2(n, gz, rows):
    y = lane_of((rows, 128))
    z = (y & 63) - 16 + 32 * gz
    return jnp.where((z >= 0) & (z < 32 * n[2]), F32(SIXTH), F32(0.0))


def third_place(n, i):
    packed = n[0] // 2
    arrays = max(1, packed // 2)
    p = i % packed
    return p % arrays, 64 * (i // packed) + 32 * (p // arrays)


def coarse_down_kernel(n, b2, coarse, black_out, rb, bb, red, black, weight, pairs):
    gz = lax.axis_index("gz")
    rows, packed = 16 * n[1], n[0] // 2
    weight[...] = domain2(n, gz, rows)
    clear_pads(red, black)
    even16 = even_mask((16, 128))
    for i in range(packed):
        for g in range(n[1]):
            a, b = b2[g, 2 * i], b2[g, 2 * i + 1]
            at = 16 * g
            r = jnp.where(even16, a, b)
            rb[i, at : at + 16] = r
            bb[i, at : at + 16] = jnp.where(even16, b, a)
            red[i + 1, PAD + at : PAD + at + 16] = r * weight[at : at + 16]

    def weights(i, r, step):
        return weight[r : r + step]

    every = range(packed)
    wrap_pairs(red, rows)
    half(black, red, bb, weights, False, every, rows, rows)
    wrap_pairs(black, rows)
    half(red, black, rb, weights, True, every, rows, rows)
    wrap_pairs(red, rows)
    half(black, red, bb, weights, False, every, rows, rows)
    wrap_pairs(black, rows)
    even = even_mask((rows, 128))
    for i in every:
        pairs[i] = residual_sum(red, black, rb, bb, i, 0, rows, even)
        black_out[i] = black[i + 1, PAD : PAD + rows]
    rows3 = rows // 2
    sums = [pairs[i, pl.ds(0, rows3, stride=2), :] + pairs[i, pl.ds(1, rows3, stride=2), :] for i in every]
    take = table(128, 128, lambda k, c: ((k & 63) >> 1) + (k & 64) == c, 0.5)
    result = dot(jnp.concatenate(sums, axis=0), take)
    arrays = coarse.shape[0]
    for r in range(arrays):
        total = result[r * rows3 : (r + 1) * rows3]
        if packed > arrays:
            total = total + pltpu.roll(result[(r + arrays) * rows3 : (r + arrays + 1) * rows3], 32, 1)
        coarse[r] = total


def up_kernel(
    n, b3, b3_left, b3_right, start2, rb2, bb2, black1, red_b1, black_b1, black0, red_b0, black_b0, out,
    red2, black2, weight2,
    rb3, bb3, red3, black3, weight3, add2,
    add1, red1, bl1, weight1,
    add0, red0, bl0, weight0,
):
    gx, gy, gz = (lax.axis_index(a) for a in ("gx", "gy", "gz"))
    rows2, rows3 = 16 * n[1], 8 * n[1]
    packed, pairs_3 = n[0] // 2, n[0] // 2

    shape3 = (rows3, 128)
    even3 = even_mask(shape3)
    lane3 = lane_of(shape3)
    z3 = lane3 - 24 + 16 * gz
    weight3[...] = jnp.where((z3 >= 0) & (z3 < 16 * n[2]) & (lane3 < 64), F32(SIXTH), F32(0.0))
    clear_pads(red3, black3)

    def plane3(i):
        at, lane = third_place(n, i)
        own, left, right = (pltpu.roll(ref[at], (to - lane) % 128, 1) if (to - lane) % 128 else ref[at] for ref, to in ((b3, 16), (b3_left, 0), (b3_right, 32)))
        return jnp.where(lane3 < 24, left, jnp.where(lane3 < 40, own, right))

    for i in range(pairs_3):
        a, b = plane3(2 * i), plane3(2 * i + 1)
        r = jnp.where(even3, a, b)
        rb3[i] = r
        bb3[i] = jnp.where(even3, b, a)
        red3[i + 1, PAD : PAD + rows3] = r * weight3[...]

    def weights3(i, r, step):
        return weight3[r : r + step]

    every3 = range(pairs_3)
    half(black3, red3, bb3, weights3, False, every3, rows3, rows3)

    def sweep3(_, carry):
        half(red3, black3, rb3, weights3, True, every3, rows3, rows3)
        half(black3, red3, bb3, weights3, False, every3, rows3, rows3)
        return carry

    lax.fori_loop(0, 7, sweep3, 0)
    planes = []
    for i in every3:
        r, b = red3[i + 1, PAD : PAD + rows3], black3[i + 1, PAD : PAD + rows3]
        planes += [jnp.where(even3, r, b), jnp.where(even3, b, r)]

    halves = [jnp.concatenate(planes[:packed], axis=0), jnp.concatenate(planes[packed:], axis=0)]
    spread = table(256, 128, lambda k, c: ((c & 63) >> 1) + 16 + 2 * (c & 64) == k)
    wide = dot(jnp.concatenate(halves, axis=1), spread)
    weight2[...] = domain2(n, gz, rows2)
    clear_pads(red2, black2)
    every2 = range(packed)
    for i in every2:
        w = wide[i * rows3 : (i + 1) * rows3]
        add2[i, pl.ds(0, rows3, stride=2), :] = w
        add2[i, pl.ds(1, rows3, stride=2), :] = w
        black2[i + 1, PAD : PAD + rows2] = start2[i] + add2[i]

    def weights2(i, r, step):
        return weight2[r : r + step]

    for _ in range(2):
        wrap_pairs(black2, rows2)
        half(red2, black2, rb2, weights2, True, every2, rows2, rows2)
        wrap_pairs(red2, rows2)
        half(black2, red2, bb2, weights2, False, every2, rows2, rows2)

    even32 = even_mask((32, 128))
    top = pl.multiple_of(16 * gy, 8)
    planes = []
    second = lane_of((32, 128)) >= 64
    for i in range(8):
        q = gx - 2 + (i + 1) // 2
        there = (q >= 0) & (q < n[0])
        upper = q >= packed
        at = jnp.clip(jnp.where(upper, q - packed, q), 0, packed - 1) + 1
        r, b = red2[at, pl.ds(top, 32), :], black2[at, pl.ds(top, 32), :]
        plane = jnp.where(even32, r, b) if i % 2 == 1 else jnp.where(even32, b, r)
        planes.append(jnp.where(there & (second == upper), plane, 0.0))
    to2 = lambda k, c: jnp.where(c < 96, (c >> 1) + 16, (c >> 1) - 48) == (k & 63)
    wide = dot(jnp.concatenate(planes, axis=0), table(128, 128, to2))
    inner = domain((ROWS1, 128), 32 * gy - EY // 2, 32 * n[1], 64 * gz, 64 * n[2], 96)
    clear_pads(red1, bl1)
    skip = PAD - EY // 4
    for i in range(8):
        q = 2 * gx - 3 + i
        weight1[i] = jnp.where((q >= 0) & (q < 2 * n[0]), inner, 0.0)
        w = wide[32 * i + skip : 32 * i + skip + ROWS1 // 2]
        add1[i, pl.ds(0, ROWS1 // 2, stride=2), :] = w
        add1[i, pl.ds(1, ROWS1 // 2, stride=2), :] = w
        bl1[i + 1, PAD : PAD + ROWS1] = black1[i] + add1[i]

    def weights1(i, r, step):
        return weight1[i, r : r + step]

    half(red1, bl1, red_b1, weights1, True, range(0, 8), ROWS1, ROWS1)
    half(bl1, red1, black_b1, weights1, False, range(1, 7), ROWS1, ROWS1)
    half(red1, bl1, red_b1, weights1, True, range(1, 7), ROWS1, ROWS1)
    half(bl1, red1, black_b1, weights1, False, range(2, 6), ROWS1, ROWS1)

    low1 = PAD + UP0 // 2
    even40 = even_mask((40, 128))
    planes = []
    for i in range(8):
        r, b = red1[3 + i // 2, low1 : low1 + 40], bl1[3 + i // 2, low1 : low1 + 40]
        planes.append(jnp.where(even40, r, b) if i % 2 == 0 else jnp.where(even40, b, r))
    wide = dot(jnp.concatenate(planes, axis=0), table(128, 256, lambda k, c: (c >> 1) == k))
    inner = domain((80, 256), 64 * gy - 8, 64 * n[1], 128 * gz, 128 * n[2], 192)
    weight0[0] = jnp.where(gx > 0, inner, 0.0)
    weight0[1] = inner
    weight0[2] = jnp.where(gx < n[0] - 1, inner, 0.0)
    clear_pads(red0, bl0)
    for i in range(8):
        for h in (0, 1):
            w = wide[40 * i : 40 * i + 40, 128 * h : 128 * h + 128]
            add0[2 * i + h, pl.ds(0, 40, stride=2), :] = w
            add0[2 * i + h, pl.ds(1, 40, stride=2), :] = w
            bl0[i + 1, PAD : PAD + 80, 128 * h : 128 * h + 128] = black0[i, :, 128 * h : 128 * h + 128] + add0[2 * i + h]

    def weights0(i, r, step):
        return weight0[(i + 2) // 4, r : r + step]

    half(red0, bl0, red_b0, weights0, True, range(0, 8), 80, 16)
    half(bl0, red0, black_b0, weights0, False, range(1, 7), 80, 16)
    half(red0, bl0, red_b0, weights0, True, range(1, 7), 80, 16)
    half(bl0, red0, black_b0, weights0, False, range(2, 6), 80, 16)
    even64 = even_mask((64, 128))
    for p in range(4):
        r = red0[p + 3, PAD + 8 : PAD + 72, :128]
        b = bl0[p + 3, PAD + 8 : PAD + 72, :128]
        out[2 * p] = jnp.where(even64, r, b)
        out[2 * p + 1] = jnp.where(even64, b, r)


def from_both(up_value, down_value, axis):
    size = lax.axis_size(axis)
    up = [(i, i + 1) for i in range(size - 1)]
    return lax.ppermute(up_value, axis, up), lax.ppermute(down_value, axis, [(b, a) for a, b in up])


def from_both_round(up_value, down_value, axis):
    size = lax.axis_size(axis)
    up = [(i, (i + 1) % size) for i in range(size)]
    return lax.ppermute(up_value, axis, up), lax.ppermute(down_value, axis, [(b, a) for a, b in up])


def gathered(value, axis, groups=None):
    size = lax.axis_size(axis) if groups is None else len(groups[0])
    copies = jnp.broadcast_to(value, (size, *value.shape))
    return lax.all_to_all(copies, axis, split_axis=0, concat_axis=0, axis_index_groups=groups, tiled=True)


def local(right_side, start):
    n = tuple(lax.axis_size(a) for a in ("gx", "gy", "gz"))
    s, up, down = call(
        pack_kernel,
        [(12, 64, 128), (6, 64, 128), (6, 64, 128)],
        [(8, 64, 128), (8, 64, 128), pltpu.SemaphoreType.DMA, pltpu.SemaphoreType.DMA],
        [pl.BlockSpec(memory_space=pltpu.HBM)] * 2,
    )(start, right_side)
    up, down = from_both(up, down, "gz")
    s_left, s_right = from_both_round(s, s, "gx")
    v, first, last = call(widen_kernel, [(12, 64, 128), (CROSS_Y, 128), (CROSS_Y, 128)])(s, up, down)
    before, after = from_both(last, first, "gy")
    up, down = call(strips_kernel, [(CROSS_X, 128)] * 2)(v, before, after, s_left, s_right)
    y_left, y_right = from_both_round(up, down, "gx")
    up0 = (8, 80, 256)
    b1, sent, black0, red_b0, black_b0 = call(
        functools.partial(fine_down_kernel, n),
        [(4, ROWS1, 128), (4 * SENT1, 128), up0, up0, up0],
        [(14, ROWS0 + 2 * PAD, 256)] * 2 + [(12, ROWS0, 256)] * 2 + [(3, ROWS0, 256), (8, ROWS0, 128)],
    )(s, v, before, after, s_left, s_right, y_left, y_right)
    groups = [[2 * chip + core for chip in range(n[0] // 2)] for core in range(2)]
    same = gathered(sent[None], "gx", groups)
    other = lax.ppermute(same, "gx", [(i, i ^ 1) for i in range(n[0])])
    all1 = (2 * n[0], ROWS1, 128)
    colour1 = (2 * n[0] + 2, ROWS1 + 2 * PAD, 128)
    window1 = (8, ROWS1, 128)
    blocks = (n[0] // 2, 4 * SENT1, 128)
    b2, black1, red_b1, black_b1 = call(
        functools.partial(middle_down_kernel, n),
        [(n[0], 16, 128), window1, window1, window1],
        [colour1, colour1, all1, all1, (ROWS1, 128), (2 * n[0], 40, 128)],
    )(b1, same.reshape(blocks), other.reshape(blocks))
    b2 = gathered(b2, "gy").reshape(n[1], n[0], 16, 128)
    rows2, rows3 = 16 * n[1], 8 * n[1]
    packed = n[0] // 2
    all2, colour2, colour3 = (packed, rows2, 128), (packed + 2, rows2 + 2 * PAD, 128), (packed + 2, rows3 + 2 * PAD, 128)
    b3, black2, red_b2, black_b2 = call(
        functools.partial(coarse_down_kernel, n),
        [(max(1, packed // 2), rows3, 128), all2, all2, all2],
        [colour2, colour2, (rows2, 128), all2],
    )(b2)
    left, right = from_both(b3, b3, "gz")
    (out,) = call(
        functools.partial(up_kernel, n),
        [(8, 64, 128)],
        [
            colour2, colour2, (rows2, 128),
            (packed, rows3, 128), (packed, rows3, 128), colour3, colour3, (rows3, 128), all2,
            window1, (10, ROWS1 + 2 * PAD, 128), (10, ROWS1 + 2 * PAD, 128), window1,
            (16, 80, 128), (10, 80 + 2 * PAD, 256), (10, 80 + 2 * PAD, 256), (3, 80, 256),
        ],
    )(b3, left, right, black2, red_b2, black_b2, black1, red_b1, black_b1, black0, red_b0, black_b0)
    return out


def solution(mesh):
    in_specs = (P("gx", "gy", "gz"), P("gx", "gy", "gz"))
    out_specs = P("gx", "gy", "gz")
    return jax.shard_map(local, mesh=mesh, in_specs=in_specs, out_specs=out_specs, check_vma=False)
```

```python
import functools

import jax
import jax.numpy as jnp
from jax import lax
from jax.experimental import pallas as pl
from jax.experimental.pallas import tpu as pltpu
from jax.sharding import PartitionSpec as P

F32 = jnp.float32
BF16 = jnp.bfloat16
SIXTH = 1.0 / 6.0
EY = 24
ROWS0 = 64 + 2 * EY
ROWS1 = ROWS0 // 2
SENT1 = 50
SENT1_AT = 3
PAD = 8
UP0 = EY - 8
VMEM_LIMIT = 40 * 1024 * 1024


def call(kernel, outs, scratch=(), in_specs=None):
    shapes = [jax.ShapeDtypeStruct(s, F32) for s in outs]
    extra = {} if in_specs is None else {"in_specs": in_specs}
    return pl.pallas_call(
        kernel,
        out_shape=shapes,
        scratch_shapes=[pltpu.VMEM(s, F32) if isinstance(s, tuple) else s for s in scratch],
        compiler_params=pltpu.CompilerParams(vmem_limit_bytes=VMEM_LIMIT),
        **extra,
    )


def even_mask(shape):
    rows = lax.broadcasted_iota(jnp.int32, shape, 0)
    lanes = lax.broadcasted_iota(jnp.int32, shape, 1)
    return ((rows + lanes) & 1) == 0


def lane_of(shape):
    return lax.broadcasted_iota(jnp.int32, shape, 1)


def domain(shape, row0, rows, lane0, lanes, cut, unused=None):
    y = lax.broadcasted_iota(jnp.int32, shape, 0) + row0
    k = lane_of(shape)
    z = jnp.where(k < cut, k, k - shape[1]) + lane0
    inside = (y >= 0) & (y < rows) & (z >= 0) & (z < lanes)
    if unused is not None:
        inside = inside & ((k < unused[0]) | (k >= unused[1]))
    return jnp.where(inside, F32(SIXTH), F32(0.0))


def beside(src, i, r, rows, even, red):
    at = PAD + r
    c = src[i + 1, at : at + rows]
    below, above = src[i, at : at + rows], src[i + 2, at : at + rows]
    s = c + (jnp.where(even, below, above) if red else jnp.where(even, above, below))
    s = s + (src[i + 1, at - 1 : at - 1 + rows] + src[i + 1, at + 1 : at + 1 + rows])
    return s + (pltpu.roll(c, 1, 1) + pltpu.roll(c, c.shape[1] - 1, 1))


def half(dst, src, b, weight, red, pairs, rows, step):
    even = even_mask((step, dst.shape[2]))
    for i in pairs:
        for r in range(0, rows, step):
            value = (b[i, r : r + step] + beside(src, i, r, step, even, red)) * weight(i, r, step)
            dst[i + 1, PAD + r : PAD + r + step] = value


def residual_sum(red, black, red_b, black_b, i, r, step, even):
    at = PAD + r
    x = red_b[i, r : r + step] - 6.0 * red[i + 1, at : at + step] + beside(black, i, r, step, even, True)
    y = black_b[i, r : r + step] - 6.0 * black[i + 1, at : at + step] + beside(red, i, r, step, even, False)
    return x + y


def clear_pads(*colours):
    for ref in colours:
        pairs, rows, lanes = ref.shape
        for i in (0, pairs - 1):
            ref[i] = jnp.zeros((rows, lanes), F32)
        for i in range(1, pairs - 1):
            ref[i, :PAD] = jnp.zeros((PAD, lanes), F32)
            ref[i, rows - PAD :] = jnp.zeros((PAD, lanes), F32)


def table(rows, cols, of, value=1.0):
    k = lax.broadcasted_iota(jnp.int32, (rows, cols), 0)
    c = lax.broadcasted_iota(jnp.int32, (rows, cols), 1)
    return jnp.where(of(k, c), F32(value), F32(0.0)).astype(BF16)


def dot(a, m):
    high = a.astype(BF16)
    rest = a - high.astype(F32)
    middle = rest.astype(BF16)
    low = (rest - middle.astype(F32)).astype(BF16)
    parts = jnp.concatenate([high, middle, low], axis=1)
    return jnp.dot(parts, jnp.concatenate([m, m, m], axis=0), preferred_element_type=F32)


def pack_kernel(start_hbm, right_hbm, s, up, down, start, right, sem_a, sem_b):
    copy_a = pltpu.make_async_copy(start_hbm, start, sem_a)
    copy_b = pltpu.make_async_copy(right_hbm, right, sem_b)
    copy_a.start()
    copy_b.start()
    even = even_mask((64, 128))
    low = lane_of((64, 128)) < 64
    copy_a.wait()
    copy_b.wait()
    for p in range(4):
        s[p] = jnp.where(even, start[2 * p + 1], start[2 * p])
        s[p + 4] = jnp.where(even, right[2 * p], right[2 * p + 1])
        s[p + 8] = jnp.where(even, right[2 * p + 1], right[2 * p])
    for p in range(6):
        a, b = s[p], pltpu.roll(s[p + 6], 64, 1)
        up[p] = jnp.where(low, b, a)
        down[p] = jnp.where(low, a, b)


def pack16(planes, first=0):
    lanes = lane_of(planes[0].shape)
    total = jnp.zeros(planes[0].shape, F32)
    for k, plane in enumerate(planes):
        at = 16 * (k + first)
        total = jnp.where((lanes >= at) & (lanes < at + 16), pltpu.roll(plane, (8 + at) % 128, 1), total)
    return total


def unpack16(packed, k):
    lanes = lane_of(packed.shape)
    shift = (-8 - 16 * k) % 128
    plane = pltpu.roll(packed, shift, 1) if shift else packed
    return jnp.where((lanes < 8) | (lanes >= 120), plane, 0.0)


UP_NEAR, UP_FAR = (1, 2, 3, 6, 7, 10, 11), (0, 4, 5, 8, 9)
DOWN_NEAR, DOWN_FAR = (0, 1, 2, 4, 5, 8, 9), (3, 6, 7, 10, 11)
NEAR, FAR = len(UP_NEAR), len(UP_FAR)
CROSS_Y = 12 * 24 + 12 * 16 + 2 * 8
STRIP_AT = 48 * NEAR
FAR_AT = STRIP_AT + 32 * NEAR
PACKED_AT = FAR_AT + 16 * FAR
WHOLE_AT = PACKED_AT + 2 * 16
CROSS_X = WHOLE_AT + 64


def widen_kernel(s, up, down, v, v_up, v_down, first, last):
    low = lane_of((64, 128)) < 64
    for p in range(6):
        v[p] = jnp.where(low, down[p], up[p])
        v[p + 6] = pltpu.roll(jnp.where(low, up[p], down[p]), 64, 1)
    for p in range(12):
        first[24 * p : 24 * p + 24] = s[p, :24]
        last[24 * p : 24 * p + 24] = s[p, 40:]
        at = 288 + 16 * p
        first[at : at + 16] = v[p, :16]
        last[at : at + 16] = v[p, 48:]
    for t in range(2):
        at = 480 + 8 * t
        first[at : at + 8] = pack16([v[6 * t + k, 16:24] for k in range(6)])
        last[at : at + 8] = pack16([v[6 * t + k, 40:48] for k in range(6)])
    for ref, near in ((v_up, UP_NEAR), (v_down, DOWN_NEAR)):
        for k, p in enumerate(near):
            ref[k] = v[p]


def strips_kernel(v, before, after, *rest):
    lanes = lane_of((8, 128))
    for ref, near, far in ((rest[-2], UP_NEAR, UP_FAR), (rest[-1], DOWN_NEAR, DOWN_FAR)):
        outer = [jnp.zeros((8, 128), F32), jnp.zeros((8, 128), F32)]
        for k, p in enumerate(near):
            ref[48 * k : 48 * k + 24] = before[24 * p : 24 * p + 24]
            ref[48 * k + 24 : 48 * k + 48] = after[24 * p : 24 * p + 24]
            at, inner = STRIP_AT + 32 * k, 288 + 16 * p
            ref[at : at + 16] = before[inner : inner + 16]
            ref[at + 16 : at + 32] = after[inner : inner + 16]
            at, shift = 480 + 8 * (p // 6), 16 * (k - p % 6) % 128
            for h, strip in enumerate((before, after)):
                plane = strip[at : at + 8]
                plane = pltpu.roll(plane, shift, 1) if shift else plane
                outer[h] = jnp.where((lanes >= 16 * k) & (lanes < 16 * k + 16), plane, outer[h])
        ref[WHOLE_AT:] = pack16([v[p] for p in far])
        edges = [[], []]
        for k, p in enumerate(far):
            at, inner = FAR_AT + 16 * k, 288 + 16 * p
            ref[at : at + 8] = before[24 * p + 16 : 24 * p + 24]
            ref[at + 8 : at + 16] = after[24 * p : 24 * p + 8]
            edges[0].append(before[inner + 8 : inner + 16])
            edges[1].append(after[inner : inner + 8])
        for h in range(2):
            at = PACKED_AT + 8 * h
            ref[at : at + 8] = outer[h]
            ref[at + 16 : at + 24] = pack16(edges[h])


def fine_down_kernel(
    n, s, v, before, after, s_left, s_right, v_left, v_right, y_left, y_right,
    coarse, sent, black_out, red_b_out, black_b_out, red, black, rb, bb, weight, pairs,
):
    gx, gy, gz = (lax.axis_index(a) for a in ("gx", "gy", "gz"))
    inner = domain((ROWS0, 256), 64 * gy - EY, 64 * n[1], 128 * gz, 128 * n[2], 192)
    has_left, has_right = gx > 0, gx < n[0] - 1
    weight[0] = jnp.where(has_left, inner, 0.0)
    weight[1] = inner
    weight[2] = jnp.where(has_right, inner, 0.0)
    clear_pads(black, red)
    block, strip = slice(0, 128), slice(128, 256)
    zero8 = jnp.zeros((8, 128), F32)
    for a, ref in enumerate((black, rb, bb)):
        off, top = (1, PAD) if a == 0 else (0, 0)

        def put(i, lo, lanes, value, there=None, ref=ref, off=off, top=top, a=a):
            if a == 0 and there is not None:
                value = jnp.where(there, value, 0.0)
            ref[i + off, top + lo : top + lo + value.shape[0], lanes] = value

        for p in range(4):
            j, i = 4 * a + p, 4 + p
            put(i, EY, block, s[j])
            put(i, EY, strip, v[j])
            put(p, EY, block, s_left[j], has_left)
            put(8 + p, EY, block, s_right[j], has_right)
            put(i, 0, block, before[24 * j : 24 * j + 24])
            put(i, EY + 64, block, after[24 * j : 24 * j + 24])
            at = 288 + 16 * j
            put(i, 8, strip, before[at : at + 16])
            put(i, EY + 64, strip, after[at : at + 16])
            at = 480 + 8 * (j // 6)
            put(i, 0, strip, unpack16(before[at : at + 8], j % 6))
            put(i, EY + 80, strip, unpack16(after[at : at + 8], j % 6))
        sides = ((0, UP_NEAR, UP_FAR, v_left, y_left, has_left), (8, DOWN_NEAR, DOWN_FAR, v_right, y_right, has_right))
        for base, near, far, strips, y, there in sides:
            for k, p in enumerate(near):
                if p // 4 != a:
                    continue
                i = base + p % 4
                put(i, EY, strip, strips[k], there)
                put(i, 0, block, y[48 * k : 48 * k + 24], there)
                put(i, EY + 64, block, y[48 * k + 24 : 48 * k + 48], there)
                at = STRIP_AT + 32 * k
                put(i, 8, strip, y[at : at + 16], there)
                put(i, EY + 64, strip, y[at + 16 : at + 32], there)
                put(i, 0, strip, unpack16(y[PACKED_AT : PACKED_AT + 8], k), there)
                put(i, EY + 80, strip, unpack16(y[PACKED_AT + 8 : PACKED_AT + 16], k), there)
            for k, p in enumerate(far):
                if p // 4 != a:
                    continue
                i = base + p % 4
                put(i, EY, strip, unpack16(y[WHOLE_AT:], k), there)
                at = FAR_AT + 16 * k
                put(i, 16, block, y[at : at + 8], there)
                put(i, EY + 64, block, y[at + 8 : at + 16], there)
                put(i, 16, strip, unpack16(y[PACKED_AT + 16 : PACKED_AT + 24], k), there)
                put(i, EY + 64, strip, unpack16(y[PACKED_AT + 24 : PACKED_AT + 32], k), there)
                for lanes in (block, strip):
                    for lo in (0, 8, EY + 72, EY + 80):
                        put(i, lo, lanes, zero8)

    def weights(i, r, step):
        return weight[i // 4, r : r + step]

    half(red, black, rb, weights, True, range(0, 12), ROWS0, 16)
    half(black, red, bb, weights, False, range(1, 11), ROWS0, 16)
    half(red, black, rb, weights, True, range(1, 11), ROWS0, 16)
    half(black, red, bb, weights, False, range(2, 10), ROWS0, 16)
    even = even_mask((16, 256))
    for p in range(4):
        for r in range(0, ROWS0, 16):
            value = residual_sum(red, black, rb, bb, p + 4, r, 16, even)
            pairs[2 * p, r : r + 16] = value[:, :128]
            pairs[2 * p + 1, r : r + 16] = value[:, 128:]
    rows = []
    for p in range(4):
        parts = [pairs[2 * p + h, pl.ds(0, ROWS1, stride=2), :] + pairs[2 * p + h, pl.ds(1, ROWS1, stride=2), :] for h in (0, 1)]
        rows.append(jnp.concatenate(parts, axis=1))
    result = dot(jnp.concatenate(rows, axis=0), table(256, 128, lambda k, c: (k >> 1) == c, 0.5))
    for p in range(4):
        coarse[p] = result[p * ROWS1 : (p + 1) * ROWS1]
        sent[SENT1 * p : SENT1 * p + SENT1] = coarse[p, SENT1_AT : SENT1_AT + SENT1]
    for p in range(8):
        black_out[p] = black[p + 3, PAD + UP0 : PAD + UP0 + 80]
        red_b_out[p] = rb[p + 2, UP0 : UP0 + 80]
        black_b_out[p] = bb[p + 2, UP0 : UP0 + 80]


def middle_down_kernel(
    n, own, same, other, coarse, black_out, red_b_out, black_b_out, red, black, rb, bb, weight, pairs
):
    gx, gy, gz = (lax.axis_index(a) for a in ("gx", "gy", "gz"))
    count = 2 * n[0]
    core = gx % 2
    even = even_mask((ROWS1, 128))
    even_sent = even_mask((SENT1, 128)) ^ (SENT1_AT % 2 == 1)
    weight[...] = domain((ROWS1, 128), 32 * gy - EY // 2, 32 * n[1], 64 * gz, 64 * n[2], 96)
    clear_pads(red, black)
    zero = jnp.zeros((SENT1_AT, 128), F32)
    for i in range(count):
        block, q = i // 2, 2 * SENT1 * (i % 2)
        mine = core == block % 2
        a, b = (jnp.where(mine, same[block // 2, at : at + SENT1], other[block // 2, at : at + SENT1]) for at in (q, q + SENT1))
        for ref, v in ((rb, jnp.where(even_sent, a, b)), (bb, jnp.where(even_sent, b, a))):
            ref[i, :SENT1_AT] = zero
            ref[i, SENT1_AT : SENT1_AT + SENT1] = v
            ref[i, SENT1_AT + SENT1 :] = zero
    for h in range(2):
        a, b = own[2 * h], own[2 * h + 1]
        rb[2 * gx + h] = jnp.where(even, a, b)
        bb[2 * gx + h] = jnp.where(even, b, a)
    for i in range(count):
        red[i + 1, PAD : PAD + ROWS1] = rb[i] * weight[...]

    def weights(i, r, step):
        return weight[r : r + step]

    every = range(count)
    half(black, red, bb, weights, False, every, ROWS1, ROWS1)
    half(red, black, rb, weights, True, every, ROWS1, ROWS1)
    half(black, red, bb, weights, False, every, ROWS1, ROWS1)
    for i in range(8):
        q = 2 * gx - 3 + i
        inside = jnp.clip(q, 0, count - 1)
        black_out[i] = black[jnp.clip(q + 1, 0, count + 1), PAD : PAD + ROWS1]
        red_b_out[i] = rb[inside]
        black_b_out[i] = bb[inside]
    top = EY // 2 - 4
    even40 = even_mask((40, 128))
    for i in every:
        pairs[i] = residual_sum(red, black, rb, bb, i, top, 40, even40)
    sums = [pairs[i, pl.ds(4, 16, stride=2), :] + pairs[i, pl.ds(5, 16, stride=2), :] for i in every]
    to2 = lambda k: jnp.where(k < 96, (k >> 1) + 16, (k >> 1) - 48)
    low = jnp.concatenate(sums[: n[0]], axis=0)
    high = jnp.concatenate(sums[n[0] :], axis=0)
    take = table(256, 128, lambda k, c: to2(k & 127) + (k & 128) // 2 == c, 0.5)
    result = dot(jnp.concatenate([low, high], axis=1), take)
    for i in range(n[0]):
        coarse[i] = result[16 * i : 16 * i + 16]


def wrap_pairs(ref, rows):
    last = ref.shape[0] - 2
    low = lane_of((rows, 128)) < 64
    ref[0, PAD : PAD + rows] = jnp.where(low, 0.0, pltpu.roll(ref[last, PAD : PAD + rows], 64, 1))
    ref[last + 1, PAD : PAD + rows] = jnp.where(low, pltpu.roll(ref[1, PAD : PAD + rows], 64, 1), 0.0)


def domain2(n, gz, rows):
    y = lane_of((rows, 128))
    z = (y & 63) - 16 + 32 * gz
    return jnp.where((z >= 0) & (z < 32 * n[2]), F32(SIXTH), F32(0.0))


def third_place(n, i):
    packed = n[0] // 2
    arrays = max(1, packed // 2)
    p = i % packed
    return p % arrays, 64 * (i // packed) + 32 * (p // arrays)


def coarse_down_kernel(n, b2, coarse, black_out, rb, bb, red, black, weight, pairs):
    gz = lax.axis_index("gz")
    rows, packed = 16 * n[1], n[0] // 2
    weight[...] = domain2(n, gz, rows)
    clear_pads(red, black)
    even16 = even_mask((16, 128))
    for i in range(packed):
        for g in range(n[1]):
            a, b = b2[g, 2 * i], b2[g, 2 * i + 1]
            at = 16 * g
            r = jnp.where(even16, a, b)
            rb[i, at : at + 16] = r
            bb[i, at : at + 16] = jnp.where(even16, b, a)
            red[i + 1, PAD + at : PAD + at + 16] = r * weight[at : at + 16]

    def weights(i, r, step):
        return weight[r : r + step]

    every = range(packed)
    wrap_pairs(red, rows)
    half(black, red, bb, weights, False, every, rows, rows)
    wrap_pairs(black, rows)
    half(red, black, rb, weights, True, every, rows, rows)
    wrap_pairs(red, rows)
    half(black, red, bb, weights, False, every, rows, rows)
    wrap_pairs(black, rows)
    even = even_mask((rows, 128))
    for i in every:
        pairs[i] = residual_sum(red, black, rb, bb, i, 0, rows, even)
        black_out[i] = black[i + 1, PAD : PAD + rows]
    rows3 = rows // 2
    sums = [pairs[i, pl.ds(0, rows3, stride=2), :] + pairs[i, pl.ds(1, rows3, stride=2), :] for i in every]
    take = table(128, 128, lambda k, c: ((k & 63) >> 1) + (k & 64) == c, 0.5)
    result = dot(jnp.concatenate(sums, axis=0), take)
    arrays = coarse.shape[0]
    for r in range(arrays):
        total = result[r * rows3 : (r + 1) * rows3]
        if packed > arrays:
            total = total + pltpu.roll(result[(r + arrays) * rows3 : (r + arrays + 1) * rows3], 32, 1)
        coarse[r] = total


def up_kernel(
    n, b3, b3_left, b3_right, start2, rb2, bb2, black1, red_b1, black_b1, black0, red_b0, black_b0, out,
    red2, black2, weight2,
    rb3, bb3, red3, black3, weight3, add2,
    add1, red1, bl1, weight1,
    add0, red0, bl0, weight0,
):
    gx, gy, gz = (lax.axis_index(a) for a in ("gx", "gy", "gz"))
    rows2, rows3 = 16 * n[1], 8 * n[1]
    packed, pairs_3 = n[0] // 2, n[0] // 2

    shape3 = (rows3, 128)
    even3 = even_mask(shape3)
    lane3 = lane_of(shape3)
    z3 = lane3 - 24 + 16 * gz
    weight3[...] = jnp.where((z3 >= 0) & (z3 < 16 * n[2]) & (lane3 < 64), F32(SIXTH), F32(0.0))
    clear_pads(red3, black3)

    def plane3(i):
        at, lane = third_place(n, i)
        own, left, right = (pltpu.roll(ref[at], (to - lane) % 128, 1) if (to - lane) % 128 else ref[at] for ref, to in ((b3, 16), (b3_left, 0), (b3_right, 32)))
        return jnp.where(lane3 < 24, left, jnp.where(lane3 < 40, own, right))

    for i in range(pairs_3):
        a, b = plane3(2 * i), plane3(2 * i + 1)
        r = jnp.where(even3, a, b)
        rb3[i] = r
        bb3[i] = jnp.where(even3, b, a)
        red3[i + 1, PAD : PAD + rows3] = r * weight3[...]

    def weights3(i, r, step):
        return weight3[r : r + step]

    every3 = range(pairs_3)
    half(black3, red3, bb3, weights3, False, every3, rows3, rows3)

    def sweep3(_, carry):
        half(red3, black3, rb3, weights3, True, every3, rows3, rows3)
        half(black3, red3, bb3, weights3, False, every3, rows3, rows3)
        return carry

    lax.fori_loop(0, 7, sweep3, 0)
    planes = []
    for i in every3:
        r, b = red3[i + 1, PAD : PAD + rows3], black3[i + 1, PAD : PAD + rows3]
        planes += [jnp.where(even3, r, b), jnp.where(even3, b, r)]

    halves = [jnp.concatenate(planes[:packed], axis=0), jnp.concatenate(planes[packed:], axis=0)]
    spread = table(256, 128, lambda k, c: ((c & 63) >> 1) + 16 + 2 * (c & 64) == k)
    wide = dot(jnp.concatenate(halves, axis=1), spread)
    weight2[...] = domain2(n, gz, rows2)
    clear_pads(red2, black2)
    every2 = range(packed)
    for i in every2:
        w = wide[i * rows3 : (i + 1) * rows3]
        add2[i, pl.ds(0, rows3, stride=2), :] = w
        add2[i, pl.ds(1, rows3, stride=2), :] = w
        black2[i + 1, PAD : PAD + rows2] = start2[i] + add2[i]

    def weights2(i, r, step):
        return weight2[r : r + step]

    for _ in range(2):
        wrap_pairs(black2, rows2)
        half(red2, black2, rb2, weights2, True, every2, rows2, rows2)
        wrap_pairs(red2, rows2)
        half(black2, red2, bb2, weights2, False, every2, rows2, rows2)

    even32 = even_mask((32, 128))
    top = pl.multiple_of(16 * gy, 8)
    planes = []
    second = lane_of((32, 128)) >= 64
    for i in range(8):
        q = gx - 2 + (i + 1) // 2
        there = (q >= 0) & (q < n[0])
        upper = q >= packed
        at = jnp.clip(jnp.where(upper, q - packed, q), 0, packed - 1) + 1
        r, b = red2[at, pl.ds(top, 32), :], black2[at, pl.ds(top, 32), :]
        plane = jnp.where(even32, r, b) if i % 2 == 1 else jnp.where(even32, b, r)
        planes.append(jnp.where(there & (second == upper), plane, 0.0))
    to2 = lambda k, c: jnp.where(c < 96, (c >> 1) + 16, (c >> 1) - 48) == (k & 63)
    wide = dot(jnp.concatenate(planes, axis=0), table(128, 128, to2))
    inner = domain((ROWS1, 128), 32 * gy - EY // 2, 32 * n[1], 64 * gz, 64 * n[2], 96)
    clear_pads(red1, bl1)
    skip = PAD - EY // 4
    for i in range(8):
        q = 2 * gx - 3 + i
        weight1[i] = jnp.where((q >= 0) & (q < 2 * n[0]), inner, 0.0)
        w = wide[32 * i + skip : 32 * i + skip + ROWS1 // 2]
        add1[i, pl.ds(0, ROWS1 // 2, stride=2), :] = w
        add1[i, pl.ds(1, ROWS1 // 2, stride=2), :] = w
        bl1[i + 1, PAD : PAD + ROWS1] = black1[i] + add1[i]

    def weights1(i, r, step):
        return weight1[i, r : r + step]

    half(red1, bl1, red_b1, weights1, True, range(0, 8), ROWS1, ROWS1)
    half(bl1, red1, black_b1, weights1, False, range(1, 7), ROWS1, ROWS1)
    half(red1, bl1, red_b1, weights1, True, range(1, 7), ROWS1, ROWS1)
    half(bl1, red1, black_b1, weights1, False, range(2, 6), ROWS1, ROWS1)

    low1 = PAD + UP0 // 2
    even40 = even_mask((40, 128))
    planes = []
    for i in range(8):
        r, b = red1[3 + i // 2, low1 : low1 + 40], bl1[3 + i // 2, low1 : low1 + 40]
        planes.append(jnp.where(even40, r, b) if i % 2 == 0 else jnp.where(even40, b, r))
    wide = dot(jnp.concatenate(planes, axis=0), table(128, 256, lambda k, c: (c >> 1) == k))
    inner = domain((80, 256), 64 * gy - 8, 64 * n[1], 128 * gz, 128 * n[2], 192)
    weight0[0] = jnp.where(gx > 0, inner, 0.0)
    weight0[1] = inner
    weight0[2] = jnp.where(gx < n[0] - 1, inner, 0.0)
    clear_pads(red0, bl0)
    for i in range(8):
        for h in (0, 1):
            w = wide[40 * i : 40 * i + 40, 128 * h : 128 * h + 128]
            add0[2 * i + h, pl.ds(0, 40, stride=2), :] = w
            add0[2 * i + h, pl.ds(1, 40, stride=2), :] = w
            bl0[i + 1, PAD : PAD + 80, 128 * h : 128 * h + 128] = black0[i, :, 128 * h : 128 * h + 128] + add0[2 * i + h]

    def weights0(i, r, step):
        return weight0[(i + 2) // 4, r : r + step]

    half(red0, bl0, red_b0, weights0, True, range(0, 8), 80, 16)
    half(bl0, red0, black_b0, weights0, False, range(1, 7), 80, 16)
    half(red0, bl0, red_b0, weights0, True, range(1, 7), 80, 16)
    half(bl0, red0, black_b0, weights0, False, range(2, 6), 80, 16)
    even64 = even_mask((64, 128))
    for p in range(4):
        r = red0[p + 3, PAD + 8 : PAD + 72, :128]
        b = bl0[p + 3, PAD + 8 : PAD + 72, :128]
        out[2 * p] = jnp.where(even64, r, b)
        out[2 * p + 1] = jnp.where(even64, b, r)


def from_both(up_value, down_value, axis):
    size = lax.axis_size(axis)
    up = [(i, i + 1) for i in range(size - 1)]
    return lax.ppermute(up_value, axis, up), lax.ppermute(down_value, axis, [(b, a) for a, b in up])


def from_both_round(up_value, down_value, axis):
    size = lax.axis_size(axis)
    up = [(i, (i + 1) % size) for i in range(size)]
    return lax.ppermute(up_value, axis, up), lax.ppermute(down_value, axis, [(b, a) for a, b in up])


def gathered(value, axis, groups=None):
    size = lax.axis_size(axis) if groups is None else len(groups[0])
    copies = jnp.broadcast_to(value, (size, *value.shape))
    return lax.all_to_all(copies, axis, split_axis=0, concat_axis=0, axis_index_groups=groups, tiled=True)


def local(right_side, start):
    n = tuple(lax.axis_size(a) for a in ("gx", "gy", "gz"))
    s, up, down = call(
        pack_kernel,
        [(12, 64, 128), (6, 64, 128), (6, 64, 128)],
        [(8, 64, 128), (8, 64, 128), pltpu.SemaphoreType.DMA, pltpu.SemaphoreType.DMA],
        [pl.BlockSpec(memory_space=pltpu.HBM)] * 2,
    )(start, right_side)
    up, down = from_both(up, down, "gz")
    s_left, s_right = from_both_round(s, s, "gx")
    near = (NEAR, 64, 128)
    v, v_up, v_down, first, last = call(widen_kernel, [(12, 64, 128), near, near, (CROSS_Y, 128), (CROSS_Y, 128)])(s, up, down)
    v_left, v_right = from_both_round(v_up, v_down, "gx")
    before, after = from_both(last, first, "gy")
    up, down = call(strips_kernel, [(CROSS_X, 128)] * 2)(v, before, after, s_left, v_left, v_right)
    y_left, y_right = from_both_round(up, down, "gx")
    up0 = (8, 80, 256)
    b1, sent, black0, red_b0, black_b0 = call(
        functools.partial(fine_down_kernel, n),
        [(4, ROWS1, 128), (4 * SENT1, 128), up0, up0, up0],
        [(14, ROWS0 + 2 * PAD, 256)] * 2 + [(12, ROWS0, 256)] * 2 + [(3, ROWS0, 256), (8, ROWS0, 128)],
    )(s, v, before, after, s_left, s_right, v_left, v_right, y_left, y_right)
    groups = [[2 * chip + core for chip in range(n[0] // 2)] for core in range(2)]
    same = gathered(sent[None], "gx", groups)
    other = lax.ppermute(same, "gx", [(i, i ^ 1) for i in range(n[0])])
    all1 = (2 * n[0], ROWS1, 128)
    colour1 = (2 * n[0] + 2, ROWS1 + 2 * PAD, 128)
    window1 = (8, ROWS1, 128)
    blocks = (n[0] // 2, 4 * SENT1, 128)
    b2, black1, red_b1, black_b1 = call(
        functools.partial(middle_down_kernel, n),
        [(n[0], 16, 128), window1, window1, window1],
        [colour1, colour1, all1, all1, (ROWS1, 128), (2 * n[0], 40, 128)],
    )(b1, same.reshape(blocks), other.reshape(blocks))
    b2 = gathered(b2, "gy").reshape(n[1], n[0], 16, 128)
    rows2, rows3 = 16 * n[1], 8 * n[1]
    packed = n[0] // 2
    all2, colour2, colour3 = (packed, rows2, 128), (packed + 2, rows2 + 2 * PAD, 128), (packed + 2, rows3 + 2 * PAD, 128)
    b3, black2, red_b2, black_b2 = call(
        functools.partial(coarse_down_kernel, n),
        [(max(1, packed // 2), rows3, 128), all2, all2, all2],
        [colour2, colour2, (rows2, 128), all2],
    )(b2)
    left, right = from_both(b3, b3, "gz")
    (out,) = call(
        functools.partial(up_kernel, n),
        [(8, 64, 128)],
        [
            colour2, colour2, (rows2, 128),
            (packed, rows3, 128), (packed, rows3, 128), colour3, colour3, (rows3, 128), all2,
            window1, (10, ROWS1 + 2 * PAD, 128), (10, ROWS1 + 2 * PAD, 128), window1,
            (16, 80, 128), (10, 80 + 2 * PAD, 256), (10, 80 + 2 * PAD, 256), (3, 80, 256),
        ],
    )(b3, left, right, black2, red_b2, black_b2, black1, red_b1, black_b1, black0, red_b0, black_b0)
    return out


def solution(mesh):
    in_specs = (P("gx", "gy", "gz"), P("gx", "gy", "gz"))
    out_specs = P("gx", "gy", "gz")
    return jax.shard_map(local, mesh=mesh, in_specs=in_specs, out_specs=out_specs, check_vma=False)
```

```python
import functools

import jax
import jax.numpy as jnp
from jax import lax
from jax.experimental import pallas as pl
from jax.experimental.pallas import tpu as pltpu
from jax.sharding import PartitionSpec as P

F32 = jnp.float32
BF16 = jnp.bfloat16
SIXTH = 1.0 / 6.0
EY = 24
ROWS0 = 64 + 2 * EY
ROWS1 = ROWS0 // 2
SENT1 = 50
SENT1_AT = 3
PAD = 8
UP0 = EY - 8
VMEM_LIMIT = 40 * 1024 * 1024


def call(kernel, outs, scratch=(), in_specs=None):
    shapes = [jax.ShapeDtypeStruct(s, F32) for s in outs]
    extra = {} if in_specs is None else {"in_specs": in_specs}
    return pl.pallas_call(
        kernel,
        out_shape=shapes,
        scratch_shapes=[pltpu.VMEM(s, F32) if isinstance(s, tuple) else s for s in scratch],
        compiler_params=pltpu.CompilerParams(vmem_limit_bytes=VMEM_LIMIT),
        **extra,
    )


def even_mask(shape):
    rows = lax.broadcasted_iota(jnp.int32, shape, 0)
    lanes = lax.broadcasted_iota(jnp.int32, shape, 1)
    return ((rows + lanes) & 1) == 0


def lane_of(shape):
    return lax.broadcasted_iota(jnp.int32, shape, 1)


def domain(shape, row0, rows, lane0, lanes, cut, unused=None):
    y = lax.broadcasted_iota(jnp.int32, shape, 0) + row0
    k = lane_of(shape)
    z = jnp.where(k < cut, k, k - shape[1]) + lane0
    inside = (y >= 0) & (y < rows) & (z >= 0) & (z < lanes)
    if unused is not None:
        inside = inside & ((k < unused[0]) | (k >= unused[1]))
    return jnp.where(inside, F32(SIXTH), F32(0.0))


def beside(src, i, r, rows, even, red):
    at = PAD + r
    c = src[i + 1, at : at + rows]
    below, above = src[i, at : at + rows], src[i + 2, at : at + rows]
    s = c + (jnp.where(even, below, above) if red else jnp.where(even, above, below))
    s = s + (src[i + 1, at - 1 : at - 1 + rows] + src[i + 1, at + 1 : at + 1 + rows])
    return s + (pltpu.roll(c, 1, 1) + pltpu.roll(c, c.shape[1] - 1, 1))


def half(dst, src, b, weight, red, pairs, rows, step):
    even = even_mask((step, dst.shape[2]))
    for i in pairs:
        for r in range(0, rows, step):
            value = (b[i, r : r + step] + beside(src, i, r, step, even, red)) * weight(i, r, step)
            dst[i + 1, PAD + r : PAD + r + step] = value


def residual_sum(red, black, red_b, black_b, i, r, step, even):
    at = PAD + r
    x = red_b[i, r : r + step] - 6.0 * red[i + 1, at : at + step] + beside(black, i, r, step, even, True)
    y = black_b[i, r : r + step] - 6.0 * black[i + 1, at : at + step] + beside(red, i, r, step, even, False)
    return x + y


def clear_pads(*colours):
    for ref in colours:
        pairs, rows, lanes = ref.shape
        for i in (0, pairs - 1):
            ref[i] = jnp.zeros((rows, lanes), F32)
        for i in range(1, pairs - 1):
            ref[i, :PAD] = jnp.zeros((PAD, lanes), F32)
            ref[i, rows - PAD :] = jnp.zeros((PAD, lanes), F32)


def table(rows, cols, of, value=1.0):
    k = lax.broadcasted_iota(jnp.int32, (rows, cols), 0)
    c = lax.broadcasted_iota(jnp.int32, (rows, cols), 1)
    return jnp.where(of(k, c), F32(value), F32(0.0)).astype(BF16)


def dot(a, m):
    high = a.astype(BF16)
    rest = a - high.astype(F32)
    middle = rest.astype(BF16)
    low = (rest - middle.astype(F32)).astype(BF16)
    parts = jnp.concatenate([high, middle, low], axis=1)
    return jnp.dot(parts, jnp.concatenate([m, m, m], axis=0), preferred_element_type=F32)


def pack_kernel(start_hbm, right_hbm, s, up, down, start, right, sem_a, sem_b):
    copy_a = pltpu.make_async_copy(start_hbm, start, sem_a)
    copy_b = pltpu.make_async_copy(right_hbm, right, sem_b)
    copy_a.start()
    copy_b.start()
    even = even_mask((64, 128))
    low = lane_of((64, 128)) < 64
    copy_a.wait()
    copy_b.wait()
    for p in range(4):
        s[p] = jnp.where(even, start[2 * p + 1], start[2 * p])
        s[p + 4] = jnp.where(even, right[2 * p], right[2 * p + 1])
        s[p + 8] = jnp.where(even, right[2 * p + 1], right[2 * p])
    for p in range(6):
        a, b = s[p], pltpu.roll(s[p + 6], 64, 1)
        up[p] = jnp.where(low, b, a)
        down[p] = jnp.where(low, a, b)


def pack16(planes, first=0):
    lanes = lane_of(planes[0].shape)
    total = jnp.zeros(planes[0].shape, F32)
    for k, plane in enumerate(planes):
        at = 16 * (k + first)
        total = jnp.where((lanes >= at) & (lanes < at + 16), pltpu.roll(plane, (8 + at) % 128, 1), total)
    return total


def unpack16(packed, k):
    lanes = lane_of(packed.shape)
    shift = (-8 - 16 * k) % 128
    plane = pltpu.roll(packed, shift, 1) if shift else packed
    return jnp.where((lanes < 8) | (lanes >= 120), plane, 0.0)


UP_NEAR, UP_FAR = (1, 2, 3, 6, 7, 10, 11), (0, 4, 5, 8, 9)
DOWN_NEAR, DOWN_FAR = (0, 1, 2, 4, 5, 8, 9), (3, 6, 7, 10, 11)
NEAR, FAR = len(UP_NEAR), len(UP_FAR)
CROSS_Y = 12 * 24 + 12 * 16 + 2 * 8
STRIP_AT = 48 * NEAR
FAR_AT = STRIP_AT + 32 * NEAR
PACKED_AT = FAR_AT + 16 * FAR
WHOLE_AT = PACKED_AT + 2 * 16
CROSS_X = WHOLE_AT + 64


def widen_kernel(s, up, down, v, v_up, v_down, first, last):
    low = lane_of((64, 128)) < 64
    for p in range(6):
        v[p] = jnp.where(low, down[p], up[p])
        v[p + 6] = pltpu.roll(jnp.where(low, up[p], down[p]), 64, 1)
    for p in range(12):
        first[24 * p : 24 * p + 24] = s[p, :24]
        last[24 * p : 24 * p + 24] = s[p, 40:]
        at = 288 + 16 * p
        first[at : at + 16] = v[p, :16]
        last[at : at + 16] = v[p, 48:]
    for t in range(2):
        at = 480 + 8 * t
        first[at : at + 8] = pack16([v[6 * t + k, 16:24] for k in range(6)])
        last[at : at + 8] = pack16([v[6 * t + k, 40:48] for k in range(6)])
    for ref, near in ((v_up, UP_NEAR), (v_down, DOWN_NEAR)):
        for k, p in enumerate(near):
            ref[k] = v[p]


def strips_kernel(v, before, after, *rest):
    lanes = lane_of((8, 128))
    for ref, near, far in ((rest[-2], UP_NEAR, UP_FAR), (rest[-1], DOWN_NEAR, DOWN_FAR)):
        outer = [jnp.zeros((8, 128), F32), jnp.zeros((8, 128), F32)]
        for k, p in enumerate(near):
            ref[48 * k : 48 * k + 24] = before[24 * p : 24 * p + 24]
            ref[48 * k + 24 : 48 * k + 48] = after[24 * p : 24 * p + 24]
            at, inner = STRIP_AT + 32 * k, 288 + 16 * p
            ref[at : at + 16] = before[inner : inner + 16]
            ref[at + 16 : at + 32] = after[inner : inner + 16]
            at, shift = 480 + 8 * (p // 6), 16 * (k - p % 6) % 128
            for h, strip in enumerate((before, after)):
                plane = strip[at : at + 8]
                plane = pltpu.roll(plane, shift, 1) if shift else plane
                outer[h] = jnp.where((lanes >= 16 * k) & (lanes < 16 * k + 16), plane, outer[h])
        ref[WHOLE_AT:] = pack16([v[p] for p in far])
        edges = [[], []]
        for k, p in enumerate(far):
            at, inner = FAR_AT + 16 * k, 288 + 16 * p
            ref[at : at + 8] = before[24 * p + 16 : 24 * p + 24]
            ref[at + 8 : at + 16] = after[24 * p : 24 * p + 8]
            edges[0].append(before[inner + 8 : inner + 16])
            edges[1].append(after[inner : inner + 8])
        for h in range(2):
            at = PACKED_AT + 8 * h
            ref[at : at + 8] = outer[h]
            ref[at + 16 : at + 24] = pack16(edges[h])


def fine_down_kernel(
    n, s, v, before, after, s_left, s_right, v_left, v_right, y_left, y_right,
    coarse, sent, black_out, red_b_out, black_b_out, red, black, rb, bb, weight, pairs,
):
    gx, gy, gz = (lax.axis_index(a) for a in ("gx", "gy", "gz"))
    inner = domain((ROWS0, 256), 64 * gy - EY, 64 * n[1], 128 * gz, 128 * n[2], 192)
    has_left, has_right = gx > 0, gx < n[0] - 1
    weight[0] = jnp.where(has_left, inner, 0.0)
    weight[1] = inner
    weight[2] = jnp.where(has_right, inner, 0.0)
    clear_pads(black, red)
    block, strip = slice(0, 128), slice(128, 256)
    zero8 = jnp.zeros((8, 128), F32)
    for a, ref in enumerate((black, rb, bb)):
        off, top = (1, PAD) if a == 0 else (0, 0)

        def put(i, lo, lanes, value, there=None, ref=ref, off=off, top=top, a=a):
            if a == 0 and there is not None:
                value = jnp.where(there, value, 0.0)
            ref[i + off, top + lo : top + lo + value.shape[0], lanes] = value

        for p in range(4):
            j, i = 4 * a + p, 4 + p
            put(i, EY, block, s[j])
            put(i, EY, strip, v[j])
            put(p, EY, block, s_left[j], has_left)
            put(8 + p, EY, block, s_right[j], has_right)
            put(i, 0, block, before[24 * j : 24 * j + 24])
            put(i, EY + 64, block, after[24 * j : 24 * j + 24])
            at = 288 + 16 * j
            put(i, 8, strip, before[at : at + 16])
            put(i, EY + 64, strip, after[at : at + 16])
            at = 480 + 8 * (j // 6)
            put(i, 0, strip, unpack16(before[at : at + 8], j % 6))
            put(i, EY + 80, strip, unpack16(after[at : at + 8], j % 6))
        sides = ((0, UP_NEAR, UP_FAR, v_left, y_left, has_left), (8, DOWN_NEAR, DOWN_FAR, v_right, y_right, has_right))
        for base, near, far, strips, y, there in sides:
            for k, p in enumerate(near):
                if p // 4 != a:
                    continue
                i = base + p % 4
                put(i, EY, strip, strips[k], there)
                put(i, 0, block, y[48 * k : 48 * k + 24], there)
                put(i, EY + 64, block, y[48 * k + 24 : 48 * k + 48], there)
                at = STRIP_AT + 32 * k
                put(i, 8, strip, y[at : at + 16], there)
                put(i, EY + 64, strip, y[at + 16 : at + 32], there)
                put(i, 0, strip, unpack16(y[PACKED_AT : PACKED_AT + 8], k), there)
                put(i, EY + 80, strip, unpack16(y[PACKED_AT + 8 : PACKED_AT + 16], k), there)
            for k, p in enumerate(far):
                if p // 4 != a:
                    continue
                i = base + p % 4
                put(i, EY, strip, unpack16(y[WHOLE_AT:], k), there)
                at = FAR_AT + 16 * k
                put(i, 16, block, y[at : at + 8], there)
                put(i, EY + 64, block, y[at + 8 : at + 16], there)
                put(i, 16, strip, unpack16(y[PACKED_AT + 16 : PACKED_AT + 24], k), there)
                put(i, EY + 64, strip, unpack16(y[PACKED_AT + 24 : PACKED_AT + 32], k), there)
                for lanes in (block, strip):
                    for lo in (0, 8, EY + 72, EY + 80):
                        put(i, lo, lanes, zero8)

    def weights(i, r, step):
        return weight[i // 4, r : r + step]

    half(red, black, rb, weights, True, range(0, 12), ROWS0, 16)
    half(black, red, bb, weights, False, range(1, 11), ROWS0, 16)
    half(red, black, rb, weights, True, range(1, 11), ROWS0, 16)
    half(black, red, bb, weights, False, range(2, 10), ROWS0, 16)
    even = even_mask((16, 256))
    for p in range(4):
        for r in range(0, ROWS0, 16):
            value = residual_sum(red, black, rb, bb, p + 4, r, 16, even)
            pairs[2 * p, r : r + 16] = value[:, :128]
            pairs[2 * p + 1, r : r + 16] = value[:, 128:]
    rows = []
    for p in range(4):
        parts = [pairs[2 * p + h, pl.ds(0, ROWS1, stride=2), :] + pairs[2 * p + h, pl.ds(1, ROWS1, stride=2), :] for h in (0, 1)]
        rows.append(jnp.concatenate(parts, axis=1))
    result = dot(jnp.concatenate(rows, axis=0), table(256, 128, lambda k, c: (k >> 1) == c, 0.5))
    for p in range(4):
        coarse[p] = result[p * ROWS1 : (p + 1) * ROWS1]
        sent[SENT1 * p : SENT1 * p + SENT1] = coarse[p, SENT1_AT : SENT1_AT + SENT1]
    for p in range(8):
        black_out[p] = black[p + 3, PAD + UP0 : PAD + UP0 + 80]
        red_b_out[p] = rb[p + 2, UP0 : UP0 + 80]
        black_b_out[p] = bb[p + 2, UP0 : UP0 + 80]


def middle_down_kernel(
    n, own, same, other, coarse, black_out, red_b_out, black_b_out, red, black, rb, bb, weight, pairs
):
    gx, gy, gz = (lax.axis_index(a) for a in ("gx", "gy", "gz"))
    count = 2 * n[0]
    core = gx % 2
    even = even_mask((ROWS1, 128))
    even_sent = even_mask((SENT1, 128)) ^ (SENT1_AT % 2 == 1)
    weight[...] = domain((ROWS1, 128), 32 * gy - EY // 2, 32 * n[1], 64 * gz, 64 * n[2], 96)
    clear_pads(red, black)
    zero = jnp.zeros((SENT1_AT, 128), F32)
    for i in range(count):
        block, q = i // 2, 2 * SENT1 * (i % 2)
        mine = core == block % 2
        a, b = (jnp.where(mine, same[block // 2, at : at + SENT1], other[block // 2, at : at + SENT1]) for at in (q, q + SENT1))
        for ref, v in ((rb, jnp.where(even_sent, a, b)), (bb, jnp.where(even_sent, b, a))):
            ref[i, :SENT1_AT] = zero
            ref[i, SENT1_AT : SENT1_AT + SENT1] = v
            ref[i, SENT1_AT + SENT1 :] = zero
    for h in range(2):
        a, b = own[2 * h], own[2 * h + 1]
        rb[2 * gx + h] = jnp.where(even, a, b)
        bb[2 * gx + h] = jnp.where(even, b, a)
    for i in range(count):
        red[i + 1, PAD : PAD + ROWS1] = rb[i] * weight[...]

    def weights(i, r, step):
        return weight[r : r + step]

    every = range(count)
    half(black, red, bb, weights, False, every, ROWS1, ROWS1)
    half(red, black, rb, weights, True, every, ROWS1, ROWS1)
    half(black, red, bb, weights, False, every, ROWS1, ROWS1)
    for i in range(8):
        q = 2 * gx - 3 + i
        inside = jnp.clip(q, 0, count - 1)
        black_out[i] = black[jnp.clip(q + 1, 0, count + 1), PAD : PAD + ROWS1]
        red_b_out[i] = rb[inside]
        black_b_out[i] = bb[inside]
    top = EY // 2 - 4
    even40 = even_mask((40, 128))
    for i in every:
        pairs[i] = residual_sum(red, black, rb, bb, i, top, 40, even40)
    sums = [pairs[i, pl.ds(4, 16, stride=2), :] + pairs[i, pl.ds(5, 16, stride=2), :] for i in every]
    to2 = lambda k: jnp.where(k < 96, (k >> 1) + 16, (k >> 1) - 48)
    low = jnp.concatenate(sums[: n[0]], axis=0)
    high = jnp.concatenate(sums[n[0] :], axis=0)
    take = table(256, 128, lambda k, c: to2(k & 127) + (k & 128) // 2 == c, 0.5)
    result = dot(jnp.concatenate([low, high], axis=1), take)
    for i in range(n[0]):
        coarse[i] = result[16 * i : 16 * i + 16]


def wrap_pairs(ref, rows):
    last = ref.shape[0] - 2
    low = lane_of((rows, 128)) < 64
    ref[0, PAD : PAD + rows] = jnp.where(low, 0.0, pltpu.roll(ref[last, PAD : PAD + rows], 64, 1))
    ref[last + 1, PAD : PAD + rows] = jnp.where(low, pltpu.roll(ref[1, PAD : PAD + rows], 64, 1), 0.0)


def domain2(n, gz, rows):
    y = lane_of((rows, 128))
    z = (y & 63) - 16 + 32 * gz
    return jnp.where((z >= 0) & (z < 32 * n[2]), F32(SIXTH), F32(0.0))


def third_place(n, i):
    packed = n[0] // 2
    arrays = max(1, packed // 2)
    p = i % packed
    return p % arrays, 64 * (i // packed) + 32 * (p // arrays)


def coarse_down_kernel(n, b2, coarse, black_out, rb, bb, red, black, weight, pairs):
    gz = lax.axis_index("gz")
    rows, packed = 16 * n[1], n[0] // 2
    weight[...] = domain2(n, gz, rows)
    clear_pads(red, black)
    even16 = even_mask((16, 128))
    for i in range(packed):
        for g in range(n[1]):
            a, b = b2[g, 2 * i], b2[g, 2 * i + 1]
            at = 16 * g
            r = jnp.where(even16, a, b)
            rb[i, at : at + 16] = r
            bb[i, at : at + 16] = jnp.where(even16, b, a)
            red[i + 1, PAD + at : PAD + at + 16] = r * weight[at : at + 16]

    def weights(i, r, step):
        return weight[r : r + step]

    every = range(packed)
    wrap_pairs(red, rows)
    half(black, red, bb, weights, False, every, rows, rows)
    wrap_pairs(black, rows)
    half(red, black, rb, weights, True, every, rows, rows)
    wrap_pairs(red, rows)
    half(black, red, bb, weights, False, every, rows, rows)
    wrap_pairs(black, rows)
    even = even_mask((rows, 128))
    for i in every:
        pairs[i] = residual_sum(red, black, rb, bb, i, 0, rows, even)
        black_out[i] = black[i + 1, PAD : PAD + rows]
    rows3 = rows // 2
    sums = [pairs[i, pl.ds(0, rows3, stride=2), :] + pairs[i, pl.ds(1, rows3, stride=2), :] for i in every]
    take = table(128, 128, lambda k, c: ((k & 63) >> 1) + (k & 64) == c, 0.5)
    result = dot(jnp.concatenate(sums, axis=0), take)
    arrays = coarse.shape[0]
    for r in range(arrays):
        total = result[r * rows3 : (r + 1) * rows3]
        if packed > arrays:
            total = total + pltpu.roll(result[(r + arrays) * rows3 : (r + arrays + 1) * rows3], 32, 1)
        coarse[r] = total


def up_kernel(
    n, b3, b3_left, b3_right, start2, rb2, bb2, black1, red_b1, black_b1, black0, red_b0, black_b0, out,
    red2, black2, weight2,
    rb3, bb3, red3, black3, weight3, add2,
    add1, red1, bl1, weight1,
    add0, red0, bl0, weight0,
):
    gx, gy, gz = (lax.axis_index(a) for a in ("gx", "gy", "gz"))
    rows2, rows3 = 16 * n[1], 8 * n[1]
    packed, pairs_3 = n[0] // 2, n[0] // 2

    shape3 = (rows3, 128)
    even3 = even_mask(shape3)
    lane3 = lane_of(shape3)
    z3 = lane3 - 24 + 16 * gz
    weight3[...] = jnp.where((z3 >= 0) & (z3 < 16 * n[2]) & (lane3 < 64), F32(SIXTH), F32(0.0))
    clear_pads(red3, black3)

    def plane3(i):
        at, lane = third_place(n, i)
        own, left, right = (pltpu.roll(ref[at], (to - lane) % 128, 1) if (to - lane) % 128 else ref[at] for ref, to in ((b3, 16), (b3_left, 0), (b3_right, 32)))
        return jnp.where(lane3 < 24, left, jnp.where(lane3 < 40, own, right))

    for i in range(pairs_3):
        a, b = plane3(2 * i), plane3(2 * i + 1)
        r = jnp.where(even3, a, b)
        rb3[i] = r
        bb3[i] = jnp.where(even3, b, a)
        red3[i + 1, PAD : PAD + rows3] = r * weight3[...]

    def weights3(i, r, step):
        return weight3[r : r + step]

    every3 = range(pairs_3)
    half(black3, red3, bb3, weights3, False, every3, rows3, rows3)

    for _ in range(7):
        half(red3, black3, rb3, weights3, True, every3, rows3, rows3)
        half(black3, red3, bb3, weights3, False, every3, rows3, rows3)
    planes = []
    for i in every3:
        r, b = red3[i + 1, PAD : PAD + rows3], black3[i + 1, PAD : PAD + rows3]
        planes += [jnp.where(even3, r, b), jnp.where(even3, b, r)]

    halves = [jnp.concatenate(planes[:packed], axis=0), jnp.concatenate(planes[packed:], axis=0)]
    spread = table(256, 128, lambda k, c: ((c & 63) >> 1) + 16 + 2 * (c & 64) == k)
    wide = dot(jnp.concatenate(halves, axis=1), spread)
    weight2[...] = domain2(n, gz, rows2)
    clear_pads(red2, black2)
    every2 = range(packed)
    for i in every2:
        w = wide[i * rows3 : (i + 1) * rows3]
        add2[i, pl.ds(0, rows3, stride=2), :] = w
        add2[i, pl.ds(1, rows3, stride=2), :] = w
        black2[i + 1, PAD : PAD + rows2] = start2[i] + add2[i]

    def weights2(i, r, step):
        return weight2[r : r + step]

    for _ in range(2):
        wrap_pairs(black2, rows2)
        half(red2, black2, rb2, weights2, True, every2, rows2, rows2)
        wrap_pairs(red2, rows2)
        half(black2, red2, bb2, weights2, False, every2, rows2, rows2)

    even32 = even_mask((32, 128))
    top = pl.multiple_of(16 * gy, 8)
    planes = []
    second = lane_of((32, 128)) >= 64
    for i in range(8):
        q = gx - 2 + (i + 1) // 2
        there = (q >= 0) & (q < n[0])
        upper = q >= packed
        at = jnp.clip(jnp.where(upper, q - packed, q), 0, packed - 1) + 1
        r, b = red2[at, pl.ds(top, 32), :], black2[at, pl.ds(top, 32), :]
        plane = jnp.where(even32, r, b) if i % 2 == 1 else jnp.where(even32, b, r)
        planes.append(jnp.where(there & (second == upper), plane, 0.0))
    to2 = lambda k, c: jnp.where(c < 96, (c >> 1) + 16, (c >> 1) - 48) == (k & 63)
    wide = dot(jnp.concatenate(planes, axis=0), table(128, 128, to2))
    inner = domain((ROWS1, 128), 32 * gy - EY // 2, 32 * n[1], 64 * gz, 64 * n[2], 96)
    clear_pads(red1, bl1)
    skip = PAD - EY // 4
    for i in range(8):
        q = 2 * gx - 3 + i
        weight1[i] = jnp.where((q >= 0) & (q < 2 * n[0]), inner, 0.0)
        w = wide[32 * i + skip : 32 * i + skip + ROWS1 // 2]
        add1[i, pl.ds(0, ROWS1 // 2, stride=2), :] = w
        add1[i, pl.ds(1, ROWS1 // 2, stride=2), :] = w
        bl1[i + 1, PAD : PAD + ROWS1] = black1[i] + add1[i]

    def weights1(i, r, step):
        return weight1[i, r : r + step]

    half(red1, bl1, red_b1, weights1, True, range(0, 8), ROWS1, ROWS1)
    half(bl1, red1, black_b1, weights1, False, range(1, 7), ROWS1, ROWS1)
    half(red1, bl1, red_b1, weights1, True, range(1, 7), ROWS1, ROWS1)
    half(bl1, red1, black_b1, weights1, False, range(2, 6), ROWS1, ROWS1)

    low1 = PAD + UP0 // 2
    even40 = even_mask((40, 128))
    planes = []
    for i in range(8):
        r, b = red1[3 + i // 2, low1 : low1 + 40], bl1[3 + i // 2, low1 : low1 + 40]
        planes.append(jnp.where(even40, r, b) if i % 2 == 0 else jnp.where(even40, b, r))
    wide = dot(jnp.concatenate(planes, axis=0), table(128, 256, lambda k, c: (c >> 1) == k))
    inner = domain((80, 256), 64 * gy - 8, 64 * n[1], 128 * gz, 128 * n[2], 192)
    weight0[0] = jnp.where(gx > 0, inner, 0.0)
    weight0[1] = inner
    weight0[2] = jnp.where(gx < n[0] - 1, inner, 0.0)
    clear_pads(red0, bl0)
    for i in range(8):
        for h in (0, 1):
            w = wide[40 * i : 40 * i + 40, 128 * h : 128 * h + 128]
            add0[2 * i + h, pl.ds(0, 40, stride=2), :] = w
            add0[2 * i + h, pl.ds(1, 40, stride=2), :] = w
            bl0[i + 1, PAD : PAD + 80, 128 * h : 128 * h + 128] = black0[i, :, 128 * h : 128 * h + 128] + add0[2 * i + h]

    def weights0(i, r, step):
        return weight0[(i + 2) // 4, r : r + step]

    half(red0, bl0, red_b0, weights0, True, range(0, 8), 80, 16)
    half(bl0, red0, black_b0, weights0, False, range(1, 7), 80, 16)
    half(red0, bl0, red_b0, weights0, True, range(1, 7), 80, 16)
    half(bl0, red0, black_b0, weights0, False, range(2, 6), 80, 16)
    even64 = even_mask((64, 128))
    for p in range(4):
        r = red0[p + 3, PAD + 8 : PAD + 72, :128]
        b = bl0[p + 3, PAD + 8 : PAD + 72, :128]
        out[2 * p] = jnp.where(even64, r, b)
        out[2 * p + 1] = jnp.where(even64, b, r)


def from_both(up_value, down_value, axis):
    size = lax.axis_size(axis)
    up = [(i, i + 1) for i in range(size - 1)]
    return lax.ppermute(up_value, axis, up), lax.ppermute(down_value, axis, [(b, a) for a, b in up])


def from_both_round(up_value, down_value, axis):
    size = lax.axis_size(axis)
    up = [(i, (i + 1) % size) for i in range(size)]
    return lax.ppermute(up_value, axis, up), lax.ppermute(down_value, axis, [(b, a) for a, b in up])


def gathered(value, axis, groups=None):
    size = lax.axis_size(axis) if groups is None else len(groups[0])
    copies = jnp.broadcast_to(value, (size, *value.shape))
    return lax.all_to_all(copies, axis, split_axis=0, concat_axis=0, axis_index_groups=groups, tiled=True)


def local(right_side, start):
    n = tuple(lax.axis_size(a) for a in ("gx", "gy", "gz"))
    s, up, down = call(
        pack_kernel,
        [(12, 64, 128), (6, 64, 128), (6, 64, 128)],
        [(8, 64, 128), (8, 64, 128), pltpu.SemaphoreType.DMA, pltpu.SemaphoreType.DMA],
        [pl.BlockSpec(memory_space=pltpu.HBM)] * 2,
    )(start, right_side)
    up, down = from_both(up, down, "gz")
    s_left, s_right = from_both_round(s, s, "gx")
    near = (NEAR, 64, 128)
    v, v_up, v_down, first, last = call(widen_kernel, [(12, 64, 128), near, near, (CROSS_Y, 128), (CROSS_Y, 128)])(s, up, down)
    v_left, v_right = from_both_round(v_up, v_down, "gx")
    before, after = from_both(last, first, "gy")
    up, down = call(strips_kernel, [(CROSS_X, 128)] * 2)(v, before, after, s_left, v_left, v_right)
    y_left, y_right = from_both_round(up, down, "gx")
    up0 = (8, 80, 256)
    b1, sent, black0, red_b0, black_b0 = call(
        functools.partial(fine_down_kernel, n),
        [(4, ROWS1, 128), (4 * SENT1, 128), up0, up0, up0],
        [(14, ROWS0 + 2 * PAD, 256)] * 2 + [(12, ROWS0, 256)] * 2 + [(3, ROWS0, 256), (8, ROWS0, 128)],
    )(s, v, before, after, s_left, s_right, v_left, v_right, y_left, y_right)
    groups = [[2 * chip + core for chip in range(n[0] // 2)] for core in range(2)]
    same = gathered(sent[None], "gx", groups)
    other = lax.ppermute(same, "gx", [(i, i ^ 1) for i in range(n[0])])
    all1 = (2 * n[0], ROWS1, 128)
    colour1 = (2 * n[0] + 2, ROWS1 + 2 * PAD, 128)
    window1 = (8, ROWS1, 128)
    blocks = (n[0] // 2, 4 * SENT1, 128)
    b2, black1, red_b1, black_b1 = call(
        functools.partial(middle_down_kernel, n),
        [(n[0], 16, 128), window1, window1, window1],
        [colour1, colour1, all1, all1, (ROWS1, 128), (2 * n[0], 40, 128)],
    )(b1, same.reshape(blocks), other.reshape(blocks))
    b2 = gathered(b2, "gy").reshape(n[1], n[0], 16, 128)
    rows2, rows3 = 16 * n[1], 8 * n[1]
    packed = n[0] // 2
    all2, colour2, colour3 = (packed, rows2, 128), (packed + 2, rows2 + 2 * PAD, 128), (packed + 2, rows3 + 2 * PAD, 128)
    b3, black2, red_b2, black_b2 = call(
        functools.partial(coarse_down_kernel, n),
        [(max(1, packed // 2), rows3, 128), all2, all2, all2],
        [colour2, colour2, (rows2, 128), all2],
    )(b2)
    left, right = from_both(b3, b3, "gz")
    (out,) = call(
        functools.partial(up_kernel, n),
        [(8, 64, 128)],
        [
            colour2, colour2, (rows2, 128),
            (packed, rows3, 128), (packed, rows3, 128), colour3, colour3, (rows3, 128), all2,
            window1, (10, ROWS1 + 2 * PAD, 128), (10, ROWS1 + 2 * PAD, 128), window1,
            (16, 80, 128), (10, 80 + 2 * PAD, 256), (10, 80 + 2 * PAD, 256), (3, 80, 256),
        ],
    )(b3, left, right, black2, red_b2, black_b2, black1, red_b1, black_b1, black0, red_b0, black_b0)
    return out


def solution(mesh):
    in_specs = (P("gx", "gy", "gz"), P("gx", "gy", "gz"))
    out_specs = P("gx", "gy", "gz")
    return jax.shard_map(local, mesh=mesh, in_specs=in_specs, out_specs=out_specs, check_vma=False)
```

```python
import functools

import jax
import jax.numpy as jnp
from jax import lax
from jax.experimental import pallas as pl
from jax.experimental.pallas import tpu as pltpu
from jax.sharding import PartitionSpec as P

F32 = jnp.float32
BF16 = jnp.bfloat16
SIXTH = 1.0 / 6.0
EY = 24
ROWS0 = 64 + 2 * EY
ROWS1 = ROWS0 // 2
SENT1 = 50
SENT1_AT = 3
PAD = 8
UP0 = EY - 8
VMEM_LIMIT = 40 * 1024 * 1024


def call(kernel, outs, scratch=(), in_specs=None):
    shapes = [jax.ShapeDtypeStruct(s, F32) for s in outs]
    extra = {} if in_specs is None else {"in_specs": in_specs}
    return pl.pallas_call(
        kernel,
        out_shape=shapes,
        scratch_shapes=[pltpu.VMEM(s, F32) if isinstance(s, tuple) else s for s in scratch],
        compiler_params=pltpu.CompilerParams(vmem_limit_bytes=VMEM_LIMIT),
        **extra,
    )


def even_mask(shape):
    rows = lax.broadcasted_iota(jnp.int32, shape, 0)
    lanes = lax.broadcasted_iota(jnp.int32, shape, 1)
    return ((rows + lanes) & 1) == 0


def lane_of(shape):
    return lax.broadcasted_iota(jnp.int32, shape, 1)


def domain(shape, row0, rows, lane0, lanes, cut, unused=None):
    y = lax.broadcasted_iota(jnp.int32, shape, 0) + row0
    k = lane_of(shape)
    z = jnp.where(k < cut, k, k - shape[1]) + lane0
    inside = (y >= 0) & (y < rows) & (z >= 0) & (z < lanes)
    if unused is not None:
        inside = inside & ((k < unused[0]) | (k >= unused[1]))
    return jnp.where(inside, F32(SIXTH), F32(0.0))


def beside(src, i, r, rows, even, red):
    at = PAD + r
    c = src[i + 1, at : at + rows]
    below, above = src[i, at : at + rows], src[i + 2, at : at + rows]
    s = c + (jnp.where(even, below, above) if red else jnp.where(even, above, below))
    s = s + (src[i + 1, at - 1 : at - 1 + rows] + src[i + 1, at + 1 : at + 1 + rows])
    return s + (pltpu.roll(c, 1, 1) + pltpu.roll(c, c.shape[1] - 1, 1))


def half(dst, src, b, weight, red, pairs, rows, step):
    even = even_mask((step, dst.shape[2]))
    for i in pairs:
        for r in range(0, rows, step):
            value = (b[i, r : r + step] + beside(src, i, r, step, even, red)) * weight(i, r, step)
            dst[i + 1, PAD + r : PAD + r + step] = value


def residual_sum(red, black, red_b, black_b, i, r, step, even):
    at = PAD + r
    x = red_b[i, r : r + step] - 6.0 * red[i + 1, at : at + step] + beside(black, i, r, step, even, True)
    y = black_b[i, r : r + step] - 6.0 * black[i + 1, at : at + step] + beside(red, i, r, step, even, False)
    return x + y


def clear_pads(*colours):
    for ref in colours:
        pairs, rows, lanes = ref.shape
        for i in (0, pairs - 1):
            ref[i] = jnp.zeros((rows, lanes), F32)
        for i in range(1, pairs - 1):
            ref[i, :PAD] = jnp.zeros((PAD, lanes), F32)
            ref[i, rows - PAD :] = jnp.zeros((PAD, lanes), F32)


def table(rows, cols, of, value=1.0):
    k = lax.broadcasted_iota(jnp.int32, (rows, cols), 0)
    c = lax.broadcasted_iota(jnp.int32, (rows, cols), 1)
    return jnp.where(of(k, c), F32(value), F32(0.0)).astype(BF16)


def dot(a, m):
    high = a.astype(BF16)
    rest = a - high.astype(F32)
    middle = rest.astype(BF16)
    low = (rest - middle.astype(F32)).astype(BF16)
    parts = jnp.concatenate([high, middle, low], axis=1)
    return jnp.dot(parts, jnp.concatenate([m, m, m], axis=0), preferred_element_type=F32)


def pack_kernel(start_hbm, right_hbm, s, up, down, start, right, sem_a, sem_b):
    copy_a = pltpu.make_async_copy(start_hbm, start, sem_a)
    copy_b = pltpu.make_async_copy(right_hbm, right, sem_b)
    copy_a.start()
    copy_b.start()
    even = even_mask((64, 128))
    low = lane_of((64, 128)) < 64
    copy_a.wait()
    copy_b.wait()
    for p in range(4):
        s[p] = jnp.where(even, start[2 * p + 1], start[2 * p])
        s[p + 4] = jnp.where(even, right[2 * p], right[2 * p + 1])
        s[p + 8] = jnp.where(even, right[2 * p + 1], right[2 * p])
    for p in range(6):
        a, b = s[p], pltpu.roll(s[p + 6], 64, 1)
        up[p] = jnp.where(low, b, a)
        down[p] = jnp.where(low, a, b)


def pack16(planes, first=0):
    lanes = lane_of(planes[0].shape)
    total = jnp.zeros(planes[0].shape, F32)
    for k, plane in enumerate(planes):
        at = 16 * (k + first)
        total = jnp.where((lanes >= at) & (lanes < at + 16), pltpu.roll(plane, (8 + at) % 128, 1), total)
    return total


def unpack16(packed, k):
    lanes = lane_of(packed.shape)
    shift = (-8 - 16 * k) % 128
    plane = pltpu.roll(packed, shift, 1) if shift else packed
    return jnp.where((lanes < 8) | (lanes >= 120), plane, 0.0)


UP_NEAR, UP_FAR = (1, 2, 3, 6, 7, 10, 11), (0, 4, 5, 8, 9)
DOWN_NEAR, DOWN_FAR = (0, 1, 2, 4, 5, 8, 9), (3, 6, 7, 10, 11)
NEAR, FAR = len(UP_NEAR), len(UP_FAR)
CROSS_Y = 12 * 24 + 12 * 16 + 2 * 8
STRIP_AT = 48 * NEAR
FAR_AT = STRIP_AT + 32 * NEAR
PACKED_AT = FAR_AT + 16 * FAR
WHOLE_AT = PACKED_AT + 2 * 16
CROSS_X = WHOLE_AT + 64


def widen_kernel(s, up, down, v, v_up, v_down, first, last):
    low = lane_of((64, 128)) < 64
    for p in range(6):
        v[p] = jnp.where(low, down[p], up[p])
        v[p + 6] = pltpu.roll(jnp.where(low, up[p], down[p]), 64, 1)
    for p in range(12):
        first[24 * p : 24 * p + 24] = s[p, :24]
        last[24 * p : 24 * p + 24] = s[p, 40:]
        at = 288 + 16 * p
        first[at : at + 16] = v[p, :16]
        last[at : at + 16] = v[p, 48:]
    for t in range(2):
        at = 480 + 8 * t
        first[at : at + 8] = pack16([v[6 * t + k, 16:24] for k in range(6)])
        last[at : at + 8] = pack16([v[6 * t + k, 40:48] for k in range(6)])
    for ref, near in ((v_up, UP_NEAR), (v_down, DOWN_NEAR)):
        for k, p in enumerate(near):
            ref[k] = v[p]


def strips_kernel(v, before, after, *rest):
    lanes = lane_of((8, 128))
    for ref, near, far in ((rest[-2], UP_NEAR, UP_FAR), (rest[-1], DOWN_NEAR, DOWN_FAR)):
        outer = [jnp.zeros((8, 128), F32), jnp.zeros((8, 128), F32)]
        for k, p in enumerate(near):
            ref[48 * k : 48 * k + 24] = before[24 * p : 24 * p + 24]
            ref[48 * k + 24 : 48 * k + 48] = after[24 * p : 24 * p + 24]
            at, inner = STRIP_AT + 32 * k, 288 + 16 * p
            ref[at : at + 16] = before[inner : inner + 16]
            ref[at + 16 : at + 32] = after[inner : inner + 16]
            at, shift = 480 + 8 * (p // 6), 16 * (k - p % 6) % 128
            for h, strip in enumerate((before, after)):
                plane = strip[at : at + 8]
                plane = pltpu.roll(plane, shift, 1) if shift else plane
                outer[h] = jnp.where((lanes >= 16 * k) & (lanes < 16 * k + 16), plane, outer[h])
        ref[WHOLE_AT:] = pack16([v[p] for p in far])
        edges = [[], []]
        for k, p in enumerate(far):
            at, inner = FAR_AT + 16 * k, 288 + 16 * p
            ref[at : at + 8] = before[24 * p + 16 : 24 * p + 24]
            ref[at + 8 : at + 16] = after[24 * p : 24 * p + 8]
            edges[0].append(before[inner + 8 : inner + 16])
            edges[1].append(after[inner : inner + 8])
        for h in range(2):
            at = PACKED_AT + 8 * h
            ref[at : at + 8] = outer[h]
            ref[at + 16 : at + 24] = pack16(edges[h])


def fine_down_kernel(
    n, s, v, before, after, s_left, s_right, v_left, v_right, y_left, y_right,
    coarse, sent, black_out, red_b_out, black_b_out, red, black, rb, bb, weight, pairs,
):
    gx, gy, gz = (lax.axis_index(a) for a in ("gx", "gy", "gz"))
    inner = domain((ROWS0, 256), 64 * gy - EY, 64 * n[1], 128 * gz, 128 * n[2], 192)
    has_left, has_right = gx > 0, gx < n[0] - 1
    weight[0] = jnp.where(has_left, inner, 0.0)
    weight[1] = inner
    weight[2] = jnp.where(has_right, inner, 0.0)
    clear_pads(black, red)
    block, strip = slice(0, 128), slice(128, 256)
    zero8 = jnp.zeros((8, 128), F32)
    for a, ref in enumerate((black, rb, bb)):
        off, top = (1, PAD) if a == 0 else (0, 0)

        def put(i, lo, lanes, value, there=None, ref=ref, off=off, top=top, a=a):
            if a == 0 and there is not None:
                value = jnp.where(there, value, 0.0)
            ref[i + off, top + lo : top + lo + value.shape[0], lanes] = value

        for p in range(4):
            j, i = 4 * a + p, 4 + p
            put(i, EY, block, s[j])
            put(i, EY, strip, v[j])
            put(p, EY, block, s_left[j], has_left)
            put(8 + p, EY, block, s_right[j], has_right)
            put(i, 0, block, before[24 * j : 24 * j + 24])
            put(i, EY + 64, block, after[24 * j : 24 * j + 24])
            at = 288 + 16 * j
            put(i, 8, strip, before[at : at + 16])
            put(i, EY + 64, strip, after[at : at + 16])
            at = 480 + 8 * (j // 6)
            put(i, 0, strip, unpack16(before[at : at + 8], j % 6))
            put(i, EY + 80, strip, unpack16(after[at : at + 8], j % 6))
        sides = ((0, UP_NEAR, UP_FAR, v_left, y_left, has_left), (8, DOWN_NEAR, DOWN_FAR, v_right, y_right, has_right))
        for base, near, far, strips, y, there in sides:
            for k, p in enumerate(near):
                if p // 4 != a:
                    continue
                i = base + p % 4
                put(i, EY, strip, strips[k], there)
                put(i, 0, block, y[48 * k : 48 * k + 24], there)
                put(i, EY + 64, block, y[48 * k + 24 : 48 * k + 48], there)
                at = STRIP_AT + 32 * k
                put(i, 8, strip, y[at : at + 16], there)
                put(i, EY + 64, strip, y[at + 16 : at + 32], there)
                put(i, 0, strip, unpack16(y[PACKED_AT : PACKED_AT + 8], k), there)
                put(i, EY + 80, strip, unpack16(y[PACKED_AT + 8 : PACKED_AT + 16], k), there)
            for k, p in enumerate(far):
                if p // 4 != a:
                    continue
                i = base + p % 4
                put(i, EY, strip, unpack16(y[WHOLE_AT:], k), there)
                at = FAR_AT + 16 * k
                put(i, 16, block, y[at : at + 8], there)
                put(i, EY + 64, block, y[at + 8 : at + 16], there)
                put(i, 16, strip, unpack16(y[PACKED_AT + 16 : PACKED_AT + 24], k), there)
                put(i, EY + 64, strip, unpack16(y[PACKED_AT + 24 : PACKED_AT + 32], k), there)
                for lanes in (block, strip):
                    for lo in (0, 8, EY + 72, EY + 80):
                        put(i, lo, lanes, zero8)

    def weights(i, r, step):
        return weight[i // 4, r : r + step]

    half(red, black, rb, weights, True, range(0, 12), ROWS0, 16)
    half(black, red, bb, weights, False, range(1, 11), ROWS0, 16)
    half(red, black, rb, weights, True, range(1, 11), ROWS0, 16)
    half(black, red, bb, weights, False, range(2, 10), ROWS0, 16)
    even = even_mask((16, 256))
    for p in range(4):
        for r in range(0, ROWS0, 16):
            value = residual_sum(red, black, rb, bb, p + 4, r, 16, even)
            pairs[2 * p, r : r + 16] = value[:, :128]
            pairs[2 * p + 1, r : r + 16] = value[:, 128:]
    rows = []
    for p in range(4):
        parts = [pairs[2 * p + h, pl.ds(0, ROWS1, stride=2), :] + pairs[2 * p + h, pl.ds(1, ROWS1, stride=2), :] for h in (0, 1)]
        rows.append(jnp.concatenate(parts, axis=1))
    result = dot(jnp.concatenate(rows, axis=0), table(256, 128, lambda k, c: (k >> 1) == c, 0.5))
    for p in range(4):
        coarse[p] = result[p * ROWS1 : (p + 1) * ROWS1]
        sent[SENT1 * p : SENT1 * p + SENT1] = coarse[p, SENT1_AT : SENT1_AT + SENT1]
    for p in range(8):
        black_out[p] = black[p + 3, PAD + UP0 : PAD + UP0 + 80]
        red_b_out[p] = rb[p + 2, UP0 : UP0 + 80]
        black_b_out[p] = bb[p + 2, UP0 : UP0 + 80]


def middle_down_kernel(
    n, own, same, other, coarse, black_out, red_b_out, black_b_out, red, black, rb, bb, weight, pairs
):
    gx, gy, gz = (lax.axis_index(a) for a in ("gx", "gy", "gz"))
    count = 2 * n[0]
    core = gx % 2
    even = even_mask((ROWS1, 128))
    even_sent = even_mask((SENT1, 128)) ^ (SENT1_AT % 2 == 1)
    weight[...] = domain((ROWS1, 128), 32 * gy - EY // 2, 32 * n[1], 64 * gz, 64 * n[2], 96)
    clear_pads(red, black)
    zero = jnp.zeros((SENT1_AT, 128), F32)
    for i in range(count):
        block, q = i // 2, 2 * SENT1 * (i % 2)
        mine = core == block % 2
        a, b = (jnp.where(mine, same[block // 2, at : at + SENT1], other[block // 2, at : at + SENT1]) for at in (q, q + SENT1))
        for ref, v in ((rb, jnp.where(even_sent, a, b)), (bb, jnp.where(even_sent, b, a))):
            ref[i, :SENT1_AT] = zero
            ref[i, SENT1_AT : SENT1_AT + SENT1] = v
            ref[i, SENT1_AT + SENT1 :] = zero
    for h in range(2):
        a, b = own[2 * h], own[2 * h + 1]
        rb[2 * gx + h] = jnp.where(even, a, b)
        bb[2 * gx + h] = jnp.where(even, b, a)
    for i in range(count):
        red[i + 1, PAD : PAD + ROWS1] = rb[i] * weight[...]

    def weights(i, r, step):
        return weight[r : r + step]

    every = range(count)
    half(black, red, bb, weights, False, every, ROWS1, ROWS1)
    half(red, black, rb, weights, True, every, ROWS1, ROWS1)
    half(black, red, bb, weights, False, every, ROWS1, ROWS1)
    for i in range(8):
        q = 2 * gx - 3 + i
        inside = jnp.clip(q, 0, count - 1)
        black_out[i] = black[jnp.clip(q + 1, 0, count + 1), PAD : PAD + ROWS1]
        red_b_out[i] = rb[inside]
        black_b_out[i] = bb[inside]
    top = EY // 2 - 4
    even40 = even_mask((40, 128))
    for i in every:
        pairs[i] = residual_sum(red, black, rb, bb, i, top, 40, even40)
    sums = [pairs[i, pl.ds(4, 16, stride=2), :] + pairs[i, pl.ds(5, 16, stride=2), :] for i in every]
    to2 = lambda k: jnp.where(k < 96, (k >> 1) + 16, (k >> 1) - 48)
    low = jnp.concatenate(sums[: n[0]], axis=0)
    high = jnp.concatenate(sums[n[0] :], axis=0)
    take = table(256, 128, lambda k, c: to2(k & 127) + (k & 128) // 2 == c, 0.5)
    result = dot(jnp.concatenate([low, high], axis=1), take)
    for i in range(n[0]):
        coarse[i] = result[16 * i : 16 * i + 16]


def wrap_pairs(ref, rows):
    last = ref.shape[0] - 2
    low = lane_of((rows, 128)) < 64
    ref[0, PAD : PAD + rows] = jnp.where(low, 0.0, pltpu.roll(ref[last, PAD : PAD + rows], 64, 1))
    ref[last + 1, PAD : PAD + rows] = jnp.where(low, pltpu.roll(ref[1, PAD : PAD + rows], 64, 1), 0.0)


def domain2(n, gz, rows):
    y = lane_of((rows, 128))
    z = (y & 63) - 16 + 32 * gz
    return jnp.where((z >= 0) & (z < 32 * n[2]), F32(SIXTH), F32(0.0))


def third_place(n, i):
    packed = n[0] // 2
    arrays = max(1, packed // 2)
    p = i % packed
    return p % arrays, 64 * (i // packed) + 32 * (p // arrays)


def coarse_down_kernel(n, b2, coarse, black_out, rb, bb, red, black, weight, pairs):
    gz = lax.axis_index("gz")
    rows, packed = 16 * n[1], n[0] // 2
    weight[...] = domain2(n, gz, rows)
    clear_pads(red, black)
    even16 = even_mask((16, 128))
    for i in range(packed):
        for g in range(n[1]):
            a, b = b2[g, 2 * i], b2[g, 2 * i + 1]
            at = 16 * g
            r = jnp.where(even16, a, b)
            rb[i, at : at + 16] = r
            bb[i, at : at + 16] = jnp.where(even16, b, a)
            red[i + 1, PAD + at : PAD + at + 16] = r * weight[at : at + 16]

    def weights(i, r, step):
        return weight[r : r + step]

    every = range(packed)
    wrap_pairs(red, rows)
    half(black, red, bb, weights, False, every, rows, rows)
    wrap_pairs(black, rows)
    half(red, black, rb, weights, True, every, rows, rows)
    wrap_pairs(red, rows)
    half(black, red, bb, weights, False, every, rows, rows)
    wrap_pairs(black, rows)
    even = even_mask((rows, 128))
    for i in every:
        pairs[i] = residual_sum(red, black, rb, bb, i, 0, rows, even)
        black_out[i] = black[i + 1, PAD : PAD + rows]
    rows3 = rows // 2
    sums = [pairs[i, pl.ds(0, rows3, stride=2), :] + pairs[i, pl.ds(1, rows3, stride=2), :] for i in every]
    take = table(128, 128, lambda k, c: ((k & 63) >> 1) + (k & 64) == c, 0.5)
    result = dot(jnp.concatenate(sums, axis=0), take)
    arrays = coarse.shape[0]
    for r in range(arrays):
        total = result[r * rows3 : (r + 1) * rows3]
        if packed > arrays:
            total = total + pltpu.roll(result[(r + arrays) * rows3 : (r + arrays + 1) * rows3], 32, 1)
        coarse[r] = total


def up_kernel(
    n, b3, b3_left, b3_right, start2, rb2, bb2, black1, red_b1, black_b1, black0, red_b0, black_b0, out,
    red2, black2, weight2,
    rb3, bb3, red3, black3, weight3, add2,
    add1, red1, bl1, weight1,
    add0, red0, bl0, weight0,
):
    gx, gy, gz = (lax.axis_index(a) for a in ("gx", "gy", "gz"))
    rows2, rows3 = 16 * n[1], 8 * n[1]
    packed, pairs_3 = n[0] // 2, n[0] // 2

    shape3 = (rows3, 128)
    even3 = even_mask(shape3)
    lane3 = lane_of(shape3)
    z3 = lane3 - 24 + 16 * gz
    weight3[...] = jnp.where((z3 >= 0) & (z3 < 16 * n[2]) & (lane3 < 64), F32(SIXTH), F32(0.0))
    clear_pads(red3, black3)

    def plane3(i):
        at, lane = third_place(n, i)
        own, left, right = (pltpu.roll(ref[at], (to - lane) % 128, 1) if (to - lane) % 128 else ref[at] for ref, to in ((b3, 16), (b3_left, 0), (b3_right, 32)))
        return jnp.where(lane3 < 24, left, jnp.where(lane3 < 40, own, right))

    for i in range(pairs_3):
        a, b = plane3(2 * i), plane3(2 * i + 1)
        r = jnp.where(even3, a, b)
        rb3[i] = r
        bb3[i] = jnp.where(even3, b, a)
        red3[i + 1, PAD : PAD + rows3] = r * weight3[...]

    def weights3(i, r, step):
        return weight3[r : r + step]

    every3 = range(pairs_3)
    half(black3, red3, bb3, weights3, False, every3, rows3, rows3)

    for _ in range(7):
        half(red3, black3, rb3, weights3, True, every3, rows3, rows3)
        half(black3, red3, bb3, weights3, False, every3, rows3, rows3)
    planes = []
    for i in every3:
        r, b = red3[i + 1, PAD : PAD + rows3], black3[i + 1, PAD : PAD + rows3]
        planes += [jnp.where(even3, r, b), jnp.where(even3, b, r)]

    halves = [jnp.concatenate(planes[:packed], axis=0), jnp.concatenate(planes[packed:], axis=0)]
    spread = table(256, 128, lambda k, c: ((c & 63) >> 1) + 16 + 2 * (c & 64) == k)
    wide = dot(jnp.concatenate(halves, axis=1), spread)
    weight2[...] = domain2(n, gz, rows2)
    clear_pads(red2, black2)
    every2 = range(packed)
    for i in every2:
        w = wide[i * rows3 : (i + 1) * rows3]
        add2[i, pl.ds(0, rows3, stride=2), :] = w
        add2[i, pl.ds(1, rows3, stride=2), :] = w
        black2[i + 1, PAD : PAD + rows2] = start2[i] + add2[i]

    def weights2(i, r, step):
        return weight2[r : r + step]

    for _ in range(2):
        wrap_pairs(black2, rows2)
        half(red2, black2, rb2, weights2, True, every2, rows2, rows2)
        wrap_pairs(red2, rows2)
        half(black2, red2, bb2, weights2, False, every2, rows2, rows2)

    even32 = even_mask((32, 128))
    top = pl.multiple_of(16 * gy, 8)
    planes = []
    second = lane_of((32, 128)) >= 64
    for i in range(8):
        q = gx - 2 + (i + 1) // 2
        there = (q >= 0) & (q < n[0])
        upper = q >= packed
        at = jnp.clip(jnp.where(upper, q - packed, q), 0, packed - 1) + 1
        r, b = red2[at, pl.ds(top, 32), :], black2[at, pl.ds(top, 32), :]
        plane = jnp.where(even32, r, b) if i % 2 == 1 else jnp.where(even32, b, r)
        planes.append(jnp.where(there & (second == upper), plane, 0.0))
    to2 = lambda k, c: jnp.where(c < 96, (c >> 1) + 16, (c >> 1) - 48) == (k & 63)
    wide = dot(jnp.concatenate(planes, axis=0), table(128, 128, to2))
    inner = domain((ROWS1, 128), 32 * gy - EY // 2, 32 * n[1], 64 * gz, 64 * n[2], 96)
    clear_pads(red1, bl1)
    skip = PAD - EY // 4
    for i in range(8):
        q = 2 * gx - 3 + i
        weight1[i] = jnp.where((q >= 0) & (q < 2 * n[0]), inner, 0.0)
        w = wide[32 * i + skip : 32 * i + skip + ROWS1 // 2]
        add1[i, pl.ds(0, ROWS1 // 2, stride=2), :] = w
        add1[i, pl.ds(1, ROWS1 // 2, stride=2), :] = w
        bl1[i + 1, PAD : PAD + ROWS1] = black1[i] + add1[i]

    def weights1(i, r, step):
        return weight1[i, r : r + step]

    half(red1, bl1, red_b1, weights1, True, range(0, 8), ROWS1, ROWS1)
    half(bl1, red1, black_b1, weights1, False, range(1, 7), ROWS1, ROWS1)
    half(red1, bl1, red_b1, weights1, True, range(1, 7), ROWS1, ROWS1)
    half(bl1, red1, black_b1, weights1, False, range(2, 6), ROWS1, ROWS1)

    low1 = PAD + UP0 // 2
    even40 = even_mask((40, 128))
    planes = []
    for i in range(8):
        r, b = red1[3 + i // 2, low1 : low1 + 40], bl1[3 + i // 2, low1 : low1 + 40]
        planes.append(jnp.where(even40, r, b) if i % 2 == 0 else jnp.where(even40, b, r))
    wide = dot(jnp.concatenate(planes, axis=0), table(128, 256, lambda k, c: (c >> 1) == k))
    inner = domain((80, 256), 64 * gy - 8, 64 * n[1], 128 * gz, 128 * n[2], 192)
    weight0[0] = jnp.where(gx > 0, inner, 0.0)
    weight0[1] = inner
    weight0[2] = jnp.where(gx < n[0] - 1, inner, 0.0)
    clear_pads(red0, bl0)
    for i in range(8):
        for h in (0, 1):
            w = wide[40 * i : 40 * i + 40, 128 * h : 128 * h + 128]
            add0[2 * i + h, pl.ds(0, 40, stride=2), :] = w
            add0[2 * i + h, pl.ds(1, 40, stride=2), :] = w
            bl0[i + 1, PAD : PAD + 80, 128 * h : 128 * h + 128] = black0[i, :, 128 * h : 128 * h + 128] + add0[2 * i + h]

    def weights0(i, r, step):
        return weight0[(i + 2) // 4, r : r + step]

    half(red0, bl0, red_b0, weights0, True, range(0, 8), 80, 16)
    half(bl0, red0, black_b0, weights0, False, range(1, 7), 80, 16)
    half(red0, bl0, red_b0, weights0, True, range(1, 7), 80, 16)
    half(bl0, red0, black_b0, weights0, False, range(2, 6), 80, 16)
    even64 = even_mask((64, 128))
    for p in range(4):
        r = red0[p + 3, PAD + 8 : PAD + 72, :128]
        b = bl0[p + 3, PAD + 8 : PAD + 72, :128]
        out[2 * p] = jnp.where(even64, r, b)
        out[2 * p + 1] = jnp.where(even64, b, r)


def from_both(up_value, down_value, axis):
    size = lax.axis_size(axis)
    up = [(i, i + 1) for i in range(size - 1)]
    return lax.ppermute(up_value, axis, up), lax.ppermute(down_value, axis, [(b, a) for a, b in up])


def from_both_round(up_value, down_value, axis):
    size = lax.axis_size(axis)
    up = [(i, (i + 1) % size) for i in range(size)]
    return lax.ppermute(up_value, axis, up), lax.ppermute(down_value, axis, [(b, a) for a, b in up])


def gathered(value, axis, groups=None):
    size = lax.axis_size(axis) if groups is None else len(groups[0])
    copies = jnp.broadcast_to(value, (size, *value.shape))
    return lax.all_to_all(copies, axis, split_axis=0, concat_axis=0, axis_index_groups=groups, tiled=True)


def local(right_side, start):
    n = tuple(lax.axis_size(a) for a in ("gx", "gy", "gz"))
    s, up, down = call(
        pack_kernel,
        [(12, 64, 128), (6, 64, 128), (6, 64, 128)],
        [(8, 64, 128), (8, 64, 128), pltpu.SemaphoreType.DMA, pltpu.SemaphoreType.DMA],
        [pl.BlockSpec(memory_space=pltpu.HBM)] * 2,
    )(start, right_side)
    up, down = from_both(up, down, "gz")
    s_left, s_right = from_both_round(s, s, "gx")
    near = (NEAR, 64, 128)
    v, v_up, v_down, first, last = call(widen_kernel, [(12, 64, 128), near, near, (CROSS_Y, 128), (CROSS_Y, 128)])(s, up, down)
    v_left, v_right = from_both_round(v_up, v_down, "gx")
    before, after = from_both(last, first, "gy")
    up, down = call(strips_kernel, [(CROSS_X, 128)] * 2)(v, before, after, s_left, s_right, v_left, v_right)
    y_left, y_right = from_both_round(up, down, "gx")
    up0 = (8, 80, 256)
    b1, sent, black0, red_b0, black_b0 = call(
        functools.partial(fine_down_kernel, n),
        [(4, ROWS1, 128), (4 * SENT1, 128), up0, up0, up0],
        [(14, ROWS0 + 2 * PAD, 256)] * 2 + [(12, ROWS0, 256)] * 2 + [(3, ROWS0, 256), (8, ROWS0, 128)],
    )(s, v, before, after, s_left, s_right, v_left, v_right, y_left, y_right)
    groups = [[2 * chip + core for chip in range(n[0] // 2)] for core in range(2)]
    same = gathered(sent[None], "gx", groups)
    other = lax.ppermute(same, "gx", [(i, i ^ 1) for i in range(n[0])])
    all1 = (2 * n[0], ROWS1, 128)
    colour1 = (2 * n[0] + 2, ROWS1 + 2 * PAD, 128)
    window1 = (8, ROWS1, 128)
    blocks = (n[0] // 2, 4 * SENT1, 128)
    b2, black1, red_b1, black_b1 = call(
        functools.partial(middle_down_kernel, n),
        [(n[0], 16, 128), window1, window1, window1],
        [colour1, colour1, all1, all1, (ROWS1, 128), (2 * n[0], 40, 128)],
    )(b1, same.reshape(blocks), other.reshape(blocks))
    b2 = gathered(b2, "gy").reshape(n[1], n[0], 16, 128)
    rows2, rows3 = 16 * n[1], 8 * n[1]
    packed = n[0] // 2
    all2, colour2, colour3 = (packed, rows2, 128), (packed + 2, rows2 + 2 * PAD, 128), (packed + 2, rows3 + 2 * PAD, 128)
    b3, black2, red_b2, black_b2 = call(
        functools.partial(coarse_down_kernel, n),
        [(max(1, packed // 2), rows3, 128), all2, all2, all2],
        [colour2, colour2, (rows2, 128), all2],
    )(b2)
    left, right = from_both(b3, b3, "gz")
    (out,) = call(
        functools.partial(up_kernel, n),
        [(8, 64, 128)],
        [
            colour2, colour2, (rows2, 128),
            (packed, rows3, 128), (packed, rows3, 128), colour3, colour3, (rows3, 128), all2,
            window1, (10, ROWS1 + 2 * PAD, 128), (10, ROWS1 + 2 * PAD, 128), window1,
            (16, 80, 128), (10, 80 + 2 * PAD, 256), (10, 80 + 2 * PAD, 256), (3, 80, 256),
        ],
    )(b3, left, right, black2, red_b2, black_b2, black1, red_b1, black_b1, black0, red_b0, black_b0)
    return out


def solution(mesh):
    in_specs = (P("gx", "gy", "gz"), P("gx", "gy", "gz"))
    out_specs = P("gx", "gy", "gz")
    return jax.shard_map(local, mesh=mesh, in_specs=in_specs, out_specs=out_specs, check_vma=False)
```
